32 devices in a mesh: dp: 16 (over z, x, core), tensor: 2 (over y).
Axes of the slice: x: 2, y: 2, z: 4, core: 2. Of those that a mesh axis runs over, the one named last changes fastest.
Arguments:
- tokens: bfloat16 [6144, 16384], P('dp', 'tensor'), may hold values from -6 to 6
- cotangent: bfloat16 [6144, 16384], P('dp', 'tensor'), may hold values from -6 to 6
- left_factor: bfloat16 [48, 16384], P('tensor'), may hold values from -0.125 to 0.125
- right_factor: bfloat16 [48, 16384], P('tensor'), may hold values from -0.125 to 0.125
- panel_rank: int32 [2], replicated, may hold values from 1 to 24, as said below
Outputs:
- token_grad: bfloat16 [6144, 16384], P('dp', 'tensor')
- left_grad: float32 [48, 2, 16, 512], P('tensor', None, 'dp')
- right_grad: float32 [48, 2, 16, 512], P('tensor', None, 'dp')
The draws below stay inside these ranges and needn't reach their ends.
Inputs may be any that keep to these rules, and one draw needn't show every extreme that they name: panel_rank[p] counts the live slots at the start of panel p; at least one panel has all 24 slots live and another has a single live slot.
All inputs are finite; a program needn't handle non-finite values.
Results may differ from the reference program's by a relative error of at most 0.0049.
Values may be sent and summed in bfloat16 or wider, within the bound.
No kernel may reach another device: no remote copies, remote signals or barrier semaphores. Data moves between devices by JAX's collectives and lax.ppermute only.
A program may use at most 128 MiB of HBM per device.

```python
import jax
import jax.numpy as jnp

D = 16384
RP = 24
PANELS = 2
RANKS = 48
TOKENS = 6144
FB = 512
N_DP = 16
N_TENSOR = 2


def draw_panel_rank(key, part):
    first_key, second_key, third_key = jax.random.split(jax.random.fold_in(key, 17), 3)
    counts = jax.random.randint(first_key, (PANELS,), 1, RP + 1)
    full_panel = jax.random.randint(second_key, (), 0, PANELS)
    offset = jax.random.randint(third_key, (), 0, PANELS - 1)
    short_panel = (full_panel + 1 + offset) % PANELS
    panel_ids = jnp.arange(PANELS)
    counts = jnp.where(panel_ids == short_panel, 1, counts)
    return jnp.where(panel_ids == full_panel, RP, counts).astype(jnp.int32)


def raised(entries, own_key, source, target, blocks, factor):
    def block_of(dim):
        return (jnp.arange(entries.shape[dim]) // (entries.shape[dim] // blocks)).reshape((-1,) + (1,) * (entries.ndim - 1 - dim))

    first = jax.random.permutation(own_key, blocks)[block_of(target)]
    second = (block_of(target) + blocks // 2) % blocks
    return jnp.where((block_of(source) == first) | (block_of(source) == second), factor * entries, entries)


def level_of(rng, shape, cuts, low, top_value):
    loudness, own = 1.0, jax.random.fold_in(rng, 6)
    for position, shards_of in cuts:
        steps = jnp.exp(jax.random.uniform(jax.random.fold_in(own, position), (shards_of,), jnp.float32, low / len(cuts), top_value / len(cuts)))
        loudness = loudness * jnp.repeat(steps, shape[position] // shards_of).reshape([-1 if axis == position else 1 for axis in range(len(shape))])
    return loudness


def centred(key, extent, spread, bound, cuts=(), held_as=jnp.bfloat16):
    array = jax.random.normal(key, extent, jnp.float32) * spread
    if len(cuts) > 0:
        array = level_of(key, extent, cuts, -0.22, 0.18) * array
    return jnp.clip(array, min=-bound, max=bound).astype(held_as)


def heavy_noise(stream_key, dims, spread, limit, shards, heavy, kind=jnp.bfloat16):
    result = spread * jax.random.normal(stream_key, dims, jnp.float32)
    if shards:
        result = result * level_of(stream_key, dims, shards, -0.22, 0.18)
    return jnp.clip(raised(result, jax.random.fold_in(stream_key, 3), *heavy), -limit, limit).astype(kind)


def setup_inputs(seed: int = 0) -> dict:
    streams_of = jax.random.split(jax.random.key(seed), 6)
    return {
        "tokens": centred(streams_of[0], (TOKENS, D), 1.0, 6.0, ((0, 16), (1, 2))),
        "cotangent": heavy_noise(streams_of[1], (TOKENS, D), 1.0, 6.0, ((0, 16), (1, 2)), (0, 1, 16, 2.0)),
        "left_factor": centred(streams_of[2], (RANKS, D), (D // 8) ** -0.5, 0.125, ((0, 2),)),
        "right_factor": centred(streams_of[3], (RANKS, D), (D // 8) ** -0.5, 0.125, ((0, 2),)),
        "panel_rank": draw_panel_rank(jax.random.fold_in(streams_of[5], 71), 0),
    }


def reference(tokens, cotangent, left_factor, right_factor, panel_rank):
    slots = jnp.arange(RANKS, dtype=jnp.int32)
    limits = jnp.repeat(panel_rank, RP, total_repeat_length=RANKS)
    live_rows = ((slots % RP) < limits).astype(left_factor.dtype)[:, None]
    left_live = left_factor * live_rows
    right_live = right_factor * live_rows
    hidden = jnp.dot(tokens, left_live.T, preferred_element_type=jnp.float32).astype(jnp.bfloat16)
    back_hidden = jnp.dot(cotangent, right_live.T, preferred_element_type=jnp.float32).astype(jnp.bfloat16)
    token_grad = jnp.dot(back_hidden, left_live, preferred_element_type=jnp.float32).astype(jnp.bfloat16)
    grad_scale = TOKENS ** -0.5
    right_grad = jnp.dot(hidden.T, cotangent, preferred_element_type=jnp.float32) * grad_scale
    left_grad = jnp.dot(back_hidden.T, tokens, preferred_element_type=jnp.float32) * grad_scale
    right_grad = right_grad.reshape(RANKS, N_TENSOR, N_DP, FB)
    left_grad = left_grad.reshape(RANKS, N_TENSOR, N_DP, FB)
    return token_grad, left_grad, right_grad
```

```python
import functools
import math

import jax
import jax.numpy as jnp
from jax import lax
from jax.experimental import pallas as pl
from jax.experimental.pallas import tpu as pltpu
from jax.sharding import PartitionSpec as P


def block_view(home):
    groups = lax.axis_size("tensor")
    width = lax.axis_size("dp")
    block = home.shape[1] // (groups * width)
    return home.reshape(home.shape[0], groups, width, block)


def own_blocks(summed):
    return lax.dynamic_slice_in_dim(summed, lax.axis_index("dp"), 1, 2)


def settle_both(left_cols, right_cols):
    left_home, right_home = (
        lax.all_to_all(left_cols, "tensor", split_axis=0, concat_axis=1, tiled=True),
        lax.all_to_all(right_cols, "tensor", split_axis=0, concat_axis=1, tiled=True),
    )
    left_home = block_view(left_home)
    right_home = block_view(right_home)
    left_sum, right_sum = lax.psum((left_home, right_home), "dp")
    return (own_blocks(left_sum), own_blocks(right_sum))


def any_panels(tokens, cotangent, left_factor, right_factor, panel_rank):
    slot_count = left_factor.shape[0]
    groups = lax.axis_size("tensor")
    all_slots = slot_count * groups
    left_cols, right_cols = (
        lax.all_to_all(left_factor, "tensor", split_axis=1, concat_axis=0, tiled=True),
        lax.all_to_all(right_factor, "tensor", split_axis=1, concat_axis=0, tiled=True),
    )
    slots = jnp.arange(all_slots, dtype=jnp.int32)
    limits = jnp.repeat(panel_rank, slot_count, total_repeat_length=all_slots)
    live_rows = (slots % slot_count < limits).astype(jnp.bfloat16)[:, None]
    left_live = left_cols * live_rows
    right_live = right_cols * live_rows
    feature_dims = (((1,), (1,)), ((), ()))
    hidden_part = lax.dot_general(
        tokens, left_live, feature_dims, preferred_element_type=jnp.float32
    )
    back_part = lax.dot_general(
        cotangent, right_live, feature_dims, preferred_element_type=jnp.float32
    )
    hidden, back_hidden = lax.psum((hidden_part, back_part), "tensor")
    hidden = hidden.astype(jnp.bfloat16)
    back_hidden = back_hidden.astype(jnp.bfloat16)
    grad_scale = 1.0 / math.sqrt(tokens.shape[0] * lax.axis_size("dp"))
    token_dims = (((0,), (0,)), ((), ()))
    right_local = (
        lax.dot_general(hidden, cotangent, token_dims, preferred_element_type=jnp.float32)
        * grad_scale
    )
    left_local = (
        lax.dot_general(back_hidden, tokens, token_dims, preferred_element_type=jnp.float32)
        * grad_scale
    )
    token_grad = jnp.dot(back_hidden, left_live, preferred_element_type=jnp.float32).astype(
        jnp.bfloat16
    )
    left_grad, right_grad = settle_both(left_local, right_local)
    return (token_grad, left_grad, right_grad)


PAD = 8
SWAP = [(0, 1), (1, 0)]
VMEM_LIMIT = 40 * 1024 * 1024


def flip(value, bit):
    size = lax.axis_size("dp")
    return lax.ppermute(value, "dp", [(i, i ^ (1 << bit)) for i in range(size)])


def live_rows_of(own, other, own_is_full):
    first = lax.broadcasted_iota(jnp.int32, (PAD, own.shape[1]), 0) == 0
    full = jnp.where(own_is_full, own, other)
    short = jnp.where(own_is_full, other[:PAD], own[:PAD])
    short = jnp.where(first, short, jnp.zeros_like(short))
    return jnp.concatenate([full, short], axis=0)


def project_kernel(half, flags, own, mine, theirs, rows_in, live_out, part_out):
    step = pl.program_id(0)
    other = jnp.where(flags[1] == step // half, mine[...], theirs[...])
    live = live_rows_of(own[...], other, flags[2] == 1)
    live_out[...] = live

    @pl.when(step == 0)
    def _():
        part_out[...] = jnp.zeros_like(part_out)

    part_out[...] += lax.dot_general(
        live, rows_in[...], (((1,), (1,)), ((), ())), preferred_element_type=jnp.float32
    )


def project(flags, factor, mine, theirs, acts):
    slots = factor.shape[0]
    tokens, width = acts.shape
    live = slots + PAD
    steps = 4
    half = steps // 2
    chunk = width // steps
    return pl.pallas_call(
        functools.partial(project_kernel, half),
        grid_spec=pltpu.PrefetchScalarGridSpec(
            num_scalar_prefetch=1,
            grid=(steps,),
            in_specs=[
                pl.BlockSpec((slots, chunk), lambda k, f: (0, f[0] * steps + k)),
                pl.BlockSpec((slots, chunk), lambda k, f: (0, k % half)),
                pl.BlockSpec((slots, chunk), lambda k, f: (0, k % half)),
                pl.BlockSpec((tokens, chunk), lambda k, f: (0, k)),
            ],
            out_specs=[
                pl.BlockSpec((live, chunk), lambda k, f: (0, k)),
                pl.BlockSpec((live, tokens), lambda k, f: (0, 0)),
            ],
        ),
        out_shape=[
            jax.ShapeDtypeStruct((live, width), jnp.bfloat16),
            jax.ShapeDtypeStruct((live, tokens), jnp.float32),
        ],
        compiler_params=pltpu.CompilerParams(vmem_limit_bytes=VMEM_LIMIT),
        cost_estimate=pl.CostEstimate(
            flops=2 * live * width * tokens, bytes_accessed=2 * width * tokens, transcendentals=0
        ),
        name="project",
    )(flags, factor, mine, theirs, acts)


def gradient_kernel(scale, flags, hidden, acts, keep, send):
    block = keep.shape[2]
    grad = jnp.dot(hidden[...], acts[...], preferred_element_type=jnp.float32) * scale
    low, high = grad[:, :block], grad[:, block:]
    even = flags[1] == 0
    keep[...] = jnp.where(even, low, high)[None]
    send[...] = jnp.where(even, high, low).astype(send.dtype)[None]


def gradient(flags, hidden, acts, scale):
    live, tokens = hidden.shape
    width = acts.shape[1]
    size = lax.axis_size("dp")
    bits = size.bit_length() - 1
    block = width // size
    pairs = size // 2

    def place(j, f):
        q = 0
        for bit in range(bits - 1):
            q = q * 2 + (j // (1 << bit)) % 2
        return (q, 0, 0)

    return pl.pallas_call(
        functools.partial(gradient_kernel, scale),
        grid_spec=pltpu.PrefetchScalarGridSpec(
            num_scalar_prefetch=1,
            grid=(pairs,),
            in_specs=[
                pl.BlockSpec((live, tokens), lambda j, f: (0, 0)),
                pl.BlockSpec((tokens, 2 * block), lambda j, f: (0, j)),
            ],
            out_specs=[
                pl.BlockSpec((1, live, block), place),
                pl.BlockSpec((1, live, block), place),
            ],
        ),
        out_shape=[
            jax.ShapeDtypeStruct((pairs, live, block), jnp.float32),
            jax.ShapeDtypeStruct((pairs, live, block), jnp.bfloat16),
        ],
        compiler_params=pltpu.CompilerParams(vmem_limit_bytes=VMEM_LIMIT),
        cost_estimate=pl.CostEstimate(
            flops=2 * live * width * tokens, bytes_accessed=2 * width * tokens, transcendentals=0
        ),
        name="gradient",
    )(flags, hidden, acts)


def spread_kernel(back, live, out):
    out[...] = lax.dot_general(
        back[...], live[...], (((0,), (0,)), ((), ())), preferred_element_type=jnp.float32
    ).astype(out.dtype)


def spread(back, live):
    rows, tokens = back.shape
    width = live.shape[1]
    steps = 8
    chunk = width // steps
    return pl.pallas_call(
        spread_kernel,
        grid=(steps,),
        in_specs=[
            pl.BlockSpec((rows, tokens), lambda k: (0, 0)),
            pl.BlockSpec((rows, chunk), lambda k: (0, k)),
        ],
        out_specs=pl.BlockSpec((tokens, chunk), lambda k: (0, k)),
        out_shape=jax.ShapeDtypeStruct((tokens, width), jnp.bfloat16),
        compiler_params=pltpu.CompilerParams(vmem_limit_bytes=VMEM_LIMIT),
        cost_estimate=pl.CostEstimate(
            flops=2 * rows * width * tokens, bytes_accessed=2 * width * tokens, transcendentals=0
        ),
        name="spread",
    )(back, live)


def fetch(factor, tensor, core):
    width = factor.shape[1] // 2
    part = width // 2
    wanted = lax.dynamic_slice_in_dim(factor, (1 - tensor) * width + core * part, part, 1)
    mine = lax.ppermute(wanted, "tensor", SWAP)
    return mine, flip(mine, 0)


def halve(keep, send, position):
    bits = lax.axis_size("dp").bit_length() - 1
    for bit in range(bits):
        total = keep + flip(send, bit).astype(jnp.float32)
        if bit == bits - 1:
            return total[0]
        low, high = jnp.split(total, 2, axis=0)
        even = (position >> (bit + 1)) % 2 == 0
        keep = jnp.where(even, low, high)
        send = jnp.where(even, high, low).astype(jnp.bfloat16)


def two_panels(tokens, cotangent, left_factor, right_factor, panel_rank):
    slots = left_factor.shape[0]
    position = lax.axis_index("dp")
    tensor = lax.axis_index("tensor")
    core = position % 2
    own_is_full = jnp.where(tensor == 0, panel_rank[0], panel_rank[1]) == slots
    flags = jnp.stack([tensor, core, own_is_full.astype(jnp.int32)]).astype(jnp.int32)
    scale = 1.0 / math.sqrt(tokens.shape[0] * lax.axis_size("dp"))

    right_mine, right_theirs = fetch(right_factor, tensor, core)
    left_mine, left_theirs = fetch(left_factor, tensor, core)
    _, back_part = project(flags, right_factor, right_mine, right_theirs, cotangent)
    left_live, hidden_part = project(flags, left_factor, left_mine, left_theirs, tokens)
    back = (back_part + lax.ppermute(back_part, "tensor", SWAP)).astype(jnp.bfloat16)
    hidden = (hidden_part + lax.ppermute(hidden_part, "tensor", SWAP)).astype(jnp.bfloat16)
    left_total = halve(*gradient(flags, back, tokens, scale), position)
    right_total = halve(*gradient(flags, hidden, cotangent, scale), position)
    token_grad = spread(back, left_live)

    total = jnp.stack([left_total, right_total])
    first = (jnp.arange(slots) == 0)[None, :, None]
    full = total[:, :slots]
    short = jnp.where(first, total[:, slots : slots + 1], 0.0)
    got = lax.ppermute(jnp.where(own_is_full, short, full), "tensor", SWAP)
    held = jnp.where(own_is_full, full, short)
    low = jnp.where(tensor == 0, held, got)
    high = jnp.where(tensor == 0, got, held)
    grads = jnp.stack([low, high], axis=2)[:, :, :, None, :]
    return token_grad, grads[0], grads[1]


def solution(mesh):
    placed = (P("dp", "tensor"), P("dp", "tensor"), P("tensor", None), P("tensor", None), P())
    size = mesh.shape["dp"]
    halves = size & (size - 1) == 0 and size >= 4
    return jax.shard_map(
        two_panels if mesh.shape["tensor"] == 2 and halves else any_panels,
        mesh=mesh,
        in_specs=placed,
        out_specs=(P("dp", "tensor"), P("tensor", None, "dp", None), P("tensor", None, "dp", None)),
        check_vma=False,
    )
```

```python
import functools
import math

import jax
import jax.numpy as jnp
from jax import lax
from jax.experimental import pallas as pl
from jax.experimental.pallas import tpu as pltpu
from jax.sharding import PartitionSpec as P


def block_view(home):
    groups = lax.axis_size("tensor")
    width = lax.axis_size("dp")
    block = home.shape[1] // (groups * width)
    return home.reshape(home.shape[0], groups, width, block)


def own_blocks(summed):
    return lax.dynamic_slice_in_dim(summed, lax.axis_index("dp"), 1, 2)


def settle_both(left_cols, right_cols):
    left_home, right_home = (
        lax.all_to_all(left_cols, "tensor", split_axis=0, concat_axis=1, tiled=True),
        lax.all_to_all(right_cols, "tensor", split_axis=0, concat_axis=1, tiled=True),
    )
    left_home = block_view(left_home)
    right_home = block_view(right_home)
    left_sum, right_sum = lax.psum((left_home, right_home), "dp")
    return (own_blocks(left_sum), own_blocks(right_sum))


def any_panels(tokens, cotangent, left_factor, right_factor, panel_rank):
    slot_count = left_factor.shape[0]
    groups = lax.axis_size("tensor")
    all_slots = slot_count * groups
    left_cols, right_cols = (
        lax.all_to_all(left_factor, "tensor", split_axis=1, concat_axis=0, tiled=True),
        lax.all_to_all(right_factor, "tensor", split_axis=1, concat_axis=0, tiled=True),
    )
    slots = jnp.arange(all_slots, dtype=jnp.int32)
    limits = jnp.repeat(panel_rank, slot_count, total_repeat_length=all_slots)
    live_rows = (slots % slot_count < limits).astype(jnp.bfloat16)[:, None]
    left_live = left_cols * live_rows
    right_live = right_cols * live_rows
    feature_dims = (((1,), (1,)), ((), ()))
    hidden_part = lax.dot_general(
        tokens, left_live, feature_dims, preferred_element_type=jnp.float32
    )
    back_part = lax.dot_general(
        cotangent, right_live, feature_dims, preferred_element_type=jnp.float32
    )
    hidden, back_hidden = lax.psum((hidden_part, back_part), "tensor")
    hidden = hidden.astype(jnp.bfloat16)
    back_hidden = back_hidden.astype(jnp.bfloat16)
    grad_scale = 1.0 / math.sqrt(tokens.shape[0] * lax.axis_size("dp"))
    token_dims = (((0,), (0,)), ((), ()))
    right_local = (
        lax.dot_general(hidden, cotangent, token_dims, preferred_element_type=jnp.float32)
        * grad_scale
    )
    left_local = (
        lax.dot_general(back_hidden, tokens, token_dims, preferred_element_type=jnp.float32)
        * grad_scale
    )
    token_grad = jnp.dot(back_hidden, left_live, preferred_element_type=jnp.float32).astype(
        jnp.bfloat16
    )
    left_grad, right_grad = settle_both(left_local, right_local)
    return (token_grad, left_grad, right_grad)


PAD = 8
SWAP = [(0, 1), (1, 0)]
WHOLE = pl.BlockSpec(memory_space=pltpu.VMEM)
SCALARS = pl.BlockSpec(memory_space=pltpu.SMEM)
FAR = pl.BlockSpec(memory_space=pltpu.HBM)
SMALL = pl.CostEstimate(flops=1, bytes_accessed=1, transcendentals=0)
PARAMS = pltpu.CompilerParams(vmem_limit_bytes=16 * 1024 * 1024)


def near(value):
    return pltpu.with_memory_space_constraint(value, pltpu.VMEM)


def far(value):
    return pltpu.with_memory_space_constraint(value, pltpu.HBM)


def flip(value, bit):
    size = lax.axis_size("dp")
    return lax.ppermute(value, "dp", [(i, i ^ (1 << bit)) for i in range(size)])


def after_all(value, *others):
    return lax.optimization_barrier((value, *others))[0]


def stage_kernel(parts, given, acts, factor, *refs):
    acts_out, factor_out = refs[given : given + 2]
    sems = refs[-1]
    width = factor_out.shape[1]
    column = pl.multiple_of(lax.axis_index("tensor") * width, width)
    rows = acts.shape[0] // parts
    copies = [pltpu.make_async_copy(factor.at[:, pl.ds(column, width)], factor_out, sems.at[0])]
    for n in range(parts):
        piece = pl.ds(n * rows, rows)
        copies.append(pltpu.make_async_copy(acts.at[piece], acts_out.at[piece], sems.at[n + 1]))
    for copy in copies:
        copy.start()
    if len(refs) == given + 4:
        rank, full_out = refs[0], refs[given + 2]
        own_rank = jnp.where(lax.axis_index("tensor") == 0, rank[0], rank[1])
        full = (own_rank == factor.shape[0]).astype(jnp.float32)
        full_out[...] = jnp.full(full_out.shape, full)
    for copy in copies:
        copy.wait()


def stage(acts, factor, rank, after):
    shapes = [
        pltpu.VMEM(acts.shape, acts.dtype),
        pltpu.VMEM((factor.shape[0], acts.shape[1]), factor.dtype),
    ]
    if rank:
        shapes.append(pltpu.VMEM((8, 128), jnp.float32))
    parts = 8 if acts.shape[0] % 128 == 0 else 1
    return pl.pallas_call(
        functools.partial(stage_kernel, parts, len(rank) + len(after)),
        in_specs=[FAR] * 2 + [SCALARS] * len(rank) + [WHOLE] * len(after),
        out_specs=[WHOLE] * len(shapes),
        out_shape=shapes,
        scratch_shapes=[pltpu.SemaphoreType.DMA((1 + parts,))],
        compiler_params=PARAMS,
        cost_estimate=SMALL,
        name="stage",
    )(far(acts), far(factor), *rank, *map(near, after))


def own_is_full(full):
    return full[0:1, 0:1] > 0.5


def both_panels(own, piece):
    gap = jnp.zeros((PAD, piece.shape[1]), piece.dtype)
    return jnp.concatenate([own, gap, piece, gap], axis=0)


def project_kernel(flipped, chunk, given, *refs):
    own, piece, acts = refs[:3]
    others, out = refs[3 : 3 + given], refs[-1]
    slots, width = piece.shape
    core = lax.axis_index("dp") % 2
    start = (1 - core if flipped else core) * width
    total = None
    for low in range(0, width, chunk):
        column = pl.ds(pl.multiple_of(start + low, chunk), chunk)
        rows = both_panels(own[:, column], piece[:, low : low + chunk])
        part = lax.dot_general(
            rows, acts[:, column], (((1,), (1,)), ((), ())), preferred_element_type=jnp.float32
        )
        total = part if total is None else total + part
    if others:
        total += others[0][...]
        full_here = own_is_full(others[1][...])
        own_part, other_part = total[:slots], total[slots + PAD : 2 * slots + PAD]
        out[:slots] = jnp.where(full_here, own_part, other_part)
        short = jnp.where(full_here, other_part[:PAD], own_part[:PAD])
        first = lax.broadcasted_iota(jnp.int32, short.shape, 0) == 0
        out[slots:] = jnp.where(first, short, 0.0)
    else:
        out[...] = total


def project(own, piece, acts, flipped, others, held):
    slots, width = piece.shape
    tokens = acts.shape[0]
    rows = slots + PAD if others else 2 * (slots + PAD)
    return pl.pallas_call(
        functools.partial(project_kernel, flipped, min(width, 2048), len(others)),
        in_specs=[WHOLE] * (3 + len(others) + len(held)),
        out_specs=WHOLE,
        out_shape=pltpu.VMEM((rows, tokens), jnp.float32),
        compiler_params=PARAMS,
        cost_estimate=SMALL,
        name="project",
    )(*map(near, (own, piece, acts, *others, *held)))


def gradient_kernel(scale, places, given, held, part, got, acts, *refs):
    outs = refs[given + held :]
    keep, send = outs[:2]
    rows, block = keep.shape[1], keep.shape[2]
    slots = part.shape[0] - PAD
    even = lax.axis_index("dp") % 2 == 0
    summed = (part[...] + got[...]).astype(jnp.bfloat16)
    row = lax.broadcasted_iota(jnp.int32, (PAD, 2 * block), 0)
    for j, q in enumerate(places):
        columns = slice(j * 2 * block, (j + 1) * 2 * block)
        grad = jnp.dot(summed, acts[:, columns], preferred_element_type=jnp.float32) * scale
        if given:
            short = jnp.where(row == 1, refs[0][q, 0:1, :], grad[slots:])
            grad = jnp.concatenate([grad[:slots], short], axis=0)
        else:
            outs[2][q] = grad[slots:]
            grad = grad[:slots]
        low, high = grad[:, :block], grad[:, block:]
        keep[q] = jnp.where(even, low, high)
        send[q] = jnp.where(even, high, low).astype(send.dtype)


def gradient(part, got, acts, scale, extra, held):
    live, tokens = part.shape
    slots = live - PAD
    width = acts.shape[1]
    size = lax.axis_size("dp")
    bits = size.bit_length() - 1
    block = width // size
    pairs = size // 2
    places = [int(format(j, "0%db" % (bits - 1))[::-1], 2) for j in range(pairs)]
    shape = (pairs, live if extra else slots, block)
    shapes = [pltpu.VMEM(shape, jnp.float32), pltpu.VMEM(shape, jnp.bfloat16)]
    if not extra:
        shapes.append(pltpu.VMEM((pairs, PAD, 2 * block), jnp.float32))
    return pl.pallas_call(
        functools.partial(gradient_kernel, scale, places, len(extra), len(held)),
        in_specs=[WHOLE] * (3 + len(extra) + len(held)),
        out_specs=[WHOLE] * len(shapes),
        out_shape=shapes,
        compiler_params=PARAMS,
        cost_estimate=SMALL,
        name="gradient",
    )(*map(near, (part, got, acts, *extra, *held)))


def spread_kernel(chunk, full, part, got, own, mine, theirs, after, out, buffer, sems):
    slots, width = mine.shape
    core = lax.axis_index("dp") % 2
    full_here = own_is_full(full[...])
    back = part[...] + got[...]
    first = lax.broadcasted_iota(jnp.int32, (slots, back.shape[1]), 0) == 0
    short = jnp.where(first, back[slots : slots + 1], 0.0)
    of_own = jnp.where(full_here, back[:slots], short)
    of_other = jnp.where(full_here, short, back[:slots])
    gap = jnp.zeros((PAD, back.shape[1]), jnp.float32)
    weights = jnp.concatenate([of_own, gap, of_other, gap], axis=0).T.astype(jnp.bfloat16)
    copies = []
    for side, piece in enumerate((mine, theirs)):
        for low in range(0, width, chunk):
            start = (core if side == 0 else 1 - core) * width + low
            column = pl.ds(pl.multiple_of(start, chunk), chunk)
            rows = both_panels(own[:, column], piece[:, low : low + chunk])
            held = buffer.at[:, side * width + low : side * width + low + chunk]
            held[...] = jnp.dot(weights, rows, preferred_element_type=jnp.float32).astype(out.dtype)
            copy = pltpu.make_async_copy(held, out.at[:, column], sems.at[len(copies)])
            copy.start()
            copies.append(copy)
    for copy in copies:
        copy.wait()


def spread(full, part, got, own, mine, theirs, after):
    tokens = part.shape[1]
    rows, width = own.shape
    chunk = min(width // 2, 1024)
    return pl.pallas_call(
        functools.partial(spread_kernel, chunk),
        in_specs=[WHOLE] * 7,
        out_specs=FAR,
        out_shape=jax.ShapeDtypeStruct((tokens, width), jnp.bfloat16),
        scratch_shapes=[
            pltpu.VMEM((tokens, width), jnp.bfloat16),
            pltpu.SemaphoreType.DMA((width // chunk,)),
        ],
        compiler_params=PARAMS,
        cost_estimate=SMALL,
        name="spread",
    )(*map(near, (full, part, got, own, mine, theirs, after)))


def settle_kernel(full, keep, got, held, send):
    slots, block = held.shape[1:]
    full_here = own_is_full(full[...])
    first = lax.broadcasted_iota(jnp.int32, (slots, block), 0) == 0
    total = keep[0] + got[0].astype(jnp.float32)
    for n, row in ((0, 1), (1, 0)):
        rows = total[n * slots : (n + 1) * slots]
        short = jnp.where(first, total[2 * slots + row : 2 * slots + row + 1], 0.0)
        held[n] = jnp.where(full_here, rows, short)
        send[n] = jnp.where(full_here, short, rows)


def settle(full, keep, got):
    rows, block = keep.shape[1:]
    shape = pltpu.VMEM((2, (rows - PAD) // 2, block), jnp.float32)
    return pl.pallas_call(
        settle_kernel,
        in_specs=[WHOLE] * 3,
        out_specs=[WHOLE, WHOLE],
        out_shape=[shape, shape],
        compiler_params=PARAMS,
        cost_estimate=SMALL,
        name="settle",
    )(near(full), near(keep), near(got))


def place_kernel(held, got, left_out, right_out):
    here = lax.axis_index("tensor") == 0
    for n, out in enumerate((left_out, right_out)):
        out[:, 0, 0, :] = jnp.where(here, held[n], got[n])
        out[:, 1, 0, :] = jnp.where(here, got[n], held[n])


def place(held, got):
    shape = jax.ShapeDtypeStruct((held.shape[1], 2, 1, held.shape[2]), jnp.float32)
    return pl.pallas_call(
        place_kernel,
        in_specs=[WHOLE, WHOLE],
        out_specs=[WHOLE, WHOLE],
        out_shape=[shape, shape],
        compiler_params=PARAMS,
        cost_estimate=SMALL,
        name="place",
    )(near(held), near(got))


def pick_kernel(factor, out, sem):
    part = out.shape[1]
    core = lax.axis_index("dp") % 2
    column = ((1 - lax.axis_index("tensor")) * 2 + core) * part
    copy = pltpu.make_async_copy(
        factor.at[:, pl.ds(pl.multiple_of(column, part), part)], out, sem
    )
    copy.start()
    copy.wait()


def pick(factor):
    slots, width = factor.shape
    return pl.pallas_call(
        pick_kernel,
        in_specs=[FAR],
        out_specs=WHOLE,
        out_shape=pltpu.VMEM((slots, width // 4), factor.dtype),
        scratch_shapes=[pltpu.SemaphoreType.DMA],
        compiler_params=PARAMS,
        cost_estimate=SMALL,
        name="pick",
    )(far(factor))


def halve_kernel(bit, count, *refs):
    keep_out, send_out = refs[2 * count :]
    blocks = keep_out.shape[0]
    even = (lax.axis_index("dp") // (1 << bit)) % 2 == 0
    row = 0
    for keep, got in zip(refs[:count], refs[count : 2 * count]):
        rows = keep.shape[1]
        low = keep[:blocks] + got[:blocks].astype(jnp.float32)
        high = keep[blocks:] + got[blocks:].astype(jnp.float32)
        keep_out[:, row : row + rows] = jnp.where(even, low, high)
        send_out[:, row : row + rows] = jnp.where(even, high, low).astype(send_out.dtype)
        row += rows


def halve(keeps, gots, bit):
    blocks, _, block = keeps[0].shape
    rows = sum(keep.shape[1] for keep in keeps)
    shape = (blocks // 2, rows, block)
    return pl.pallas_call(
        functools.partial(halve_kernel, bit, len(keeps)),
        in_specs=[WHOLE] * (2 * len(keeps)),
        out_specs=[WHOLE, WHOLE],
        out_shape=[pltpu.VMEM(shape, jnp.float32), pltpu.VMEM(shape, jnp.bfloat16)],
        compiler_params=PARAMS,
        cost_estimate=SMALL,
        name="halve",
    )(*map(near, (*keeps, *gots)))


def two_panels(tokens, cotangent, left_factor, right_factor, panel_rank):
    scale = 1.0 / math.sqrt(tokens.shape[0] * lax.axis_size("dp"))

    right_wanted = pick(right_factor)
    left_wanted = pick(left_factor)
    right_mine = lax.ppermute(right_wanted, "tensor", SWAP)
    left_mine = lax.ppermute(left_wanted, "tensor", SWAP)
    cotangent, right_own = stage(cotangent, right_factor, (), (left_wanted,))
    tokens, left_own, full = stage(tokens, left_factor, (panel_rank,), (right_own,))
    right_mine = after_all(right_mine, left_own)
    right_theirs = flip(right_mine, 0)
    back = project(right_own, right_mine, cotangent, False, (), ())
    left_mine = after_all(left_mine, back)
    back = project(right_own, right_theirs, cotangent, True, (back, full), ())
    left_theirs = flip(left_mine, 0)
    back_got = lax.ppermute(back, "tensor", SWAP)
    hidden = project(left_own, left_mine, tokens, False, (), (cotangent,))
    hidden = project(left_own, left_theirs, tokens, True, (hidden, full), (cotangent,))
    hidden_got = lax.ppermute(hidden, "tensor", SWAP)

    left_keep, left_send, extra = gradient(
        back, back_got, tokens, scale, (), (hidden, cotangent)
    )
    left_got = flip(left_send, 0)
    right_keep, right_send = gradient(hidden, hidden_got, cotangent, scale, (extra,), ())
    right_got = flip(right_send, 0)
    left_got = after_all(left_got, right_send)
    left_keep, left_send = halve((left_keep,), (left_got,), 1)
    left_got = flip(left_send, 1)
    right_keep, right_send = halve((right_keep,), (right_got,), 1)
    right_got = flip(right_send, 1)
    token_grad = spread(full, back, back_got, left_own, left_mine, left_theirs, right_send)
    left_got = after_all(left_got, token_grad)
    keep, send = halve((left_keep, right_keep), (left_got, right_got), 2)
    got = flip(send, 2)
    for bit in range(3, lax.axis_size("dp").bit_length() - 1):
        keep, send = halve((keep,), (got,), bit)
        got = flip(send, bit)

    held, send = settle(full, keep, got)
    return token_grad, *place(held, lax.ppermute(send, "tensor", SWAP))


def solution(mesh):
    placed = (P("dp", "tensor"), P("dp", "tensor"), P("tensor", None), P("tensor", None), P())
    size = mesh.shape["dp"]
    halves = size & (size - 1) == 0 and size >= 8
    return jax.shard_map(
        two_panels if mesh.shape["tensor"] == 2 and halves else any_panels,
        mesh=mesh,
        in_specs=placed,
        out_specs=(P("dp", "tensor"), P("tensor", None, "dp", None), P("tensor", None, "dp", None)),
        check_vma=False,
    )
```

```python
import functools
import math

import jax
import jax.numpy as jnp
from jax import lax
from jax.experimental import pallas as pl
from jax.experimental.pallas import tpu as pltpu
from jax.sharding import PartitionSpec as P


def block_view(home):
    groups = lax.axis_size("tensor")
    width = lax.axis_size("dp")
    block = home.shape[1] // (groups * width)
    return home.reshape(home.shape[0], groups, width, block)


def own_blocks(summed):
    return lax.dynamic_slice_in_dim(summed, lax.axis_index("dp"), 1, 2)


def settle_both(left_cols, right_cols):
    left_home, right_home = (
        lax.all_to_all(left_cols, "tensor", split_axis=0, concat_axis=1, tiled=True),
        lax.all_to_all(right_cols, "tensor", split_axis=0, concat_axis=1, tiled=True),
    )
    left_home = block_view(left_home)
    right_home = block_view(right_home)
    left_sum, right_sum = lax.psum((left_home, right_home), "dp")
    return (own_blocks(left_sum), own_blocks(right_sum))


def any_panels(tokens, cotangent, left_factor, right_factor, panel_rank):
    slot_count = left_factor.shape[0]
    groups = lax.axis_size("tensor")
    all_slots = slot_count * groups
    left_cols, right_cols = (
        lax.all_to_all(left_factor, "tensor", split_axis=1, concat_axis=0, tiled=True),
        lax.all_to_all(right_factor, "tensor", split_axis=1, concat_axis=0, tiled=True),
    )
    slots = jnp.arange(all_slots, dtype=jnp.int32)
    limits = jnp.repeat(panel_rank, slot_count, total_repeat_length=all_slots)
    live_rows = (slots % slot_count < limits).astype(jnp.bfloat16)[:, None]
    left_live = left_cols * live_rows
    right_live = right_cols * live_rows
    feature_dims = (((1,), (1,)), ((), ()))
    hidden_part = lax.dot_general(
        tokens, left_live, feature_dims, preferred_element_type=jnp.float32
    )
    back_part = lax.dot_general(
        cotangent, right_live, feature_dims, preferred_element_type=jnp.float32
    )
    hidden, back_hidden = lax.psum((hidden_part, back_part), "tensor")
    hidden = hidden.astype(jnp.bfloat16)
    back_hidden = back_hidden.astype(jnp.bfloat16)
    grad_scale = 1.0 / math.sqrt(tokens.shape[0] * lax.axis_size("dp"))
    token_dims = (((0,), (0,)), ((), ()))
    right_local = (
        lax.dot_general(hidden, cotangent, token_dims, preferred_element_type=jnp.float32)
        * grad_scale
    )
    left_local = (
        lax.dot_general(back_hidden, tokens, token_dims, preferred_element_type=jnp.float32)
        * grad_scale
    )
    token_grad = jnp.dot(back_hidden, left_live, preferred_element_type=jnp.float32).astype(
        jnp.bfloat16
    )
    left_grad, right_grad = settle_both(left_local, right_local)
    return (token_grad, left_grad, right_grad)


PAD = 8
SWAP = [(0, 1), (1, 0)]
WHOLE = pl.BlockSpec(memory_space=pltpu.VMEM)
FAR = pl.BlockSpec(memory_space=pltpu.HBM)
SMALL = pl.CostEstimate(flops=1, bytes_accessed=1, transcendentals=0)
PARAMS = pltpu.CompilerParams(vmem_limit_bytes=16 * 1024 * 1024)


def near(value):
    return pltpu.with_memory_space_constraint(value, pltpu.VMEM)


def far(value):
    return pltpu.with_memory_space_constraint(value, pltpu.HBM)


def flip(value, *bits):
    mask = sum(1 << bit for bit in bits)
    return lax.ppermute(value, "dp", [(i, i ^ mask) for i in range(lax.axis_size("dp"))])


def after_all(value, *others):
    return lax.optimization_barrier((value, *others))[0]


def stage_kernel(parts, rank, *refs):
    sources, outs, full_out, rank_here, sems = refs[:4], refs[6:10], *refs[10:]
    copies = [pltpu.make_async_copy(rank, rank_here, sems.at[0])]
    for source, out in zip(sources, outs):
        if source.shape == out.shape:
            rows = source.shape[0] // parts
            pairs = [
                (source.at[pl.ds(n * rows, rows)], out.at[pl.ds(n * rows, rows)])
                for n in range(parts)
            ]
        else:
            width = out.shape[1]
            column = pl.multiple_of(lax.axis_index("tensor") * width, width)
            pairs = [(source.at[:, pl.ds(column, width)], out)]
        for pair in pairs:
            copies.append(pltpu.make_async_copy(*pair, sems.at[len(copies)]))
    for copy in copies:
        copy.start()
    copies.pop(0).wait()
    own_rank = jnp.where(lax.axis_index("tensor") == 0, rank_here[0], rank_here[1])
    full = (own_rank == outs[0].shape[0]).astype(jnp.float32)
    full_out[...] = jnp.full(full_out.shape, full)
    for copy in copies:
        copy.wait()


def stage(rank, right, cotangent, left, tokens, after):
    acts = pltpu.VMEM(tokens.shape, tokens.dtype)
    own = pltpu.VMEM((left.shape[0], tokens.shape[1]), left.dtype)
    parts = 8 if tokens.shape[0] % 128 == 0 else 1
    return pl.pallas_call(
        functools.partial(stage_kernel, parts),
        in_specs=[FAR] * 5 + [WHOLE] * 2,
        out_specs=[WHOLE] * 5,
        out_shape=[own, acts, own, acts, pltpu.VMEM((8, 128), jnp.float32)],
        scratch_shapes=[
            pltpu.SMEM(rank.shape, rank.dtype),
            pltpu.SemaphoreType.DMA((3 + 2 * parts,)),
        ],
        compiler_params=PARAMS,
        cost_estimate=SMALL,
        name="stage",
    )(*map(far, (rank, right, cotangent, left, tokens)), *map(near, after))


def own_is_full(full):
    return full[0:1, 0:1] > 0.5


def both_panels(own, piece):
    gap = jnp.zeros((PAD, piece.shape[1]), piece.dtype)
    return jnp.concatenate([own, gap, piece, gap], axis=0)


def project_kernel(flipped, chunk, given, *refs):
    own, piece, acts = refs[:3]
    others, out = refs[3 : 3 + given], refs[-1]
    slots, width = piece.shape
    core = lax.axis_index("dp") % 2
    start = (1 - core if flipped else core) * width
    total = None
    for low in range(0, width, chunk):
        column = pl.ds(pl.multiple_of(start + low, chunk), chunk)
        rows = both_panels(own[:, column], piece[:, low : low + chunk])
        part = lax.dot_general(
            rows, acts[:, column], (((1,), (1,)), ((), ())), preferred_element_type=jnp.float32
        )
        total = part if total is None else total + part
    if others:
        total += others[0][...]
        full_here = own_is_full(others[1][...])
        own_part, other_part = total[:slots], total[slots + PAD : 2 * slots + PAD]
        out[:slots] = jnp.where(full_here, own_part, other_part)
        short = jnp.where(full_here, other_part[:PAD], own_part[:PAD])
        first = lax.broadcasted_iota(jnp.int32, short.shape, 0) == 0
        out[slots:] = jnp.where(first, short, 0.0)
    else:
        out[...] = total


def project(own, piece, acts, flipped, others, held):
    slots, width = piece.shape
    tokens = acts.shape[0]
    rows = slots + PAD if others else 2 * (slots + PAD)
    return pl.pallas_call(
        functools.partial(project_kernel, flipped, min(width, 2048), len(others)),
        in_specs=[WHOLE] * (3 + len(others) + len(held)),
        out_specs=WHOLE,
        out_shape=pltpu.VMEM((rows, tokens), jnp.float32),
        compiler_params=PARAMS,
        cost_estimate=SMALL,
        name="project",
    )(*map(near, (own, piece, acts, *others, *held)))


def gradient_kernel(scale, places, given, held, part, got, acts, *refs):
    outs = refs[given + held :]
    keep, send = outs[:2]
    rows, block = keep.shape[1], keep.shape[2]
    slots = part.shape[0] - PAD
    even = lax.axis_index("dp") % 2 == 0
    summed = (part[...] + got[...]).astype(jnp.bfloat16)
    row = lax.broadcasted_iota(jnp.int32, (PAD, 2 * block), 0)
    for j, q in enumerate(places):
        columns = slice(j * 2 * block, (j + 1) * 2 * block)
        grad = jnp.dot(summed, acts[:, columns], preferred_element_type=jnp.float32) * scale
        if given:
            short = jnp.where(row == 1, refs[0][q, 0:1, :], grad[slots:])
            grad = jnp.concatenate([grad[:slots], short], axis=0)
        else:
            outs[2][q] = grad[slots:]
            grad = grad[:slots]
        low, high = grad[:, :block], grad[:, block:]
        keep[q] = jnp.where(even, low, high)
        send[q] = jnp.where(even, high, low).astype(send.dtype)


def gradient(part, got, acts, scale, extra, held):
    live, tokens = part.shape
    slots = live - PAD
    width = acts.shape[1]
    size = lax.axis_size("dp")
    bits = size.bit_length() - 1
    block = width // size
    pairs = size // 2
    places = [int(format(j, "0%db" % (bits - 1))[::-1], 2) for j in range(pairs)]
    shape = (pairs, live if extra else slots, block)
    shapes = [pltpu.VMEM(shape, jnp.float32), pltpu.VMEM(shape, jnp.bfloat16)]
    if not extra:
        shapes.append(pltpu.VMEM((pairs, PAD, 2 * block), jnp.float32))
    return pl.pallas_call(
        functools.partial(gradient_kernel, scale, places, len(extra), len(held)),
        in_specs=[WHOLE] * (3 + len(extra) + len(held)),
        out_specs=[WHOLE] * len(shapes),
        out_shape=shapes,
        compiler_params=PARAMS,
        cost_estimate=SMALL,
        name="gradient",
    )(*map(near, (part, got, acts, *extra, *held)))


def spread_kernel(chunk, full, part, got, own, mine, theirs, after, out, buffer, sems):
    slots, width = mine.shape
    core = lax.axis_index("dp") % 2
    full_here = own_is_full(full[...])
    back = part[...] + got[...]
    first = lax.broadcasted_iota(jnp.int32, (slots, back.shape[1]), 0) == 0
    short = jnp.where(first, back[slots : slots + 1], 0.0)
    of_own = jnp.where(full_here, back[:slots], short)
    of_other = jnp.where(full_here, short, back[:slots])
    gap = jnp.zeros((PAD, back.shape[1]), jnp.float32)
    weights = jnp.concatenate([of_own, gap, of_other, gap], axis=0).T.astype(jnp.bfloat16)
    copies = []
    for side, piece in enumerate((mine, theirs)):
        for low in range(0, width, chunk):
            start = (core if side == 0 else 1 - core) * width + low
            column = pl.ds(pl.multiple_of(start, chunk), chunk)
            rows = both_panels(own[:, column], piece[:, low : low + chunk])
            held = buffer.at[:, side * width + low : side * width + low + chunk]
            held[...] = jnp.dot(weights, rows, preferred_element_type=jnp.float32).astype(out.dtype)
            copy = pltpu.make_async_copy(held, out.at[:, column], sems.at[len(copies)])
            copy.start()
            copies.append(copy)
    for copy in copies:
        copy.wait()


def spread(full, part, got, own, mine, theirs, after):
    tokens = part.shape[1]
    rows, width = own.shape
    chunk = min(width // 2, 1024)
    return pl.pallas_call(
        functools.partial(spread_kernel, chunk),
        in_specs=[WHOLE] * 7,
        out_specs=FAR,
        out_shape=jax.ShapeDtypeStruct((tokens, width), jnp.bfloat16),
        scratch_shapes=[
            pltpu.VMEM((tokens, width), jnp.bfloat16),
            pltpu.SemaphoreType.DMA((width // chunk,)),
        ],
        compiler_params=PARAMS,
        cost_estimate=SMALL,
        name="spread",
    )(*map(near, (full, part, got, own, mine, theirs, after)))


def settle_kernel(full, keep, got, held, send):
    slots, block = held.shape[1:]
    full_here = own_is_full(full[...])
    first = lax.broadcasted_iota(jnp.int32, (slots, block), 0) == 0
    total = keep[0] + got[0].astype(jnp.float32)
    for n, row in ((0, 1), (1, 0)):
        rows = total[n * slots : (n + 1) * slots]
        short = jnp.where(first, total[2 * slots + row : 2 * slots + row + 1], 0.0)
        held[n] = jnp.where(full_here, rows, short)
        send[n] = jnp.where(full_here, short, rows).astype(send.dtype)


def settle(full, keep, got):
    rows, block = keep.shape[1:]
    shape = (2, (rows - PAD) // 2, block)
    return pl.pallas_call(
        settle_kernel,
        in_specs=[WHOLE] * 3,
        out_specs=[WHOLE, WHOLE],
        out_shape=[pltpu.VMEM(shape, jnp.float32), pltpu.VMEM(shape, jnp.bfloat16)],
        compiler_params=PARAMS,
        cost_estimate=SMALL,
        name="settle",
    )(near(full), near(keep), near(got))


def place_kernel(held, got, left_out, right_out):
    here = lax.axis_index("tensor") == 0
    for n, out in enumerate((left_out, right_out)):
        arrived = got[n].astype(out.dtype)
        out[:, 0, 0, :] = jnp.where(here, held[n], arrived)
        out[:, 1, 0, :] = jnp.where(here, arrived, held[n])


def place(held, got):
    shape = jax.ShapeDtypeStruct((held.shape[1], 2, 1, held.shape[2]), jnp.float32)
    return pl.pallas_call(
        place_kernel,
        in_specs=[WHOLE, WHOLE],
        out_specs=[WHOLE, WHOLE],
        out_shape=[shape, shape],
        compiler_params=PARAMS,
        cost_estimate=SMALL,
        name="place",
    )(near(held), near(got))


def pick_kernel(*refs):
    sources, outs, sems = refs[:2], refs[2:4], refs[4]
    part = outs[0].shape[1]
    core = lax.axis_index("dp") % 2
    column = ((1 - lax.axis_index("tensor")) * 2 + core) * part
    here = pl.ds(pl.multiple_of(column, part), part)
    copies = [
        pltpu.make_async_copy(source.at[:, here], out, sems.at[n])
        for n, (source, out) in enumerate(zip(sources, outs))
    ]
    for copy in copies:
        copy.start()
    for copy in copies:
        copy.wait()


def pick(right, left):
    slots, width = left.shape
    return pl.pallas_call(
        pick_kernel,
        in_specs=[FAR] * 2,
        out_specs=[WHOLE] * 2,
        out_shape=[pltpu.VMEM((slots, width // 4), left.dtype)] * 2,
        scratch_shapes=[pltpu.SemaphoreType.DMA((2,))],
        compiler_params=PARAMS,
        cost_estimate=SMALL,
        name="pick",
    )(far(right), far(left))


def quarter_kernel(*refs):
    keeps, gots, outs = refs[:2], refs[2:4], refs[4:]
    blocks = outs[0].shape[0]
    place = lax.axis_index("dp") // 2
    for n, out in enumerate(outs):
        bit_1, bit_2 = (place + n % 2) % 2, (place // 2 + n // 2) % 2
        first = (bit_1 * 2 + bit_2) * blocks
        row = 0
        for keep, got in zip(keeps, gots):
            rows = keep.shape[1]
            for block in range(blocks):
                total = keep[first + block] + got[first + block].astype(jnp.float32)
                out[block, row : row + rows] = total.astype(out.dtype)
            row += rows


def quarter(keeps, gots):
    blocks, _, block = keeps[0].shape
    shape = (blocks // 4, sum(keep.shape[1] for keep in keeps), block)
    return pl.pallas_call(
        quarter_kernel,
        in_specs=[WHOLE] * 4,
        out_specs=[WHOLE] * 4,
        out_shape=[pltpu.VMEM(shape, jnp.float32)] + [pltpu.VMEM(shape, jnp.bfloat16)] * 3,
        compiler_params=PARAMS,
        cost_estimate=SMALL,
        name="quarter",
    )(*map(near, (*keeps, *gots)))


def halve_kernel(bit, keep, *refs):
    gots, (keep_out, send_out) = refs[:-2], refs[-2:]
    blocks = keep_out.shape[0]
    even = (lax.axis_index("dp") // (1 << bit)) % 2 == 0
    low, high = keep[:blocks], keep[blocks:]
    for got in gots:
        low += got[:blocks].astype(jnp.float32)
        high += got[blocks:].astype(jnp.float32)
    keep_out[...] = jnp.where(even, low, high)
    send_out[...] = jnp.where(even, high, low).astype(send_out.dtype)


def halve(keep, gots, bit):
    blocks, rows, block = keep.shape
    shape = (blocks // 2, rows, block)
    return pl.pallas_call(
        functools.partial(halve_kernel, bit),
        in_specs=[WHOLE] * (1 + len(gots)),
        out_specs=[WHOLE, WHOLE],
        out_shape=[pltpu.VMEM(shape, jnp.float32), pltpu.VMEM(shape, jnp.bfloat16)],
        compiler_params=PARAMS,
        cost_estimate=SMALL,
        name="halve",
    )(*map(near, (keep, *gots)))


def two_panels(tokens, cotangent, left_factor, right_factor, panel_rank):
    scale = 1.0 / math.sqrt(tokens.shape[0] * lax.axis_size("dp"))

    right_wanted, left_wanted = pick(right_factor, left_factor)
    right_mine = lax.ppermute(right_wanted, "tensor", SWAP)
    left_mine = lax.ppermute(left_wanted, "tensor", SWAP)
    right_own, cotangent, left_own, tokens, full = stage(
        panel_rank, right_factor, cotangent, left_factor, tokens, (right_wanted, left_wanted)
    )
    right_mine = after_all(right_mine, left_own)
    right_theirs = flip(right_mine, 0)
    back = project(right_own, right_mine, cotangent, False, (), ())
    left_mine = after_all(left_mine, back)
    left_theirs = flip(left_mine, 0)
    back = project(right_own, right_theirs, cotangent, True, (back, full), ())
    hidden = project(left_own, left_mine, tokens, False, (), (cotangent,))
    hidden = project(left_own, left_theirs, tokens, True, (hidden, full), (cotangent,))
    back, hidden = lax.optimization_barrier((back, hidden))
    back_got = lax.ppermute(back, "tensor", SWAP)
    hidden_got = lax.ppermute(hidden, "tensor", SWAP)

    left_keep, left_send, extra = gradient(
        back, back_got, tokens, scale, (), (cotangent,)
    )
    left_got = flip(left_send, 0)
    right_keep, right_send = gradient(hidden, hidden_got, cotangent, scale, (extra,), ())
    right_got = flip(right_send, 0)
    keep, *sends = quarter((left_keep, right_keep), (left_got, right_got))
    gots = [flip(sends[2], 1, 2), flip(sends[0], 1), flip(sends[1], 2)]
    token_grad = spread(full, back, back_got, left_own, left_mine, left_theirs, sends[0])
    gots[0] = after_all(gots[0], token_grad)
    for bit in range(3, lax.axis_size("dp").bit_length() - 1):
        keep, send = halve(keep, gots, bit)
        gots = (flip(send, bit),)

    held, send = settle(full, keep, gots[0])
    return token_grad, *place(held, lax.ppermute(send, "tensor", SWAP))


def solution(mesh):
    placed = (P("dp", "tensor"), P("dp", "tensor"), P("tensor", None), P("tensor", None), P())
    size = mesh.shape["dp"]
    halves = size & (size - 1) == 0 and size >= 16
    return jax.shard_map(
        two_panels if mesh.shape["tensor"] == 2 and halves else any_panels,
        mesh=mesh,
        in_specs=placed,
        out_specs=(P("dp", "tensor"), P("tensor", None, "dp", None), P("tensor", None, "dp", None)),
        check_vma=False,
    )
```

```python
import functools
import math

import jax
import jax.numpy as jnp
from jax import lax
from jax.experimental import pallas as pl
from jax.experimental.pallas import tpu as pltpu
from jax.sharding import PartitionSpec as P


def block_view(home):
    groups = lax.axis_size("tensor")
    width = lax.axis_size("dp")
    block = home.shape[1] // (groups * width)
    return home.reshape(home.shape[0], groups, width, block)


def own_blocks(summed):
    return lax.dynamic_slice_in_dim(summed, lax.axis_index("dp"), 1, 2)


def settle_both(left_cols, right_cols):
    left_home, right_home = (
        lax.all_to_all(left_cols, "tensor", split_axis=0, concat_axis=1, tiled=True),
        lax.all_to_all(right_cols, "tensor", split_axis=0, concat_axis=1, tiled=True),
    )
    left_home = block_view(left_home)
    right_home = block_view(right_home)
    left_sum, right_sum = lax.psum((left_home, right_home), "dp")
    return (own_blocks(left_sum), own_blocks(right_sum))


def any_panels(tokens, cotangent, left_factor, right_factor, panel_rank):
    slot_count = left_factor.shape[0]
    groups = lax.axis_size("tensor")
    all_slots = slot_count * groups
    left_cols, right_cols = (
        lax.all_to_all(left_factor, "tensor", split_axis=1, concat_axis=0, tiled=True),
        lax.all_to_all(right_factor, "tensor", split_axis=1, concat_axis=0, tiled=True),
    )
    slots = jnp.arange(all_slots, dtype=jnp.int32)
    limits = jnp.repeat(panel_rank, slot_count, total_repeat_length=all_slots)
    live_rows = (slots % slot_count < limits).astype(jnp.bfloat16)[:, None]
    left_live = left_cols * live_rows
    right_live = right_cols * live_rows
    feature_dims = (((1,), (1,)), ((), ()))
    hidden_part = lax.dot_general(
        tokens, left_live, feature_dims, preferred_element_type=jnp.float32
    )
    back_part = lax.dot_general(
        cotangent, right_live, feature_dims, preferred_element_type=jnp.float32
    )
    hidden, back_hidden = lax.psum((hidden_part, back_part), "tensor")
    hidden = hidden.astype(jnp.bfloat16)
    back_hidden = back_hidden.astype(jnp.bfloat16)
    grad_scale = 1.0 / math.sqrt(tokens.shape[0] * lax.axis_size("dp"))
    token_dims = (((0,), (0,)), ((), ()))
    right_local = (
        lax.dot_general(hidden, cotangent, token_dims, preferred_element_type=jnp.float32)
        * grad_scale
    )
    left_local = (
        lax.dot_general(back_hidden, tokens, token_dims, preferred_element_type=jnp.float32)
        * grad_scale
    )
    token_grad = jnp.dot(back_hidden, left_live, preferred_element_type=jnp.float32).astype(
        jnp.bfloat16
    )
    left_grad, right_grad = settle_both(left_local, right_local)
    return (token_grad, left_grad, right_grad)


PAD = 8
SWAP = [(0, 1), (1, 0)]
WHOLE = pl.BlockSpec(memory_space=pltpu.VMEM)
FAR = pl.BlockSpec(memory_space=pltpu.HBM)
SMALL = pl.CostEstimate(flops=1, bytes_accessed=1, transcendentals=0)
LONG = pl.CostEstimate(flops=10**10, bytes_accessed=10**8, transcendentals=0)
PARAMS = pltpu.CompilerParams(vmem_limit_bytes=16 * 1024 * 1024)


def near(value):
    return pltpu.with_memory_space_constraint(value, pltpu.VMEM)


def far(value):
    return pltpu.with_memory_space_constraint(value, pltpu.HBM)


def flip(value, *bits):
    mask = sum(1 << bit for bit in bits)
    return lax.ppermute(value, "dp", [(i, i ^ mask) for i in range(lax.axis_size("dp"))])


def after_all(value, *others):
    return lax.optimization_barrier((value, *others))[0]


def stage_kernel(parts, rank, *refs):
    sources, outs, full_out, rank_here, sems = refs[:4], refs[6:10], *refs[10:]
    copies = [pltpu.make_async_copy(rank, rank_here, sems.at[0])]
    for source, out in zip(sources, outs):
        if source.shape == out.shape:
            rows = source.shape[0] // parts
            pairs = [
                (source.at[pl.ds(n * rows, rows)], out.at[pl.ds(n * rows, rows)])
                for n in range(parts)
            ]
        else:
            width = out.shape[1]
            column = pl.multiple_of(lax.axis_index("tensor") * width, width)
            pairs = [(source.at[:, pl.ds(column, width)], out)]
        for pair in pairs:
            copies.append(pltpu.make_async_copy(*pair, sems.at[len(copies)]))
    for copy in copies:
        copy.start()
    copies.pop(0).wait()
    own_rank = jnp.where(lax.axis_index("tensor") == 0, rank_here[0], rank_here[1])
    full = (own_rank == outs[0].shape[0]).astype(jnp.float32)
    full_out[...] = jnp.full(full_out.shape, full)
    for copy in copies:
        copy.wait()


def stage(rank, right, cotangent, left, tokens, after):
    acts = pltpu.VMEM(tokens.shape, tokens.dtype)
    own = pltpu.VMEM((left.shape[0], tokens.shape[1]), left.dtype)
    parts = 8 if tokens.shape[0] % 128 == 0 else 1
    return pl.pallas_call(
        functools.partial(stage_kernel, parts),
        in_specs=[FAR] * 5 + [WHOLE] * 2,
        out_specs=[WHOLE] * 5,
        out_shape=[own, acts, own, acts, pltpu.VMEM((8, 128), jnp.float32)],
        scratch_shapes=[
            pltpu.SMEM(rank.shape, rank.dtype),
            pltpu.SemaphoreType.DMA((3 + 2 * parts,)),
        ],
        compiler_params=PARAMS,
        cost_estimate=SMALL,
        name="stage",
    )(*map(far, (rank, right, cotangent, left, tokens)), *map(near, after))


def own_is_full(full):
    return full[0:1, 0:1] > 0.5


def both_panels(own, piece):
    gap = jnp.zeros((PAD, piece.shape[1]), piece.dtype)
    return jnp.concatenate([own, gap, piece, gap], axis=0)


def project_kernel(flipped, chunk, given, *refs):
    own, piece, acts = refs[:3]
    others, out = refs[3 : 3 + given], refs[-1]
    slots, width = piece.shape
    core = lax.axis_index("dp") % 2
    start = (1 - core if flipped else core) * width
    total = None
    for low in range(0, width, chunk):
        column = pl.ds(pl.multiple_of(start + low, chunk), chunk)
        rows = both_panels(own[:, column], piece[:, low : low + chunk])
        part = lax.dot_general(
            rows, acts[:, column], (((1,), (1,)), ((), ())), preferred_element_type=jnp.float32
        )
        total = part if total is None else total + part
    if others:
        total += others[0][...]
        full_here = own_is_full(others[1][...])
        own_part, other_part = total[:slots], total[slots + PAD : 2 * slots + PAD]
        out[:slots] = jnp.where(full_here, own_part, other_part)
        short = jnp.where(full_here, other_part[:PAD], own_part[:PAD])
        first = lax.broadcasted_iota(jnp.int32, short.shape, 0) == 0
        out[slots:] = jnp.where(first, short, 0.0)
    else:
        out[...] = total


def project(own, piece, acts, flipped, others, held):
    slots, width = piece.shape
    tokens = acts.shape[0]
    rows = slots + PAD if others else 2 * (slots + PAD)
    return pl.pallas_call(
        functools.partial(project_kernel, flipped, min(width, 2048), len(others)),
        in_specs=[WHOLE] * (3 + len(others) + len(held)),
        out_specs=WHOLE,
        out_shape=pltpu.VMEM((rows, tokens), jnp.float32),
        compiler_params=PARAMS,
        cost_estimate=SMALL,
        name="project",
    )(*map(near, (own, piece, acts, *others, *held)))


def gradient_kernel(scale, places, own, given, held, part, got, acts, *refs):
    outs = refs[given + held :]
    keep, send = outs[:2]
    block = keep.shape[2]
    slots = part.shape[0] - PAD
    position = lax.axis_index("dp")
    even = position % 2 == 0
    bit_3 = (position // 8 + (0 if own else 1)) % 2
    summed = (part[...] + got[...]).astype(jnp.bfloat16)
    row = lax.broadcasted_iota(jnp.int32, (PAD, 2 * block), 0)
    for j, q in enumerate(places):
        start = (bit_3 * len(places) + j) * 2 * block
        columns = pl.ds(pl.multiple_of(start, 2 * block), 2 * block)
        grad = jnp.dot(summed, acts[:, columns], preferred_element_type=jnp.float32) * scale
        if given:
            short = jnp.where(row == 1, refs[0][q, 0:1, :], grad[slots:])
            grad = jnp.concatenate([grad[:slots], short], axis=0)
        else:
            outs[2][q] = grad[slots:]
            grad = grad[:slots]
        low, high = grad[:, :block], grad[:, block:]
        keep[q] = jnp.where(even, low, high)
        send[q] = jnp.where(even, high, low).astype(send.dtype)


def gradient(part, got, acts, scale, own, extra, held):
    live, tokens = part.shape
    slots = live - PAD
    width = acts.shape[1]
    block = width // lax.axis_size("dp")
    places = (0, 2, 1, 3)
    shape = (len(places), live if extra else slots, block)
    shapes = [pltpu.VMEM(shape, jnp.float32), pltpu.VMEM(shape, jnp.bfloat16)]
    if not extra:
        shapes.append(pltpu.VMEM((len(places), PAD, 2 * block), jnp.float32))
    return pl.pallas_call(
        functools.partial(gradient_kernel, scale, places, own, len(extra), len(held)),
        in_specs=[WHOLE] * (3 + len(extra) + len(held)),
        out_specs=[WHOLE] * len(shapes),
        out_shape=shapes,
        compiler_params=PARAMS,
        cost_estimate=SMALL,
        name="gradient",
    )(*map(near, (part, got, acts, *extra, *held)))


def spread_kernel(theirs, chunk, given, full, part, got, own, piece, *refs):
    out, buffer, sems = refs[given:]
    slots, width = piece.shape
    full_here = own_is_full(full[...])
    back = part[...] + got[...]
    first = lax.broadcasted_iota(jnp.int32, (slots, back.shape[1]), 0) == 0
    short = jnp.where(first, back[slots : slots + 1], 0.0)
    of_own = jnp.where(full_here, back[:slots], short)
    of_other = jnp.where(full_here, short, back[:slots])
    gap = jnp.zeros((PAD, back.shape[1]), jnp.float32)
    weights = jnp.concatenate([of_own, gap, of_other, gap], axis=0).T.astype(jnp.bfloat16)
    core = lax.axis_index("dp") % 2
    start = (1 - core if theirs else core) * width
    copies = []
    for low in range(0, width, chunk):
        column = pl.ds(pl.multiple_of(start + low, chunk), chunk)
        rows = both_panels(own[:, column], piece[:, low : low + chunk])
        held = buffer.at[:, low : low + chunk]
        held[...] = jnp.dot(weights, rows, preferred_element_type=jnp.float32).astype(out.dtype)
        copy = pltpu.make_async_copy(held, out.at[:, column], sems.at[len(copies)])
        copy.start()
        copies.append(copy)
    for copy in copies:
        copy.wait()


def spread(full, part, got, own, piece, after, before):
    tokens = part.shape[1]
    width = piece.shape[1]
    chunk = min(width, 1024)
    operands = tuple(map(near, (full, part, got, own, piece, after)))
    return pl.pallas_call(
        functools.partial(spread_kernel, len(before) > 0, chunk, 1 + len(before)),
        in_specs=[WHOLE] * len(operands) + [FAR] * len(before),
        out_specs=FAR,
        out_shape=jax.ShapeDtypeStruct((tokens, 2 * width), jnp.bfloat16),
        input_output_aliases={len(operands): 0} if before else {},
        scratch_shapes=[
            pltpu.VMEM((tokens, width), jnp.bfloat16),
            pltpu.SemaphoreType.DMA((width // chunk,)),
        ],
        compiler_params=PARAMS,
        cost_estimate=LONG,
        name="spread",
    )(*operands, *before)


def settle_kernel(count, full, keep, *refs):
    gots, (held, send) = refs[:count], refs[count:]
    slots, block = held.shape[1:]
    full_here = own_is_full(full[...])
    first = lax.broadcasted_iota(jnp.int32, (slots, block), 0) == 0
    total = keep[...]
    for got in gots:
        total += got[...].astype(jnp.float32)
    for n, row in ((0, 1), (1, 0)):
        rows = total[n * slots : (n + 1) * slots]
        short = jnp.where(first, total[2 * slots + row : 2 * slots + row + 1], 0.0)
        held[n] = jnp.where(full_here, rows, short)
        send[n] = jnp.where(full_here, short, rows).astype(send.dtype)


def settle(full, keep, gots):
    rows, block = keep.shape
    shape = (2, (rows - PAD) // 2, block)
    return pl.pallas_call(
        functools.partial(settle_kernel, len(gots)),
        in_specs=[WHOLE] * (2 + len(gots)),
        out_specs=[WHOLE, WHOLE],
        out_shape=[pltpu.VMEM(shape, jnp.float32), pltpu.VMEM(shape, jnp.bfloat16)],
        compiler_params=PARAMS,
        cost_estimate=SMALL,
        name="settle",
    )(*map(near, (full, keep, *gots)))


def place_kernel(held, got, left_out, right_out):
    here = lax.axis_index("tensor") == 0
    for n, out in enumerate((left_out, right_out)):
        arrived = got[n].astype(out.dtype)
        out[:, 0, 0, :] = jnp.where(here, held[n], arrived)
        out[:, 1, 0, :] = jnp.where(here, arrived, held[n])


def place(held, got):
    shape = jax.ShapeDtypeStruct((held.shape[1], 2, 1, held.shape[2]), jnp.float32)
    return pl.pallas_call(
        place_kernel,
        in_specs=[WHOLE, WHOLE],
        out_specs=[WHOLE, WHOLE],
        out_shape=[shape, shape],
        compiler_params=PARAMS,
        cost_estimate=SMALL,
        name="place",
    )(near(held), near(got))


def pick_kernel(*refs):
    sources, outs, sems = refs[:2], refs[2:4], refs[4]
    part = outs[0].shape[1]
    core = lax.axis_index("dp") % 2
    column = ((1 - lax.axis_index("tensor")) * 2 + core) * part
    here = pl.ds(pl.multiple_of(column, part), part)
    copies = [
        pltpu.make_async_copy(source.at[:, here], out, sems.at[n])
        for n, (source, out) in enumerate(zip(sources, outs))
    ]
    for copy in copies:
        copy.start()
    for copy in copies:
        copy.wait()


def pick(right, left):
    slots, width = left.shape
    return pl.pallas_call(
        pick_kernel,
        in_specs=[FAR] * 2,
        out_specs=[WHOLE] * 2,
        out_shape=[pltpu.VMEM((slots, width // 4), left.dtype)] * 2,
        scratch_shapes=[pltpu.SemaphoreType.DMA((2,))],
        compiler_params=PARAMS,
        cost_estimate=SMALL,
        name="pick",
    )(far(right), far(left))


def quarter_kernel(*refs):
    keeps, gots, outs = refs[:2], refs[2:4], refs[4:]
    place = lax.axis_index("dp") // 2
    for n, out in enumerate(outs):
        block = (place + n % 2) % 2 * 2 + (place // 2 + n // 2) % 2
        row = 0
        for keep, got in zip(keeps, gots):
            rows = keep.shape[1]
            total = keep[block] + got[block].astype(jnp.float32)
            out[row : row + rows] = total.astype(out.dtype)
            row += rows


def quarter(keeps, gots):
    shape = (sum(keep.shape[1] for keep in keeps), keeps[0].shape[2])
    return pl.pallas_call(
        quarter_kernel,
        in_specs=[WHOLE] * 4,
        out_specs=[WHOLE] * 4,
        out_shape=[pltpu.VMEM(shape, kind) for kind in [jnp.float32] + [jnp.bfloat16] * 3],
        compiler_params=PARAMS,
        cost_estimate=SMALL,
        name="quarter",
    )(*map(near, (*keeps, *gots)))


def trade(sends):
    return [flip(sends[2], 1, 2), flip(sends[0], 1), flip(sends[1], 2)]


def add_kernel(*refs):
    total = refs[0][...]
    for got in refs[1:-1]:
        total += got[...].astype(jnp.float32)
    refs[-1][...] = total.astype(refs[-1].dtype)


def add(keep, gots, kind):
    return pl.pallas_call(
        add_kernel,
        in_specs=[WHOLE] * (1 + len(gots)),
        out_specs=WHOLE,
        out_shape=pltpu.VMEM(keep.shape, kind),
        compiler_params=PARAMS,
        cost_estimate=SMALL,
        name="add",
    )(*map(near, (keep, *gots)))


def two_panels(tokens, cotangent, left_factor, right_factor, panel_rank):
    scale = 1.0 / math.sqrt(tokens.shape[0] * lax.axis_size("dp"))

    right_wanted, left_wanted = pick(right_factor, left_factor)
    right_mine = lax.ppermute(right_wanted, "tensor", SWAP)
    left_mine = lax.ppermute(left_wanted, "tensor", SWAP)
    right_own, cotangent, left_own, tokens, full = stage(
        panel_rank, right_factor, cotangent, left_factor, tokens, (right_wanted, left_wanted)
    )
    right_mine = after_all(right_mine, left_own)
    right_theirs = flip(right_mine, 0)
    back = project(right_own, right_mine, cotangent, False, (), ())
    left_mine = after_all(left_mine, back)
    left_theirs = flip(left_mine, 0)
    back = project(right_own, right_theirs, cotangent, True, (back, full), ())
    hidden = project(left_own, left_mine, tokens, False, (), (cotangent,))
    hidden = project(left_own, left_theirs, tokens, True, (hidden, full), (cotangent,))
    back, hidden = lax.optimization_barrier((back, hidden))
    back_got = lax.ppermute(back, "tensor", SWAP)
    hidden_got = lax.ppermute(hidden, "tensor", SWAP)

    lefts = [
        gradient(back, back_got, tokens, scale, own, (), (cotangent,)) for own in (False, True)
    ]
    quarters = []
    for own, (left_keep, left_send, extra) in enumerate(lefts):
        right_keep, right_send = gradient(
            hidden, hidden_got, cotangent, scale, own == 1, (extra,), (lefts[1][1],)
        )
        quarters.append(
            quarter((left_keep, right_keep), (flip(left_send, 0), flip(right_send, 0)))
        )
    other, own = quarters
    other_gots, own_gots = trade(other[1:]), trade(own[1:])
    got = flip(add(other[0], other_gots, jnp.bfloat16), 3)
    keep = add(own[0], own_gots, jnp.float32)
    token_grad = spread(full, back, back_got, left_own, left_mine, keep, ())
    got = after_all(got, token_grad)

    held, send = settle(full, keep, (got,))
    got = lax.ppermute(send, "tensor", SWAP)
    token_grad = spread(full, back, back_got, left_own, left_theirs, send, (token_grad,))
    return token_grad, *place(held, after_all(got, token_grad))


def solution(mesh):
    placed = (P("dp", "tensor"), P("dp", "tensor"), P("tensor", None), P("tensor", None), P())
    return jax.shard_map(
        two_panels if (mesh.shape["tensor"], mesh.shape["dp"]) == (2, 16) else any_panels,
        mesh=mesh,
        in_specs=placed,
        out_specs=(P("dp", "tensor"), P("tensor", None, "dp", None), P("tensor", None, "dp", None)),
        check_vma=False,
    )
```

```python
import functools
import math

import jax
import jax.numpy as jnp
from jax import lax
from jax.experimental import pallas as pl
from jax.experimental.pallas import tpu as pltpu
from jax.sharding import PartitionSpec as P


def block_view(home):
    groups = lax.axis_size("tensor")
    width = lax.axis_size("dp")
    block = home.shape[1] // (groups * width)
    return home.reshape(home.shape[0], groups, width, block)


def own_blocks(summed):
    return lax.dynamic_slice_in_dim(summed, lax.axis_index("dp"), 1, 2)


def settle_both(left_cols, right_cols):
    left_home, right_home = (
        lax.all_to_all(left_cols, "tensor", split_axis=0, concat_axis=1, tiled=True),
        lax.all_to_all(right_cols, "tensor", split_axis=0, concat_axis=1, tiled=True),
    )
    left_home = block_view(left_home)
    right_home = block_view(right_home)
    left_sum, right_sum = lax.psum((left_home, right_home), "dp")
    return (own_blocks(left_sum), own_blocks(right_sum))


def any_panels(tokens, cotangent, left_factor, right_factor, panel_rank):
    slot_count = left_factor.shape[0]
    groups = lax.axis_size("tensor")
    all_slots = slot_count * groups
    left_cols, right_cols = (
        lax.all_to_all(left_factor, "tensor", split_axis=1, concat_axis=0, tiled=True),
        lax.all_to_all(right_factor, "tensor", split_axis=1, concat_axis=0, tiled=True),
    )
    slots = jnp.arange(all_slots, dtype=jnp.int32)
    limits = jnp.repeat(panel_rank, slot_count, total_repeat_length=all_slots)
    live_rows = (slots % slot_count < limits).astype(jnp.bfloat16)[:, None]
    left_live = left_cols * live_rows
    right_live = right_cols * live_rows
    feature_dims = (((1,), (1,)), ((), ()))
    hidden_part = lax.dot_general(
        tokens, left_live, feature_dims, preferred_element_type=jnp.float32
    )
    back_part = lax.dot_general(
        cotangent, right_live, feature_dims, preferred_element_type=jnp.float32
    )
    hidden, back_hidden = lax.psum((hidden_part, back_part), "tensor")
    hidden = hidden.astype(jnp.bfloat16)
    back_hidden = back_hidden.astype(jnp.bfloat16)
    grad_scale = 1.0 / math.sqrt(tokens.shape[0] * lax.axis_size("dp"))
    token_dims = (((0,), (0,)), ((), ()))
    right_local = (
        lax.dot_general(hidden, cotangent, token_dims, preferred_element_type=jnp.float32)
        * grad_scale
    )
    left_local = (
        lax.dot_general(back_hidden, tokens, token_dims, preferred_element_type=jnp.float32)
        * grad_scale
    )
    token_grad = jnp.dot(back_hidden, left_live, preferred_element_type=jnp.float32).astype(
        jnp.bfloat16
    )
    left_grad, right_grad = settle_both(left_local, right_local)
    return (token_grad, left_grad, right_grad)


PAD = 8
SWAP = [(0, 1), (1, 0)]
WHOLE = pl.BlockSpec(memory_space=pltpu.VMEM)
FAR = pl.BlockSpec(memory_space=pltpu.HBM)
SMALL = pl.CostEstimate(flops=1, bytes_accessed=1, transcendentals=0)
LONG = pl.CostEstimate(flops=10**10, bytes_accessed=10**8, transcendentals=0)
PARAMS = pltpu.CompilerParams(vmem_limit_bytes=16 * 1024 * 1024)


def near(value):
    return pltpu.with_memory_space_constraint(value, pltpu.VMEM)


def far(value):
    return pltpu.with_memory_space_constraint(value, pltpu.HBM)


def flip(value, *bits):
    mask = sum(1 << bit for bit in bits)
    return lax.ppermute(value, "dp", [(i, i ^ mask) for i in range(lax.axis_size("dp"))])


def after_all(value, *others):
    return lax.optimization_barrier((value, *others))[0]


def stage_kernel(parts, rank, *refs):
    sources, outs, full_out, rank_here, sems = refs[:4], refs[6:10], *refs[10:]
    copies = [pltpu.make_async_copy(rank, rank_here, sems.at[0])]
    for source, out in zip(sources, outs):
        if source.shape == out.shape:
            rows = source.shape[0] // parts
            pairs = [
                (source.at[pl.ds(n * rows, rows)], out.at[pl.ds(n * rows, rows)])
                for n in range(parts)
            ]
        else:
            width = out.shape[1]
            column = pl.multiple_of(lax.axis_index("tensor") * width, width)
            pairs = [(source.at[:, pl.ds(column, width)], out)]
        for pair in pairs:
            copies.append(pltpu.make_async_copy(*pair, sems.at[len(copies)]))
    for copy in copies:
        copy.start()
    copies.pop(0).wait()
    own_rank = jnp.where(lax.axis_index("tensor") == 0, rank_here[0], rank_here[1])
    full = (own_rank == outs[0].shape[0]).astype(jnp.float32)
    full_out[...] = jnp.full(full_out.shape, full)
    for copy in copies:
        copy.wait()


def stage(rank, right, cotangent, left, tokens, after):
    acts = pltpu.VMEM(tokens.shape, tokens.dtype)
    own = pltpu.VMEM((left.shape[0], tokens.shape[1]), left.dtype)
    parts = 8 if tokens.shape[0] % 128 == 0 else 1
    return pl.pallas_call(
        functools.partial(stage_kernel, parts),
        in_specs=[FAR] * 5 + [WHOLE] * 2,
        out_specs=[WHOLE] * 5,
        out_shape=[own, acts, own, acts, pltpu.VMEM((8, 128), jnp.float32)],
        scratch_shapes=[
            pltpu.SMEM(rank.shape, rank.dtype),
            pltpu.SemaphoreType.DMA((3 + 2 * parts,)),
        ],
        compiler_params=PARAMS,
        cost_estimate=SMALL,
        name="stage",
    )(*map(far, (rank, right, cotangent, left, tokens)), *map(near, after))


def across(value):
    pairs = [(i, i ^ 17) for i in range(2 * lax.axis_size("dp"))]
    return lax.ppermute(value, ("dp", "tensor"), pairs)


def own_is_full(full):
    return full[0:1, 0:1] > 0.5


def both_panels(own, piece):
    gap = jnp.zeros((PAD, piece.shape[1]), piece.dtype)
    return jnp.concatenate([own, gap, piece, gap], axis=0)


def project_kernel(flipped, chunk, given, *refs):
    own, piece, acts = refs[:3]
    others, out = refs[3 : 3 + given], refs[-1]
    slots, width = piece.shape
    core = lax.axis_index("dp") % 2
    start = (1 - core if flipped else core) * width
    total = others[0][...] if others else None
    for low in range(0, width, chunk):
        column = pl.ds(pl.multiple_of(start + low, chunk), chunk)
        rows = both_panels(own[:, column], piece[:, low : low + chunk])
        part = lax.dot_general(
            rows, acts[:, column], (((1,), (1,)), ((), ())), preferred_element_type=jnp.float32
        )
        total = part if total is None else total + part
    if given < 3:
        out[...] = total
        return
    full_here = own_is_full(others[1][...])
    shorts = []
    for n, value in enumerate((others[2][...], total)):
        own_part, other_part = value[:slots], value[slots + PAD : 2 * slots + PAD]
        out[n * slots : (n + 1) * slots] = jnp.where(full_here, own_part, other_part)
        shorts.append(jnp.where(full_here, other_part[:1], own_part[:1]))
    row = lax.broadcasted_iota(jnp.int32, (PAD, out.shape[1]), 0)
    out[2 * slots :] = jnp.where(row == 0, shorts[0], jnp.where(row == 1, shorts[1], 0.0))


def project(own, piece, acts, flipped, others, held):
    slots, width = piece.shape
    tokens = acts.shape[0]
    rows = 2 * slots + (PAD if len(others) == 3 else 2 * PAD)
    return pl.pallas_call(
        functools.partial(project_kernel, flipped, min(width, 2048), len(others)),
        in_specs=[WHOLE] * (3 + len(others) + len(held)),
        out_specs=WHOLE,
        out_shape=pltpu.VMEM((rows, tokens), jnp.float32),
        compiler_params=PARAMS,
        cost_estimate=SMALL,
        name="project",
    )(*map(near, (own, piece, acts, *others, *held)))


def summed_rows(parts, got, n):
    slots = (parts.shape[0] - PAD) // 2
    full = slice(n * slots, (n + 1) * slots)
    short = slice(2 * slots + n, 2 * slots + n + 1)
    return parts[full] + got[full], parts[short] + got[short]


def gradient_kernel(scale, places, own, parts, got, tokens, cotangent, *refs):
    keep, send = refs[-2:]
    rows, block = keep.shape[1:]
    slots = (rows - PAD) // 2
    position = lax.axis_index("dp")
    even = position % 2 == 0
    bit_3 = (position // 8 + (0 if own else 1)) % 2
    first = lax.broadcasted_iota(jnp.int32, (PAD, tokens.shape[0]), 0) == 0
    weights = []
    for n in range(2):
        full, short = summed_rows(parts, got, n)
        both = jnp.concatenate([full, jnp.where(first, short, 0.0)], axis=0)
        weights.append(both.astype(jnp.bfloat16))
    row = lax.broadcasted_iota(jnp.int32, (PAD, 2 * block), 0)
    for j, q in enumerate(places):
        start = (bit_3 * len(places) + j) * 2 * block
        columns = pl.ds(pl.multiple_of(start, 2 * block), 2 * block)
        left = jnp.dot(weights[0], tokens[:, columns], preferred_element_type=jnp.float32)
        right = jnp.dot(weights[1], cotangent[:, columns], preferred_element_type=jnp.float32)
        short = jnp.where(row == 1, right[slots : slots + 1], left[slots:])
        grad = jnp.concatenate([left[:slots], right[:slots], short], axis=0) * scale
        low, high = grad[:, :block], grad[:, block:]
        keep[q] = jnp.where(even, low, high)
        send[q] = jnp.where(even, high, low).astype(send.dtype)


def gradient(parts, got, tokens, cotangent, scale, own, after):
    places = (0, 2, 1, 3)
    shape = (len(places), parts.shape[0], tokens.shape[1] // lax.axis_size("dp"))
    return pl.pallas_call(
        functools.partial(gradient_kernel, scale, places, own),
        in_specs=[WHOLE] * (4 + len(after)),
        out_specs=[WHOLE] * 2,
        out_shape=[pltpu.VMEM(shape, jnp.float32), pltpu.VMEM(shape, jnp.bfloat16)],
        compiler_params=PARAMS,
        cost_estimate=SMALL,
        name="gradient",
    )(*map(near, (parts, got, tokens, cotangent, *after)))


def spread_kernel(chunk, full, parts, got, own, mine, theirs, after, out, buffer, sems):
    slots, width = mine.shape
    full_here = own_is_full(full[...])
    back, short = summed_rows(parts, got, 0)
    first = lax.broadcasted_iota(jnp.int32, back.shape, 0) == 0
    short = jnp.where(first, short, 0.0)
    of_own = jnp.where(full_here, back, short)
    of_other = jnp.where(full_here, short, back)
    gap = jnp.zeros((PAD, back.shape[1]), jnp.float32)
    weights = jnp.concatenate([of_own, gap, of_other, gap], axis=0).T.astype(jnp.bfloat16)
    core = lax.axis_index("dp") % 2
    copies = []
    for side, piece in enumerate((mine, theirs)):
        for low in range(0, width, chunk):
            start = (core if side == 0 else 1 - core) * width + low
            column = pl.ds(pl.multiple_of(start, chunk), chunk)
            rows = both_panels(own[:, column], piece[:, low : low + chunk])
            held = buffer.at[:, side * width + low : side * width + low + chunk]
            held[...] = jnp.dot(weights, rows, preferred_element_type=jnp.float32).astype(out.dtype)
            copy = pltpu.make_async_copy(held, out.at[:, column], sems.at[len(copies)])
            copy.start()
            copies.append(copy)
    for copy in copies:
        copy.wait()


def spread(full, parts, got, own, mine, theirs, after):
    tokens = parts.shape[1]
    width = own.shape[1]
    chunk = min(width // 2, 1024)
    return pl.pallas_call(
        functools.partial(spread_kernel, chunk),
        in_specs=[WHOLE] * 7,
        out_specs=FAR,
        out_shape=jax.ShapeDtypeStruct((tokens, width), jnp.bfloat16),
        scratch_shapes=[
            pltpu.VMEM((tokens, width), jnp.bfloat16),
            pltpu.SemaphoreType.DMA((width // chunk,)),
        ],
        compiler_params=PARAMS,
        cost_estimate=LONG,
        name="spread",
    )(*map(near, (full, parts, got, own, mine, theirs, after)))


def settle_kernel(full, keep, *refs):
    gots, (near_out, far_out) = refs[:-2], refs[-2:]
    slots, block = near_out.shape[1:]
    full_here = own_is_full(full[...])
    first = lax.broadcasted_iota(jnp.int32, (slots, block), 0) == 0
    total = keep[...]
    for got in gots:
        total += got[...].astype(jnp.float32)
    for n in range(2):
        rows = total[n * slots : (n + 1) * slots]
        short = jnp.where(first, total[2 * slots + n : 2 * slots + n + 1], 0.0)
        near_out[n] = jnp.where(full_here, rows, short).astype(near_out.dtype)
        far_out[n] = jnp.where(full_here, short, rows).astype(far_out.dtype)


def settle(full, keep, gots, kind):
    rows, block = keep.shape
    shape = (2, (rows - PAD) // 2, block)
    return pl.pallas_call(
        settle_kernel,
        in_specs=[WHOLE] * (2 + len(gots)),
        out_specs=[WHOLE, WHOLE],
        out_shape=[pltpu.VMEM(shape, kind), pltpu.VMEM(shape, jnp.bfloat16)],
        compiler_params=PARAMS,
        cost_estimate=SMALL,
        name="settle",
    )(*map(near, (full, keep, *gots)))


def gather_kernel(*refs):
    total = refs[0][...].astype(jnp.float32)
    for value in refs[1:-1]:
        total += value[...].astype(jnp.float32)
    refs[-1][...] = total


def gather(*values):
    return pl.pallas_call(
        gather_kernel,
        in_specs=[WHOLE] * len(values),
        out_specs=WHOLE,
        out_shape=pltpu.VMEM(values[0].shape, jnp.float32),
        compiler_params=PARAMS,
        cost_estimate=SMALL,
        name="gather",
    )(*map(near, values))


def place_kernel(held, far, got, left_out, right_out):
    here = lax.axis_index("tensor") == 0
    for n, out in enumerate((left_out, right_out)):
        other = far[n] + got[n].astype(out.dtype)
        out[:, 0, 0, :] = jnp.where(here, held[n], other)
        out[:, 1, 0, :] = jnp.where(here, other, held[n])


def place(held, far, got):
    shape = jax.ShapeDtypeStruct((held.shape[1], 2, 1, held.shape[2]), jnp.float32)
    return pl.pallas_call(
        place_kernel,
        in_specs=[WHOLE] * 3,
        out_specs=[WHOLE, WHOLE],
        out_shape=[shape, shape],
        compiler_params=PARAMS,
        cost_estimate=SMALL,
        name="place",
    )(*map(near, (held, far, got)))


def pick_kernel(*refs):
    sources, outs, sems = refs[:2], refs[2:4], refs[4]
    part = outs[0].shape[1]
    core = lax.axis_index("dp") % 2
    column = ((1 - lax.axis_index("tensor")) * 2 + core) * part
    here = pl.ds(pl.multiple_of(column, part), part)
    copies = [
        pltpu.make_async_copy(source.at[:, here], out, sems.at[n])
        for n, (source, out) in enumerate(zip(sources, outs))
    ]
    for copy in copies:
        copy.start()
    for copy in copies:
        copy.wait()


def pick(right, left):
    slots, width = left.shape
    return pl.pallas_call(
        pick_kernel,
        in_specs=[FAR] * 2,
        out_specs=[WHOLE] * 2,
        out_shape=[pltpu.VMEM((slots, width // 4), left.dtype)] * 2,
        scratch_shapes=[pltpu.SemaphoreType.DMA((2,))],
        compiler_params=PARAMS,
        cost_estimate=SMALL,
        name="pick",
    )(far(right), far(left))


def quarter_kernel(keep, got, *outs):
    place = lax.axis_index("dp") // 2
    for n, out in enumerate(outs):
        block = (place + n % 2) % 2 * 2 + (place // 2 + n // 2) % 2
        out[...] = (keep[block] + got[block].astype(jnp.float32)).astype(out.dtype)


def quarter(keep, got):
    kinds = [jnp.float32] + [jnp.bfloat16] * 3
    return pl.pallas_call(
        quarter_kernel,
        in_specs=[WHOLE] * 2,
        out_specs=[WHOLE] * 4,
        out_shape=[pltpu.VMEM(keep.shape[1:], kind) for kind in kinds],
        compiler_params=PARAMS,
        cost_estimate=SMALL,
        name="quarter",
    )(near(keep), near(got))


def trade(sends):
    return [flip(sends[2], 1, 2), flip(sends[0], 1), flip(sends[1], 2)]


def two_panels(tokens, cotangent, left_factor, right_factor, panel_rank):
    scale = 1.0 / math.sqrt(tokens.shape[0] * lax.axis_size("dp"))

    right_wanted, left_wanted = pick(right_factor, left_factor)
    right_mine = lax.ppermute(right_wanted, "tensor", SWAP)
    left_mine = lax.ppermute(left_wanted, "tensor", SWAP)
    right_own, cotangent, left_own, tokens, full = stage(
        panel_rank, right_factor, cotangent, left_factor, tokens, (right_wanted, left_wanted)
    )
    right_mine = after_all(right_mine, left_own)
    right_theirs = flip(right_mine, 0)
    back = project(right_own, right_mine, cotangent, False, (), ())
    left_mine = after_all(left_mine, back)
    left_theirs = flip(left_mine, 0)
    back = project(right_own, right_theirs, cotangent, True, (back,), ())
    hidden = project(left_own, left_mine, tokens, False, (), (cotangent,))
    parts = project(left_own, left_theirs, tokens, True, (hidden, full, back), (cotangent,))
    parts_got = lax.ppermute(parts, "tensor", SWAP)

    acts = (tokens, cotangent)
    other_keep, other_send = gradient(parts, parts_got, *acts, scale, False, ())
    own_keep, own_send = gradient(parts, parts_got, *acts, scale, True, (other_send,))
    other = quarter(other_keep, flip(other_send, 0))
    own = quarter(own_keep, flip(own_send, 0))
    other_gots, own_gots = trade(other[1:]), trade(own[1:])
    near_send, far_send = settle(full, other[0], other_gots, jnp.bfloat16)
    far_got = across(far_send)
    near_got = flip(near_send, 3)
    held, send = settle(full, own[0], own_gots, jnp.float32)
    got = lax.ppermute(send, "tensor", SWAP)
    token_grad = spread(full, parts, parts_got, left_own, left_mine, left_theirs, send)
    far = gather(far_got)
    far, near_got = lax.optimization_barrier((far, near_got))
    held = gather(held, near_got)
    return token_grad, *place(held, far, after_all(got, token_grad, held))


def solution(mesh):
    placed = (P("dp", "tensor"), P("dp", "tensor"), P("tensor", None), P("tensor", None), P())
    return jax.shard_map(
        two_panels if (mesh.shape["tensor"], mesh.shape["dp"]) == (2, 16) else any_panels,
        mesh=mesh,
        in_specs=placed,
        out_specs=(P("dp", "tensor"), P("tensor", None, "dp", None), P("tensor", None, "dp", None)),
        check_vma=False,
    )
```

```python
import functools
import math

import jax
import jax.numpy as jnp
from jax import lax
from jax.experimental import pallas as pl
from jax.experimental.pallas import tpu as pltpu
from jax.sharding import PartitionSpec as P


def block_view(home):
    groups = lax.axis_size("tensor")
    width = lax.axis_size("dp")
    block = home.shape[1] // (groups * width)
    return home.reshape(home.shape[0], groups, width, block)


def own_blocks(summed):
    return lax.dynamic_slice_in_dim(summed, lax.axis_index("dp"), 1, 2)


def settle_both(left_cols, right_cols):
    left_home, right_home = (
        lax.all_to_all(left_cols, "tensor", split_axis=0, concat_axis=1, tiled=True),
        lax.all_to_all(right_cols, "tensor", split_axis=0, concat_axis=1, tiled=True),
    )
    left_home = block_view(left_home)
    right_home = block_view(right_home)
    left_sum, right_sum = lax.psum((left_home, right_home), "dp")
    return (own_blocks(left_sum), own_blocks(right_sum))


def any_panels(tokens, cotangent, left_factor, right_factor, panel_rank):
    slot_count = left_factor.shape[0]
    groups = lax.axis_size("tensor")
    all_slots = slot_count * groups
    left_cols, right_cols = (
        lax.all_to_all(left_factor, "tensor", split_axis=1, concat_axis=0, tiled=True),
        lax.all_to_all(right_factor, "tensor", split_axis=1, concat_axis=0, tiled=True),
    )
    slots = jnp.arange(all_slots, dtype=jnp.int32)
    limits = jnp.repeat(panel_rank, slot_count, total_repeat_length=all_slots)
    live_rows = (slots % slot_count < limits).astype(jnp.bfloat16)[:, None]
    left_live = left_cols * live_rows
    right_live = right_cols * live_rows
    feature_dims = (((1,), (1,)), ((), ()))
    hidden_part = lax.dot_general(
        tokens, left_live, feature_dims, preferred_element_type=jnp.float32
    )
    back_part = lax.dot_general(
        cotangent, right_live, feature_dims, preferred_element_type=jnp.float32
    )
    hidden, back_hidden = lax.psum((hidden_part, back_part), "tensor")
    hidden = hidden.astype(jnp.bfloat16)
    back_hidden = back_hidden.astype(jnp.bfloat16)
    grad_scale = 1.0 / math.sqrt(tokens.shape[0] * lax.axis_size("dp"))
    token_dims = (((0,), (0,)), ((), ()))
    right_local = (
        lax.dot_general(hidden, cotangent, token_dims, preferred_element_type=jnp.float32)
        * grad_scale
    )
    left_local = (
        lax.dot_general(back_hidden, tokens, token_dims, preferred_element_type=jnp.float32)
        * grad_scale
    )
    token_grad = jnp.dot(back_hidden, left_live, preferred_element_type=jnp.float32).astype(
        jnp.bfloat16
    )
    left_grad, right_grad = settle_both(left_local, right_local)
    return (token_grad, left_grad, right_grad)


PAD = 8
SWAP = [(0, 1), (1, 0)]
WHOLE = pl.BlockSpec(memory_space=pltpu.VMEM)
FAR = pl.BlockSpec(memory_space=pltpu.HBM)
SMALL = pl.CostEstimate(flops=1, bytes_accessed=1, transcendentals=0)
LONG = pl.CostEstimate(flops=10**10, bytes_accessed=10**8, transcendentals=0)
PARAMS = pltpu.CompilerParams(vmem_limit_bytes=16 * 1024 * 1024)


def near(value):
    return pltpu.with_memory_space_constraint(value, pltpu.VMEM)


def far(value):
    return pltpu.with_memory_space_constraint(value, pltpu.HBM)


def flip(value, *bits):
    mask = sum(1 << bit for bit in bits)
    return lax.ppermute(value, "dp", [(i, i ^ mask) for i in range(lax.axis_size("dp"))])


def after_all(value, *others):
    return lax.optimization_barrier((value, *others))[0]


def stage_kernel(parts, rank, *refs):
    sources, outs, full_out, rank_here, sems = refs[:4], refs[6:10], *refs[10:]
    copies = [pltpu.make_async_copy(rank, rank_here, sems.at[0])]
    for source, out in zip(sources, outs):
        if source.shape == out.shape:
            rows = source.shape[0] // parts
            pairs = [
                (source.at[pl.ds(n * rows, rows)], out.at[pl.ds(n * rows, rows)])
                for n in range(parts)
            ]
        else:
            width = out.shape[1]
            column = pl.multiple_of(lax.axis_index("tensor") * width, width)
            pairs = [(source.at[:, pl.ds(column, width)], out)]
        for pair in pairs:
            copies.append(pltpu.make_async_copy(*pair, sems.at[len(copies)]))
    for copy in copies:
        copy.start()
    copies.pop(0).wait()
    own_rank = jnp.where(lax.axis_index("tensor") == 0, rank_here[0], rank_here[1])
    full = (own_rank == outs[0].shape[0]).astype(jnp.float32)
    full_out[...] = jnp.full(full_out.shape, full)
    for copy in copies:
        copy.wait()


def stage(rank, right, cotangent, left, tokens, after):
    acts = pltpu.VMEM(tokens.shape, tokens.dtype)
    own = pltpu.VMEM((left.shape[0], tokens.shape[1]), left.dtype)
    parts = 8 if tokens.shape[0] % 128 == 0 else 1
    return pl.pallas_call(
        functools.partial(stage_kernel, parts),
        in_specs=[FAR] * 5 + [WHOLE] * 2,
        out_specs=[WHOLE] * 5,
        out_shape=[own, acts, own, acts, pltpu.VMEM((8, 128), jnp.float32)],
        scratch_shapes=[
            pltpu.SMEM(rank.shape, rank.dtype),
            pltpu.SemaphoreType.DMA((3 + 2 * parts,)),
        ],
        compiler_params=PARAMS,
        cost_estimate=SMALL,
        name="stage",
    )(*map(far, (rank, right, cotangent, left, tokens)), *map(near, after))


def across(value):
    pairs = [(i, i ^ 17) for i in range(2 * lax.axis_size("dp"))]
    return lax.ppermute(value, ("dp", "tensor"), pairs)


def own_is_full(full):
    return full[0:1, 0:1] > 0.5


def both_panels(own, piece):
    gap = jnp.zeros((PAD, piece.shape[1]), piece.dtype)
    return jnp.concatenate([own, gap, piece, gap], axis=0)


def project_kernel(flipped, chunk, given, *refs):
    own, piece, acts = refs[:3]
    others, out = refs[3 : 3 + given], refs[-1]
    slots, width = piece.shape
    core = lax.axis_index("dp") % 2
    start = (1 - core if flipped else core) * width
    total = others[0][...] if others else None
    for low in range(0, width, chunk):
        column = pl.ds(pl.multiple_of(start + low, chunk), chunk)
        rows = both_panels(own[:, column], piece[:, low : low + chunk])
        part = lax.dot_general(
            rows, acts[:, column], (((1,), (1,)), ((), ())), preferred_element_type=jnp.float32
        )
        total = part if total is None else total + part
    if given < 3:
        out[...] = total
        return
    full_here = own_is_full(others[1][...])
    shorts = []
    for n, value in enumerate((others[2][...], total)):
        own_part, other_part = value[:slots], value[slots + PAD : 2 * slots + PAD]
        out[n * slots : (n + 1) * slots] = jnp.where(full_here, own_part, other_part)
        shorts.append(jnp.where(full_here, other_part[:1], own_part[:1]))
    row = lax.broadcasted_iota(jnp.int32, (PAD, out.shape[1]), 0)
    out[2 * slots :] = jnp.where(row == 0, shorts[0], jnp.where(row == 1, shorts[1], 0.0))


def project(own, piece, acts, flipped, others, held):
    slots, width = piece.shape
    tokens = acts.shape[0]
    rows = 2 * slots + (PAD if len(others) == 3 else 2 * PAD)
    return pl.pallas_call(
        functools.partial(project_kernel, flipped, min(width, 2048), len(others)),
        in_specs=[WHOLE] * (3 + len(others) + len(held)),
        out_specs=WHOLE,
        out_shape=pltpu.VMEM((rows, tokens), jnp.float32),
        compiler_params=PARAMS,
        cost_estimate=SMALL,
        name="project",
    )(*map(near, (own, piece, acts, *others, *held)))


def summed_rows(parts, got, n):
    slots = (parts.shape[0] - PAD) // 2
    full = slice(n * slots, (n + 1) * slots)
    short = slice(2 * slots + n, 2 * slots + n + 1)
    return parts[full] + got[full], parts[short] + got[short]


def gradient_kernel(scale, places, own, keep, parts, got, tokens, cotangent, *refs):
    out = refs[-1]
    rows, block = out.shape[1:]
    slots = (rows - PAD) // 2
    position = lax.axis_index("dp")
    core = (position + (0 if keep else 1)) % 2
    bit_3 = (position // 8 + (0 if own else 1)) % 2
    first = lax.broadcasted_iota(jnp.int32, (PAD, tokens.shape[0]), 0) == 0
    weights = []
    for n in range(2):
        full, short = summed_rows(parts, got, n)
        both = jnp.concatenate([full, jnp.where(first, short, 0.0)], axis=0)
        weights.append(both.astype(jnp.bfloat16))
    row = lax.broadcasted_iota(jnp.int32, (PAD, block), 0)
    for j, q in enumerate(places):
        start = ((bit_3 * len(places) + j) * 2 + core) * block
        columns = pl.ds(pl.multiple_of(start, block), block)
        left = jnp.dot(weights[0], tokens[:, columns], preferred_element_type=jnp.float32)
        right = jnp.dot(weights[1], cotangent[:, columns], preferred_element_type=jnp.float32)
        short = jnp.where(row == 1, right[slots : slots + 1], left[slots:])
        grad = jnp.concatenate([left[:slots], right[:slots], short], axis=0) * scale
        out[q] = grad.astype(out.dtype)


def gradient(parts, got, tokens, cotangent, scale, own, keep, after):
    places = (0, 2, 1, 3)
    shape = (len(places), parts.shape[0], tokens.shape[1] // lax.axis_size("dp"))
    return pl.pallas_call(
        functools.partial(gradient_kernel, scale, places, own, keep),
        in_specs=[WHOLE] * (4 + len(after)),
        out_specs=WHOLE,
        out_shape=pltpu.VMEM(shape, jnp.float32 if keep else jnp.bfloat16),
        compiler_params=PARAMS,
        cost_estimate=SMALL,
        name="gradient",
    )(*map(near, (parts, got, tokens, cotangent, *after)))


def spread_kernel(chunk, full, parts, got, own, mine, theirs, after, out, buffer, sems):
    slots, width = mine.shape
    full_here = own_is_full(full[...])
    back, short = summed_rows(parts, got, 0)
    first = lax.broadcasted_iota(jnp.int32, back.shape, 0) == 0
    short = jnp.where(first, short, 0.0)
    of_own = jnp.where(full_here, back, short)
    of_other = jnp.where(full_here, short, back)
    gap = jnp.zeros((PAD, back.shape[1]), jnp.float32)
    weights = jnp.concatenate([of_own, gap, of_other, gap], axis=0).T.astype(jnp.bfloat16)
    core = lax.axis_index("dp") % 2
    copies = []
    for side, piece in enumerate((mine, theirs)):
        for low in range(0, width, chunk):
            start = (core if side == 0 else 1 - core) * width + low
            column = pl.ds(pl.multiple_of(start, chunk), chunk)
            rows = both_panels(own[:, column], piece[:, low : low + chunk])
            held = buffer.at[:, side * width + low : side * width + low + chunk]
            held[...] = jnp.dot(weights, rows, preferred_element_type=jnp.float32).astype(out.dtype)
            copy = pltpu.make_async_copy(held, out.at[:, column], sems.at[len(copies)])
            copy.start()
            copies.append(copy)
    for copy in copies:
        copy.wait()


def spread(full, parts, got, own, mine, theirs, after):
    tokens = parts.shape[1]
    width = own.shape[1]
    chunk = min(width // 2, 1024)
    return pl.pallas_call(
        functools.partial(spread_kernel, chunk),
        in_specs=[WHOLE] * 7,
        out_specs=FAR,
        out_shape=jax.ShapeDtypeStruct((tokens, width), jnp.bfloat16),
        scratch_shapes=[
            pltpu.VMEM((tokens, width), jnp.bfloat16),
            pltpu.SemaphoreType.DMA((width // chunk,)),
        ],
        compiler_params=PARAMS,
        cost_estimate=LONG,
        name="spread",
    )(*map(near, (full, parts, got, own, mine, theirs, after)))


def settle_kernel(full, keep, *refs):
    gots, (near_out, far_out) = refs[:-2], refs[-2:]
    slots, block = near_out.shape[1:]
    full_here = own_is_full(full[...])
    first = lax.broadcasted_iota(jnp.int32, (slots, block), 0) == 0
    total = keep[...]
    for got in gots:
        total += got[...].astype(jnp.float32)
    for n in range(2):
        rows = total[n * slots : (n + 1) * slots]
        short = jnp.where(first, total[2 * slots + n : 2 * slots + n + 1], 0.0)
        near_out[n] = jnp.where(full_here, rows, short).astype(near_out.dtype)
        far_out[n] = jnp.where(full_here, short, rows).astype(far_out.dtype)


def settle(full, keep, gots, kind):
    rows, block = keep.shape
    shape = (2, (rows - PAD) // 2, block)
    return pl.pallas_call(
        settle_kernel,
        in_specs=[WHOLE] * (2 + len(gots)),
        out_specs=[WHOLE, WHOLE],
        out_shape=[pltpu.VMEM(shape, kind), pltpu.VMEM(shape, jnp.bfloat16)],
        compiler_params=PARAMS,
        cost_estimate=SMALL,
        name="settle",
    )(*map(near, (full, keep, *gots)))


def gather_kernel(*refs):
    total = refs[0][...].astype(jnp.float32)
    for value in refs[1:-1]:
        total += value[...].astype(jnp.float32)
    refs[-1][...] = total


def gather(*values):
    return pl.pallas_call(
        gather_kernel,
        in_specs=[WHOLE] * len(values),
        out_specs=WHOLE,
        out_shape=pltpu.VMEM(values[0].shape, jnp.float32),
        compiler_params=PARAMS,
        cost_estimate=SMALL,
        name="gather",
    )(*map(near, values))


def place_kernel(held, far, got, left_out, right_out):
    here = lax.axis_index("tensor") == 0
    for n, out in enumerate((left_out, right_out)):
        other = far[n] + got[n].astype(out.dtype)
        out[:, 0, 0, :] = jnp.where(here, held[n], other)
        out[:, 1, 0, :] = jnp.where(here, other, held[n])


def place(held, far, got):
    shape = jax.ShapeDtypeStruct((held.shape[1], 2, 1, held.shape[2]), jnp.float32)
    return pl.pallas_call(
        place_kernel,
        in_specs=[WHOLE] * 3,
        out_specs=[WHOLE, WHOLE],
        out_shape=[shape, shape],
        compiler_params=PARAMS,
        cost_estimate=SMALL,
        name="place",
    )(*map(near, (held, far, got)))


def pick_kernel(*refs):
    sources, outs, sems = refs[:2], refs[2:4], refs[4]
    part = outs[0].shape[1]
    core = lax.axis_index("dp") % 2
    column = ((1 - lax.axis_index("tensor")) * 2 + core) * part
    here = pl.ds(pl.multiple_of(column, part), part)
    copies = [
        pltpu.make_async_copy(source.at[:, here], out, sems.at[n])
        for n, (source, out) in enumerate(zip(sources, outs))
    ]
    for copy in copies:
        copy.start()
    for copy in copies:
        copy.wait()


def pick(right, left):
    slots, width = left.shape
    return pl.pallas_call(
        pick_kernel,
        in_specs=[FAR] * 2,
        out_specs=[WHOLE] * 2,
        out_shape=[pltpu.VMEM((slots, width // 4), left.dtype)] * 2,
        scratch_shapes=[pltpu.SemaphoreType.DMA((2,))],
        compiler_params=PARAMS,
        cost_estimate=SMALL,
        name="pick",
    )(far(right), far(left))


def quarter_kernel(keep, got, *outs):
    place = lax.axis_index("dp") // 2
    for n, out in enumerate(outs):
        block = (place + n % 2) % 2 * 2 + (place // 2 + n // 2) % 2
        out[...] = (keep[block] + got[block].astype(jnp.float32)).astype(out.dtype)


def quarter(keep, got):
    kinds = [jnp.float32] + [jnp.bfloat16] * 3
    return pl.pallas_call(
        quarter_kernel,
        in_specs=[WHOLE] * 2,
        out_specs=[WHOLE] * 4,
        out_shape=[pltpu.VMEM(keep.shape[1:], kind) for kind in kinds],
        compiler_params=PARAMS,
        cost_estimate=SMALL,
        name="quarter",
    )(near(keep), near(got))


def trade(sends):
    return [flip(sends[2], 1, 2), flip(sends[0], 1), flip(sends[1], 2)]


def two_panels(tokens, cotangent, left_factor, right_factor, panel_rank):
    scale = 1.0 / math.sqrt(tokens.shape[0] * lax.axis_size("dp"))

    right_wanted, left_wanted = pick(right_factor, left_factor)
    right_mine = lax.ppermute(right_wanted, "tensor", SWAP)
    left_mine = lax.ppermute(left_wanted, "tensor", SWAP)
    right_own, cotangent, left_own, tokens, full = stage(
        panel_rank, right_factor, cotangent, left_factor, tokens, (right_wanted, left_wanted)
    )
    right_mine = after_all(right_mine, left_own)
    right_theirs = flip(right_mine, 0)
    back = project(right_own, right_mine, cotangent, False, (), ())
    left_mine = after_all(left_mine, back)
    left_theirs = flip(left_mine, 0)
    back = project(right_own, right_theirs, cotangent, True, (back,), ())
    hidden = project(left_own, left_mine, tokens, False, (), (cotangent,))
    parts = project(left_own, left_theirs, tokens, True, (hidden, full, back), (cotangent,))
    parts_got = lax.ppermute(parts, "tensor", SWAP)

    operands = (parts, parts_got, tokens, cotangent, scale)
    other_send = gradient(*operands, False, False, ())
    other_keep = gradient(*operands, False, True, (other_send,))
    own_send = gradient(*operands, True, False, (other_keep,))
    other = quarter(other_keep, flip(other_send, 0))
    own_keep = gradient(*operands, True, True, (own_send, other[1]))
    own = quarter(own_keep, flip(own_send, 0))
    other_gots, own_gots = trade(other[1:]), trade(own[1:])
    near_send, far_send = settle(full, other[0], other_gots, jnp.bfloat16)
    far_got = across(far_send)
    near_got = flip(near_send, 3)
    held, send = settle(full, own[0], own_gots, jnp.float32)
    got = lax.ppermute(send, "tensor", SWAP)
    token_grad = spread(full, parts, parts_got, left_own, left_mine, left_theirs, send)
    far = gather(far_got)
    far, near_got = lax.optimization_barrier((far, near_got))
    held = gather(held, near_got)
    return token_grad, *place(held, far, after_all(got, token_grad, held))


def solution(mesh):
    placed = (P("dp", "tensor"), P("dp", "tensor"), P("tensor", None), P("tensor", None), P())
    return jax.shard_map(
        two_panels if (mesh.shape["tensor"], mesh.shape["dp"]) == (2, 16) else any_panels,
        mesh=mesh,
        in_specs=placed,
        out_specs=(P("dp", "tensor"), P("tensor", None, "dp", None), P("tensor", None, "dp", None)),
        check_vma=False,
    )
```

```python
import functools
import math

import jax
import jax.numpy as jnp
from jax import lax
from jax.experimental import pallas as pl
from jax.experimental.pallas import tpu as pltpu
from jax.sharding import PartitionSpec as P


def block_view(home):
    groups = lax.axis_size("tensor")
    width = lax.axis_size("dp")
    block = home.shape[1] // (groups * width)
    return home.reshape(home.shape[0], groups, width, block)


def own_blocks(summed):
    return lax.dynamic_slice_in_dim(summed, lax.axis_index("dp"), 1, 2)


def settle_both(left_cols, right_cols):
    left_home, right_home = (
        lax.all_to_all(left_cols, "tensor", split_axis=0, concat_axis=1, tiled=True),
        lax.all_to_all(right_cols, "tensor", split_axis=0, concat_axis=1, tiled=True),
    )
    left_home = block_view(left_home)
    right_home = block_view(right_home)
    left_sum, right_sum = lax.psum((left_home, right_home), "dp")
    return (own_blocks(left_sum), own_blocks(right_sum))


def any_panels(tokens, cotangent, left_factor, right_factor, panel_rank):
    slot_count = left_factor.shape[0]
    groups = lax.axis_size("tensor")
    all_slots = slot_count * groups
    left_cols, right_cols = (
        lax.all_to_all(left_factor, "tensor", split_axis=1, concat_axis=0, tiled=True),
        lax.all_to_all(right_factor, "tensor", split_axis=1, concat_axis=0, tiled=True),
    )
    slots = jnp.arange(all_slots, dtype=jnp.int32)
    limits = jnp.repeat(panel_rank, slot_count, total_repeat_length=all_slots)
    live_rows = (slots % slot_count < limits).astype(jnp.bfloat16)[:, None]
    left_live = left_cols * live_rows
    right_live = right_cols * live_rows
    feature_dims = (((1,), (1,)), ((), ()))
    hidden_part = lax.dot_general(
        tokens, left_live, feature_dims, preferred_element_type=jnp.float32
    )
    back_part = lax.dot_general(
        cotangent, right_live, feature_dims, preferred_element_type=jnp.float32
    )
    hidden, back_hidden = lax.psum((hidden_part, back_part), "tensor")
    hidden = hidden.astype(jnp.bfloat16)
    back_hidden = back_hidden.astype(jnp.bfloat16)
    grad_scale = 1.0 / math.sqrt(tokens.shape[0] * lax.axis_size("dp"))
    token_dims = (((0,), (0,)), ((), ()))
    right_local = (
        lax.dot_general(hidden, cotangent, token_dims, preferred_element_type=jnp.float32)
        * grad_scale
    )
    left_local = (
        lax.dot_general(back_hidden, tokens, token_dims, preferred_element_type=jnp.float32)
        * grad_scale
    )
    token_grad = jnp.dot(back_hidden, left_live, preferred_element_type=jnp.float32).astype(
        jnp.bfloat16
    )
    left_grad, right_grad = settle_both(left_local, right_local)
    return (token_grad, left_grad, right_grad)


PAD = 8
SWAP = [(0, 1), (1, 0)]
WHOLE = pl.BlockSpec(memory_space=pltpu.VMEM)
FAR = pl.BlockSpec(memory_space=pltpu.HBM)
SMALL = pl.CostEstimate(flops=1, bytes_accessed=1, transcendentals=0)
LONG = pl.CostEstimate(flops=10**10, bytes_accessed=10**8, transcendentals=0)
PARAMS = pltpu.CompilerParams(vmem_limit_bytes=16 * 1024 * 1024)


def near(value):
    return pltpu.with_memory_space_constraint(value, pltpu.VMEM)


def far(value):
    return pltpu.with_memory_space_constraint(value, pltpu.HBM)


def flip(value, *bits):
    mask = sum(1 << bit for bit in bits)
    return lax.ppermute(value, "dp", [(i, i ^ mask) for i in range(lax.axis_size("dp"))])


def after_all(value, *others):
    return lax.optimization_barrier((value, *others))[0]


def stage_kernel(parts, rank, *refs):
    sources, outs, full_out, rank_here, sems = refs[:4], refs[-7:-3], *refs[-3:]
    copies = [pltpu.make_async_copy(rank, rank_here, sems.at[0])]
    for source, out in zip(sources, outs):
        if source.shape == out.shape:
            rows = source.shape[0] // parts
            pairs = [
                (source.at[pl.ds(n * rows, rows)], out.at[pl.ds(n * rows, rows)])
                for n in range(parts)
            ]
        else:
            width = out.shape[1]
            column = pl.multiple_of(lax.axis_index("tensor") * width, width)
            pairs = [(source.at[:, pl.ds(column, width)], out)]
        for pair in pairs:
            copies.append(pltpu.make_async_copy(*pair, sems.at[len(copies)]))
    for copy in copies:
        copy.start()
    copies.pop(0).wait()
    own_rank = jnp.where(lax.axis_index("tensor") == 0, rank_here[0], rank_here[1])
    full = (own_rank == outs[0].shape[0]).astype(jnp.float32)
    full_out[...] = jnp.full(full_out.shape, full)
    for copy in copies:
        copy.wait()


def stage(rank, right, cotangent, left, tokens, after):
    acts = pltpu.VMEM(tokens.shape, tokens.dtype)
    own = pltpu.VMEM((left.shape[0], tokens.shape[1]), left.dtype)
    parts = 8 if tokens.shape[0] % 128 == 0 else 1
    return pl.pallas_call(
        functools.partial(stage_kernel, parts),
        in_specs=[FAR] * 5 + [WHOLE] * len(after),
        out_specs=[WHOLE] * 5,
        out_shape=[own, acts, own, acts, pltpu.VMEM((8, 128), jnp.float32)],
        scratch_shapes=[
            pltpu.SMEM(rank.shape, rank.dtype),
            pltpu.SemaphoreType.DMA((3 + 2 * parts,)),
        ],
        compiler_params=PARAMS,
        cost_estimate=SMALL,
        name="stage",
    )(*map(far, (rank, right, cotangent, left, tokens)), *map(near, after))


def across(value, mask):
    pairs = [(i, i ^ mask) for i in range(2 * lax.axis_size("dp"))]
    return lax.ppermute(value, ("dp", "tensor"), pairs)


def own_is_full(full):
    return full[0:1, 0:1] > 0.5


def both_panels(own, piece):
    gap = jnp.zeros((PAD, piece.shape[1]), piece.dtype)
    return jnp.concatenate([own, gap, piece, gap], axis=0)


def project_kernel(flipped, low_column, chunk, given, *refs):
    own, piece, acts = refs[:3]
    others, out = refs[3 : 3 + given], refs[-1]
    slots, width = piece.shape
    core = lax.axis_index("dp") % 2
    start = (1 - core if flipped else core) * (own.shape[1] // 2) + low_column
    total = others[0][...] if others else None
    for low in range(0, width, chunk):
        column = pl.ds(pl.multiple_of(start + low, chunk), chunk)
        rows = both_panels(own[:, column], piece[:, low : low + chunk])
        part = lax.dot_general(
            rows, acts[:, column], (((1,), (1,)), ((), ())), preferred_element_type=jnp.float32
        )
        total = part if total is None else total + part
    if given < 3:
        out[...] = total
        return
    full_here = own_is_full(others[1][...])
    shorts = []
    for n, value in enumerate((others[2][...], total)):
        own_part, other_part = value[:slots], value[slots + PAD : 2 * slots + PAD]
        out[n * slots : (n + 1) * slots] = jnp.where(full_here, own_part, other_part)
        shorts.append(jnp.where(full_here, other_part[:1], own_part[:1]))
    row = lax.broadcasted_iota(jnp.int32, (PAD, out.shape[1]), 0)
    out[2 * slots :] = jnp.where(row == 0, shorts[0], jnp.where(row == 1, shorts[1], 0.0))


def project(own, piece, acts, flipped, others, held, low=0):
    slots, width = piece.shape
    tokens = acts.shape[0]
    rows = 2 * slots + (PAD if len(others) == 3 else 2 * PAD)
    return pl.pallas_call(
        functools.partial(project_kernel, flipped, low, min(width, 1024), len(others)),
        in_specs=[WHOLE] * (3 + len(others) + len(held)),
        out_specs=WHOLE,
        out_shape=pltpu.VMEM((rows, tokens), jnp.float32),
        compiler_params=PARAMS,
        cost_estimate=SMALL,
        name="project",
    )(*map(near, (own, piece, acts, *others, *held)))


def summed_rows(parts, got, n):
    slots = (parts.shape[0] - PAD) // 2
    full = slice(n * slots, (n + 1) * slots)
    short = slice(2 * slots + n, 2 * slots + n + 1)
    return parts[full] + got[full], parts[short] + got[short]


def gradient_kernel(scale, places, own, keep, parts, got, tokens, cotangent, *refs):
    out = refs[-1]
    rows, block = out.shape[1:]
    slots = (rows - PAD) // 2
    position = lax.axis_index("dp")
    core = (position + (0 if keep else 1)) % 2
    bit_3 = (position // 8 + (0 if own else 1)) % 2
    first = lax.broadcasted_iota(jnp.int32, (PAD, tokens.shape[0]), 0) == 0
    weights = []
    for n in range(2):
        full, short = summed_rows(parts, got, n)
        both = jnp.concatenate([full, jnp.where(first, short, 0.0)], axis=0)
        weights.append(both.astype(jnp.bfloat16))
    row = lax.broadcasted_iota(jnp.int32, (PAD, block), 0)
    for j, q in enumerate(places):
        start = ((bit_3 * len(places) + j) * 2 + core) * block
        columns = pl.ds(pl.multiple_of(start, block), block)
        left = jnp.dot(weights[0], tokens[:, columns], preferred_element_type=jnp.float32)
        right = jnp.dot(weights[1], cotangent[:, columns], preferred_element_type=jnp.float32)
        short = jnp.where(row == 1, right[slots : slots + 1], left[slots:])
        grad = jnp.concatenate([left[:slots], right[:slots], short], axis=0) * scale
        out[q] = grad.astype(out.dtype)


def gradient(parts, got, tokens, cotangent, scale, own, keep, after):
    places = (0, 2, 1, 3)
    shape = (len(places), parts.shape[0], tokens.shape[1] // lax.axis_size("dp"))
    return pl.pallas_call(
        functools.partial(gradient_kernel, scale, places, own, keep),
        in_specs=[WHOLE] * (4 + len(after)),
        out_specs=WHOLE,
        out_shape=pltpu.VMEM(shape, jnp.float32 if keep else jnp.bfloat16),
        compiler_params=PARAMS,
        cost_estimate=SMALL,
        name="gradient",
    )(*map(near, (parts, got, tokens, cotangent, *after)))


def spread_kernel(chunk, full, parts, got, own, mine, theirs, after, out, buffer, sems):
    slots, width = mine.shape
    full_here = own_is_full(full[...])
    back, short = summed_rows(parts, got, 0)
    first = lax.broadcasted_iota(jnp.int32, back.shape, 0) == 0
    short = jnp.where(first, short, 0.0)
    of_own = jnp.where(full_here, back, short)
    of_other = jnp.where(full_here, short, back)
    gap = jnp.zeros((PAD, back.shape[1]), jnp.float32)
    weights = jnp.concatenate([of_own, gap, of_other, gap], axis=0).T.astype(jnp.bfloat16)
    core = lax.axis_index("dp") % 2
    copies = []
    for side, piece in enumerate((mine, theirs)):
        for low in range(0, width, chunk):
            start = (core if side == 0 else 1 - core) * width + low
            column = pl.ds(pl.multiple_of(start, chunk), chunk)
            rows = both_panels(own[:, column], piece[:, low : low + chunk])
            held = buffer.at[:, side * width + low : side * width + low + chunk]
            held[...] = jnp.dot(weights, rows, preferred_element_type=jnp.float32).astype(out.dtype)
            copy = pltpu.make_async_copy(held, out.at[:, column], sems.at[len(copies)])
            copy.start()
            copies.append(copy)
    for copy in copies:
        copy.wait()


def spread(full, parts, got, own, mine, theirs, after):
    tokens = parts.shape[1]
    width = own.shape[1]
    chunk = min(width // 2, 1024)
    return pl.pallas_call(
        functools.partial(spread_kernel, chunk),
        in_specs=[WHOLE] * 7,
        out_specs=FAR,
        out_shape=jax.ShapeDtypeStruct((tokens, width), jnp.bfloat16),
        scratch_shapes=[
            pltpu.VMEM((tokens, width), jnp.bfloat16),
            pltpu.SemaphoreType.DMA((width // chunk,)),
        ],
        compiler_params=PARAMS,
        cost_estimate=LONG,
        name="spread",
    )(*map(near, (full, parts, got, own, mine, theirs, after)))


def settle_kernel(full, keep, *refs):
    gots, (near_out, far_out) = refs[:-2], refs[-2:]
    slots, block = near_out.shape[1:]
    full_here = own_is_full(full[...])
    first = lax.broadcasted_iota(jnp.int32, (slots, block), 0) == 0
    total = keep[...]
    for got in gots:
        total += got[...].astype(jnp.float32)
    for n in range(2):
        rows = total[n * slots : (n + 1) * slots]
        short = jnp.where(first, total[2 * slots + n : 2 * slots + n + 1], 0.0)
        near_out[n] = jnp.where(full_here, rows, short).astype(near_out.dtype)
        far_out[n] = jnp.where(full_here, short, rows).astype(far_out.dtype)


def settle(full, keep, gots, kind):
    rows, block = keep.shape
    shape = (2, (rows - PAD) // 2, block)
    return pl.pallas_call(
        settle_kernel,
        in_specs=[WHOLE] * (2 + len(gots)),
        out_specs=[WHOLE, WHOLE],
        out_shape=[pltpu.VMEM(shape, kind), pltpu.VMEM(shape, jnp.bfloat16)],
        compiler_params=PARAMS,
        cost_estimate=SMALL,
        name="settle",
    )(*map(near, (full, keep, *gots)))


def gather_kernel(*refs):
    total = refs[0][...].astype(jnp.float32)
    for value in refs[1:-1]:
        total += value[...].astype(jnp.float32)
    refs[-1][...] = total


def gather(*values):
    return pl.pallas_call(
        gather_kernel,
        in_specs=[WHOLE] * len(values),
        out_specs=WHOLE,
        out_shape=pltpu.VMEM(values[0].shape, jnp.float32),
        compiler_params=PARAMS,
        cost_estimate=SMALL,
        name="gather",
    )(*map(near, values))


def place_kernel(held, far, got, left_out, right_out):
    here = lax.axis_index("tensor") == 0
    for n, out in enumerate((left_out, right_out)):
        other = far[n] + got[n].astype(out.dtype)
        out[:, 0, 0, :] = jnp.where(here, held[n], other)
        out[:, 1, 0, :] = jnp.where(here, other, held[n])


def place(held, far, got):
    shape = jax.ShapeDtypeStruct((held.shape[1], 2, 1, held.shape[2]), jnp.float32)
    return pl.pallas_call(
        place_kernel,
        in_specs=[WHOLE] * 3,
        out_specs=[WHOLE, WHOLE],
        out_shape=[shape, shape],
        compiler_params=PARAMS,
        cost_estimate=SMALL,
        name="place",
    )(*map(near, (held, far, got)))


def pick_kernel(right, left, *refs):
    outs, sems = refs[:-1], refs[-1]
    part = right.shape[1] // 4
    core = lax.axis_index("dp") % 2
    low = 0
    copies = []
    for n, out in enumerate(outs):
        size = out.shape[1]
        source = left if n else right
        column = ((1 - lax.axis_index("tensor")) * 2 + (1 - core if n == 2 else core)) * part
        here = pl.ds(pl.multiple_of(column + low, 128), size)
        copies.append(pltpu.make_async_copy(source.at[:, here], out, sems.at[n]))
        low = low + size if n else 0
    for copy in copies:
        copy.start()
    for copy in copies:
        copy.wait()


def pick(right, left):
    slots, width = left.shape
    part = width // 4
    sizes = (part, part // 2, part // 2)
    return pl.pallas_call(
        pick_kernel,
        in_specs=[FAR] * 2,
        out_specs=[WHOLE] * 3,
        out_shape=[pltpu.VMEM((slots, size), left.dtype) for size in sizes],
        scratch_shapes=[pltpu.SemaphoreType.DMA((3,))],
        compiler_params=PARAMS,
        cost_estimate=SMALL,
        name="pick",
    )(far(right), far(left))


def quarter_kernel(keep, got, *outs):
    place = lax.axis_index("dp") // 2
    for n, out in enumerate(outs):
        block = (place + n % 2) % 2 * 2 + (place // 2 + n // 2) % 2
        out[...] = (keep[block] + got[block].astype(jnp.float32)).astype(out.dtype)


def quarter(keep, got):
    kinds = [jnp.float32] + [jnp.bfloat16] * 3
    return pl.pallas_call(
        quarter_kernel,
        in_specs=[WHOLE] * 2,
        out_specs=[WHOLE] * 4,
        out_shape=[pltpu.VMEM(keep.shape[1:], kind) for kind in kinds],
        compiler_params=PARAMS,
        cost_estimate=SMALL,
        name="quarter",
    )(near(keep), near(got))


def trade(sends):
    return [flip(sends[2], 1, 2), flip(sends[0], 1), flip(sends[1], 2)]


def two_panels(tokens, cotangent, left_factor, right_factor, panel_rank):
    scale = 1.0 / math.sqrt(tokens.shape[0] * lax.axis_size("dp"))

    wanted = pick(right_factor, left_factor)
    right_mine, left_first = (lax.ppermute(w, "tensor", SWAP) for w in wanted[:2])
    left_second = across(wanted[2], 3)
    right_own, cotangent, left_own, tokens, full = stage(
        panel_rank, right_factor, cotangent, left_factor, tokens, wanted
    )
    right_mine = after_all(right_mine, right_own)
    right_theirs = flip(right_mine, 0)
    back = project(right_own, right_mine, cotangent, False, (), ())
    left_first = after_all(left_first, back)
    hidden = project(left_own, left_first, tokens, False, (), (cotangent,))
    left_second = after_all(left_second, hidden)
    left_mine = jnp.concatenate([left_first, left_second], axis=1)
    left_theirs = flip(left_mine, 0)
    hidden = project(
        left_own, left_second, tokens, False, (hidden,), (cotangent,), left_first.shape[1]
    )
    back = project(right_own, right_theirs, cotangent, True, (back,), (hidden,))
    parts = project(left_own, left_theirs, tokens, True, (hidden, full, back), (cotangent,))
    parts_got = lax.ppermute(parts, "tensor", SWAP)

    operands = (parts, parts_got, tokens, cotangent, scale)
    other_send = gradient(*operands, False, False, ())
    other_keep = gradient(*operands, False, True, (other_send,))
    own_send = gradient(*operands, True, False, (other_keep,))
    other = quarter(other_keep, flip(other_send, 0))
    own_keep = gradient(*operands, True, True, (own_send, other[1]))
    own = quarter(own_keep, flip(own_send, 0))
    other_gots, own_gots = trade(other[1:]), trade(own[1:])
    near_send, far_send = settle(full, other[0], other_gots, jnp.bfloat16)
    far_got = across(far_send, 17)
    near_got = flip(near_send, 3)
    held, send = settle(full, own[0], own_gots, jnp.float32)
    got = lax.ppermute(send, "tensor", SWAP)
    token_grad = spread(full, parts, parts_got, left_own, left_mine, left_theirs, send)
    far = gather(far_got)
    far, near_got = lax.optimization_barrier((far, near_got))
    held = gather(held, near_got)
    return token_grad, *place(held, far, after_all(got, token_grad, held))


def solution(mesh):
    placed = (P("dp", "tensor"), P("dp", "tensor"), P("tensor", None), P("tensor", None), P())
    return jax.shard_map(
        two_panels if (mesh.shape["tensor"], mesh.shape["dp"]) == (2, 16) else any_panels,
        mesh=mesh,
        in_specs=placed,
        out_specs=(P("dp", "tensor"), P("tensor", None, "dp", None), P("tensor", None, "dp", None)),
        check_vma=False,
    )
```

```python
import functools
import math

import jax
import jax.numpy as jnp
from jax import lax
from jax.experimental import pallas as pl
from jax.experimental.pallas import tpu as pltpu
from jax.sharding import PartitionSpec as P


def block_view(home):
    groups = lax.axis_size("tensor")
    width = lax.axis_size("dp")
    block = home.shape[1] // (groups * width)
    return home.reshape(home.shape[0], groups, width, block)


def own_blocks(summed):
    return lax.dynamic_slice_in_dim(summed, lax.axis_index("dp"), 1, 2)


def settle_both(left_cols, right_cols):
    left_home, right_home = (
        lax.all_to_all(left_cols, "tensor", split_axis=0, concat_axis=1, tiled=True),
        lax.all_to_all(right_cols, "tensor", split_axis=0, concat_axis=1, tiled=True),
    )
    left_home = block_view(left_home)
    right_home = block_view(right_home)
    left_sum, right_sum = lax.psum((left_home, right_home), "dp")
    return (own_blocks(left_sum), own_blocks(right_sum))


def any_panels(tokens, cotangent, left_factor, right_factor, panel_rank):
    slot_count = left_factor.shape[0]
    groups = lax.axis_size("tensor")
    all_slots = slot_count * groups
    left_cols, right_cols = (
        lax.all_to_all(left_factor, "tensor", split_axis=1, concat_axis=0, tiled=True),
        lax.all_to_all(right_factor, "tensor", split_axis=1, concat_axis=0, tiled=True),
    )
    slots = jnp.arange(all_slots, dtype=jnp.int32)
    limits = jnp.repeat(panel_rank, slot_count, total_repeat_length=all_slots)
    live_rows = (slots % slot_count < limits).astype(jnp.bfloat16)[:, None]
    left_live = left_cols * live_rows
    right_live = right_cols * live_rows
    feature_dims = (((1,), (1,)), ((), ()))
    hidden_part = lax.dot_general(
        tokens, left_live, feature_dims, preferred_element_type=jnp.float32
    )
    back_part = lax.dot_general(
        cotangent, right_live, feature_dims, preferred_element_type=jnp.float32
    )
    hidden, back_hidden = lax.psum((hidden_part, back_part), "tensor")
    hidden = hidden.astype(jnp.bfloat16)
    back_hidden = back_hidden.astype(jnp.bfloat16)
    grad_scale = 1.0 / math.sqrt(tokens.shape[0] * lax.axis_size("dp"))
    token_dims = (((0,), (0,)), ((), ()))
    right_local = (
        lax.dot_general(hidden, cotangent, token_dims, preferred_element_type=jnp.float32)
        * grad_scale
    )
    left_local = (
        lax.dot_general(back_hidden, tokens, token_dims, preferred_element_type=jnp.float32)
        * grad_scale
    )
    token_grad = jnp.dot(back_hidden, left_live, preferred_element_type=jnp.float32).astype(
        jnp.bfloat16
    )
    left_grad, right_grad = settle_both(left_local, right_local)
    return (token_grad, left_grad, right_grad)


PAD = 8
SWAP = [(0, 1), (1, 0)]
WHOLE = pl.BlockSpec(memory_space=pltpu.VMEM)
FAR = pl.BlockSpec(memory_space=pltpu.HBM)
SMALL = pl.CostEstimate(flops=1, bytes_accessed=1, transcendentals=0)
LONG = pl.CostEstimate(flops=10**10, bytes_accessed=10**8, transcendentals=0)
PARAMS = pltpu.CompilerParams(vmem_limit_bytes=16 * 1024 * 1024)


def near(value):
    return pltpu.with_memory_space_constraint(value, pltpu.VMEM)


def far(value):
    return pltpu.with_memory_space_constraint(value, pltpu.HBM)


def flip(value, *bits):
    mask = sum(1 << bit for bit in bits)
    return lax.ppermute(value, "dp", [(i, i ^ mask) for i in range(lax.axis_size("dp"))])


def after_all(value, *others):
    return lax.optimization_barrier((value, *others))[0]


def stage_kernel(parts, rank, *refs):
    sources, outs, full_out, rank_here, sems = refs[:4], refs[-7:-3], *refs[-3:]
    copies = [pltpu.make_async_copy(rank, rank_here, sems.at[0])]
    for source, out in zip(sources, outs):
        if source.shape == out.shape:
            rows = source.shape[0] // parts
            pairs = [
                (source.at[pl.ds(n * rows, rows)], out.at[pl.ds(n * rows, rows)])
                for n in range(parts)
            ]
        else:
            width = out.shape[1]
            column = pl.multiple_of(lax.axis_index("tensor") * width, width)
            pairs = [(source.at[:, pl.ds(column, width)], out)]
        for pair in pairs:
            copies.append(pltpu.make_async_copy(*pair, sems.at[len(copies)]))
    for copy in copies:
        copy.start()
    copies.pop(0).wait()
    own_rank = jnp.where(lax.axis_index("tensor") == 0, rank_here[0], rank_here[1])
    full = (own_rank == outs[0].shape[0]).astype(jnp.float32)
    full_out[...] = jnp.full(full_out.shape, full)
    for copy in copies:
        copy.wait()


def stage(rank, right, cotangent, left, tokens, after):
    acts = pltpu.VMEM(tokens.shape, tokens.dtype)
    own = pltpu.VMEM((left.shape[0], tokens.shape[1]), left.dtype)
    parts = 8 if tokens.shape[0] % 128 == 0 else 1
    return pl.pallas_call(
        functools.partial(stage_kernel, parts),
        in_specs=[FAR] * 5 + [WHOLE] * len(after),
        out_specs=[WHOLE] * 5,
        out_shape=[own, acts, own, acts, pltpu.VMEM((8, 128), jnp.float32)],
        scratch_shapes=[
            pltpu.SMEM(rank.shape, rank.dtype),
            pltpu.SemaphoreType.DMA((3 + 2 * parts,)),
        ],
        compiler_params=PARAMS,
        cost_estimate=SMALL,
        name="stage",
    )(*map(far, (rank, right, cotangent, left, tokens)), *map(near, after))


def across(value, mask):
    pairs = [(i, i ^ mask) for i in range(2 * lax.axis_size("dp"))]
    return lax.ppermute(value, ("dp", "tensor"), pairs)


def own_is_full(full):
    return full[0:1, 0:1] > 0.5


def both_panels(own, piece):
    gap = jnp.zeros((PAD, piece.shape[1]), piece.dtype)
    return jnp.concatenate([own, gap, piece, gap], axis=0)


def project_kernel(flipped, low_column, chunk, given, *refs):
    own, piece, acts = refs[:3]
    others, out = refs[3 : 3 + given], refs[-1 if given < 3 else -2]
    slots, width = piece.shape
    core = lax.axis_index("dp") % 2
    start = (1 - core if flipped else core) * (own.shape[1] // 2) + low_column
    total = others[0][...] if others else None
    for low in range(0, width, chunk):
        column = pl.ds(pl.multiple_of(start + low, chunk), chunk)
        rows = both_panels(own[:, column], piece[:, low : low + chunk])
        part = lax.dot_general(
            rows, acts[:, column], (((1,), (1,)), ((), ())), preferred_element_type=jnp.float32
        )
        total = part if total is None else total + part
    if given < 3:
        out[...] = total
        return
    full_here = own_is_full(others[1][...])
    shorts = []
    for n, value in enumerate((others[2][...], total)):
        own_part, other_part = value[:slots], value[slots + PAD : 2 * slots + PAD]
        out[n * slots : (n + 1) * slots] = jnp.where(full_here, own_part, other_part)
        shorts.append(jnp.where(full_here, other_part[:1], own_part[:1]))
    row = lax.broadcasted_iota(jnp.int32, (PAD, out.shape[1]), 0)
    out[2 * slots :] = jnp.where(row == 0, shorts[0], jnp.where(row == 1, shorts[1], 0.0))
    refs[-1][...] = out[...].astype(refs[-1].dtype)


def project(own, piece, acts, flipped, others, held, low=0):
    slots, width = piece.shape
    tokens = acts.shape[0]
    last = len(others) == 3
    shape = (2 * slots + (PAD if last else 2 * PAD), tokens)
    kinds = (jnp.float32, jnp.bfloat16) if last else (jnp.float32,)
    return pl.pallas_call(
        functools.partial(project_kernel, flipped, low, min(width, 1024), len(others)),
        in_specs=[WHOLE] * (3 + len(others) + len(held)),
        out_specs=[WHOLE] * len(kinds),
        out_shape=[pltpu.VMEM(shape, kind) for kind in kinds],
        compiler_params=PARAMS,
        cost_estimate=SMALL,
        name="project",
    )(*map(near, (own, piece, acts, *others, *held)))


def summed_rows(parts, got, n):
    slots = (parts.shape[0] - PAD) // 2
    full = slice(n * slots, (n + 1) * slots)
    short = slice(2 * slots + n, 2 * slots + n + 1)
    total = parts[...] + got[...].astype(parts.dtype)
    return total[full], total[short]


def gradient_kernel(scale, places, own, keep, parts, got, tokens, cotangent, *refs):
    out = refs[-1]
    rows, block = out.shape[1:]
    slots = (rows - PAD) // 2
    position = lax.axis_index("dp")
    core = (position + (0 if keep else 1)) % 2
    bit_3 = (position // 8 + (0 if own else 1)) % 2
    first = lax.broadcasted_iota(jnp.int32, (PAD, tokens.shape[0]), 0) == 0
    weights = []
    for n in range(2):
        full, short = summed_rows(parts, got, n)
        both = jnp.concatenate([full, jnp.where(first, short, 0.0)], axis=0)
        weights.append(both.astype(jnp.bfloat16))
    row = lax.broadcasted_iota(jnp.int32, (PAD, block), 0)
    for j, q in enumerate(places):
        start = ((bit_3 * len(places) + j) * 2 + core) * block
        columns = pl.ds(pl.multiple_of(start, block), block)
        left = jnp.dot(weights[0], tokens[:, columns], preferred_element_type=jnp.float32)
        right = jnp.dot(weights[1], cotangent[:, columns], preferred_element_type=jnp.float32)
        short = jnp.where(row == 1, right[slots : slots + 1], left[slots:])
        grad = jnp.concatenate([left[:slots], right[:slots], short], axis=0) * scale
        out[q] = grad.astype(out.dtype)


def gradient(parts, got, tokens, cotangent, scale, own, keep, after):
    places = (0, 2, 1, 3)
    shape = (len(places), parts.shape[0], tokens.shape[1] // lax.axis_size("dp"))
    return pl.pallas_call(
        functools.partial(gradient_kernel, scale, places, own, keep),
        in_specs=[WHOLE] * (4 + len(after)),
        out_specs=WHOLE,
        out_shape=pltpu.VMEM(shape, jnp.float32 if keep else jnp.bfloat16),
        compiler_params=PARAMS,
        cost_estimate=SMALL,
        name="gradient",
    )(*map(near, (parts, got, tokens, cotangent, *after)))


def spread_kernel(chunk, full, parts, got, own, mine, theirs, after, out, buffer, sems):
    slots, width = mine.shape
    full_here = own_is_full(full[...])
    back, short = summed_rows(parts, got, 0)
    first = lax.broadcasted_iota(jnp.int32, back.shape, 0) == 0
    short = jnp.where(first, short, 0.0)
    of_own = jnp.where(full_here, back, short)
    of_other = jnp.where(full_here, short, back)
    gap = jnp.zeros((PAD, back.shape[1]), jnp.float32)
    weights = jnp.concatenate([of_own, gap, of_other, gap], axis=0).T.astype(jnp.bfloat16)
    core = lax.axis_index("dp") % 2
    copies = []
    for side, piece in enumerate((mine, theirs)):
        for low in range(0, width, chunk):
            start = (core if side == 0 else 1 - core) * width + low
            column = pl.ds(pl.multiple_of(start, chunk), chunk)
            rows = both_panels(own[:, column], piece[:, low : low + chunk])
            held = buffer.at[:, side * width + low : side * width + low + chunk]
            held[...] = jnp.dot(weights, rows, preferred_element_type=jnp.float32).astype(out.dtype)
            copy = pltpu.make_async_copy(held, out.at[:, column], sems.at[len(copies)])
            copy.start()
            copies.append(copy)
    for copy in copies:
        copy.wait()


def spread(full, parts, got, own, mine, theirs, after):
    tokens = parts.shape[1]
    width = own.shape[1]
    chunk = min(width // 2, 1024)
    return pl.pallas_call(
        functools.partial(spread_kernel, chunk),
        in_specs=[WHOLE] * 7,
        out_specs=FAR,
        out_shape=jax.ShapeDtypeStruct((tokens, width), jnp.bfloat16),
        scratch_shapes=[
            pltpu.VMEM((tokens, width), jnp.bfloat16),
            pltpu.SemaphoreType.DMA((width // chunk,)),
        ],
        compiler_params=PARAMS,
        cost_estimate=LONG,
        name="spread",
    )(*map(near, (full, parts, got, own, mine, theirs, after)))


def settle_kernel(full, keep, *refs):
    gots, (near_out, far_out) = refs[:-2], refs[-2:]
    slots, block = near_out.shape[1:]
    full_here = own_is_full(full[...])
    first = lax.broadcasted_iota(jnp.int32, (slots, block), 0) == 0
    total = keep[...]
    for got in gots:
        total += got[...].astype(jnp.float32)
    for n in range(2):
        rows = total[n * slots : (n + 1) * slots]
        short = jnp.where(first, total[2 * slots + n : 2 * slots + n + 1], 0.0)
        near_out[n] = jnp.where(full_here, rows, short).astype(near_out.dtype)
        far_out[n] = jnp.where(full_here, short, rows).astype(far_out.dtype)


def settle(full, keep, gots, kind):
    rows, block = keep.shape
    shape = (2, (rows - PAD) // 2, block)
    return pl.pallas_call(
        settle_kernel,
        in_specs=[WHOLE] * (2 + len(gots)),
        out_specs=[WHOLE, WHOLE],
        out_shape=[pltpu.VMEM(shape, kind), pltpu.VMEM(shape, jnp.bfloat16)],
        compiler_params=PARAMS,
        cost_estimate=SMALL,
        name="settle",
    )(*map(near, (full, keep, *gots)))


def gather_kernel(*refs):
    total = refs[0][...].astype(jnp.float32)
    for value in refs[1:-1]:
        total += value[...].astype(jnp.float32)
    refs[-1][...] = total


def gather(*values):
    return pl.pallas_call(
        gather_kernel,
        in_specs=[WHOLE] * len(values),
        out_specs=WHOLE,
        out_shape=pltpu.VMEM(values[0].shape, jnp.float32),
        compiler_params=PARAMS,
        cost_estimate=SMALL,
        name="gather",
    )(*map(near, values))


def place_kernel(held, far, got, left_out, right_out):
    here = lax.axis_index("tensor") == 0
    for n, out in enumerate((left_out, right_out)):
        other = far[n] + got[n].astype(out.dtype)
        out[:, 0, 0, :] = jnp.where(here, held[n], other)
        out[:, 1, 0, :] = jnp.where(here, other, held[n])


def place(held, far, got):
    shape = jax.ShapeDtypeStruct((held.shape[1], 2, 1, held.shape[2]), jnp.float32)
    return pl.pallas_call(
        place_kernel,
        in_specs=[WHOLE] * 3,
        out_specs=[WHOLE, WHOLE],
        out_shape=[shape, shape],
        compiler_params=PARAMS,
        cost_estimate=SMALL,
        name="place",
    )(*map(near, (held, far, got)))


def pick_kernel(right, left, *refs):
    outs, sems = refs[:-1], refs[-1]
    part = right.shape[1] // 4
    core = lax.axis_index("dp") % 2
    low = 0
    copies = []
    for n, out in enumerate(outs):
        size = out.shape[1]
        source = left if n else right
        column = ((1 - lax.axis_index("tensor")) * 2 + (1 - core if n == 2 else core)) * part
        here = pl.ds(pl.multiple_of(column + low, 128), size)
        copies.append(pltpu.make_async_copy(source.at[:, here], out, sems.at[n]))
        low = low + size if n else 0
    for copy in copies:
        copy.start()
    for copy in copies:
        copy.wait()


def pick(right, left):
    slots, width = left.shape
    part = width // 4
    sizes = (part, part // 2, part // 2)
    return pl.pallas_call(
        pick_kernel,
        in_specs=[FAR] * 2,
        out_specs=[WHOLE] * 3,
        out_shape=[pltpu.VMEM((slots, size), left.dtype) for size in sizes],
        scratch_shapes=[pltpu.SemaphoreType.DMA((3,))],
        compiler_params=PARAMS,
        cost_estimate=SMALL,
        name="pick",
    )(far(right), far(left))


def quarter_kernel(keep, got, *outs):
    place = lax.axis_index("dp") // 2
    for n, out in enumerate(outs):
        block = (place + n % 2) % 2 * 2 + (place // 2 + n // 2) % 2
        out[...] = (keep[block] + got[block].astype(jnp.float32)).astype(out.dtype)


def quarter(keep, got):
    kinds = [jnp.float32] + [jnp.bfloat16] * 3
    return pl.pallas_call(
        quarter_kernel,
        in_specs=[WHOLE] * 2,
        out_specs=[WHOLE] * 4,
        out_shape=[pltpu.VMEM(keep.shape[1:], kind) for kind in kinds],
        compiler_params=PARAMS,
        cost_estimate=SMALL,
        name="quarter",
    )(near(keep), near(got))


def trade(sends):
    return [flip(sends[2], 1, 2), flip(sends[0], 1), flip(sends[1], 2)]


def two_panels(tokens, cotangent, left_factor, right_factor, panel_rank):
    scale = 1.0 / math.sqrt(tokens.shape[0] * lax.axis_size("dp"))

    wanted = pick(right_factor, left_factor)
    right_mine, left_first = (lax.ppermute(w, "tensor", SWAP) for w in wanted[:2])
    left_second = across(wanted[2], 3)
    right_own, cotangent, left_own, tokens, full = stage(
        panel_rank, right_factor, cotangent, left_factor, tokens, wanted
    )
    right_mine = after_all(right_mine, right_own)
    right_theirs = flip(right_mine, 0)
    (back,) = project(right_own, right_mine, cotangent, False, (), ())
    left_first = after_all(left_first, back)
    (hidden,) = project(left_own, left_first, tokens, False, (), (cotangent,))
    left_second = after_all(left_second, hidden)
    left_mine = jnp.concatenate([left_first, left_second], axis=1)
    left_theirs = flip(left_mine, 0)
    (hidden,) = project(
        left_own, left_second, tokens, False, (hidden,), (cotangent,), left_first.shape[1]
    )
    (back,) = project(right_own, right_theirs, cotangent, True, (back,), (hidden,))
    parts, parts_send = project(
        left_own, left_theirs, tokens, True, (hidden, full, back), (cotangent,)
    )
    parts_got = lax.ppermute(parts_send, "tensor", SWAP)

    operands = (parts, parts_got, tokens, cotangent, scale)
    other_send = gradient(*operands, False, False, ())
    other_keep = gradient(*operands, False, True, (other_send,))
    own_send = gradient(*operands, True, False, (other_keep,))
    other = quarter(other_keep, flip(other_send, 0))
    own_keep = gradient(*operands, True, True, (own_send, other[1]))
    own = quarter(own_keep, flip(own_send, 0))
    other_gots, own_gots = trade(other[1:]), trade(own[1:])
    near_send, far_send = settle(full, other[0], other_gots, jnp.bfloat16)
    far_got = across(far_send, 17)
    near_got = flip(near_send, 3)
    held, send = settle(full, own[0], own_gots, jnp.float32)
    got = lax.ppermute(send, "tensor", SWAP)
    token_grad = spread(full, parts, parts_got, left_own, left_mine, left_theirs, send)
    far = gather(far_got)
    far, near_got = lax.optimization_barrier((far, near_got))
    held = gather(held, near_got)
    return token_grad, *place(held, far, after_all(got, token_grad, held))


def solution(mesh):
    placed = (P("dp", "tensor"), P("dp", "tensor"), P("tensor", None), P("tensor", None), P())
    return jax.shard_map(
        two_panels if (mesh.shape["tensor"], mesh.shape["dp"]) == (2, 16) else any_panels,
        mesh=mesh,
        in_specs=placed,
        out_specs=(P("dp", "tensor"), P("tensor", None, "dp", None), P("tensor", None, "dp", None)),
        check_vma=False,
    )
```

```python
import functools
import math

import jax
import jax.numpy as jnp
from jax import lax
from jax.experimental import pallas as pl
from jax.experimental.pallas import tpu as pltpu
from jax.sharding import PartitionSpec as P


def block_view(home):
    groups = lax.axis_size("tensor")
    width = lax.axis_size("dp")
    block = home.shape[1] // (groups * width)
    return home.reshape(home.shape[0], groups, width, block)


def own_blocks(summed):
    return lax.dynamic_slice_in_dim(summed, lax.axis_index("dp"), 1, 2)


def settle_both(left_cols, right_cols):
    left_home, right_home = (
        lax.all_to_all(left_cols, "tensor", split_axis=0, concat_axis=1, tiled=True),
        lax.all_to_all(right_cols, "tensor", split_axis=0, concat_axis=1, tiled=True),
    )
    left_home = block_view(left_home)
    right_home = block_view(right_home)
    left_sum, right_sum = lax.psum((left_home, right_home), "dp")
    return (own_blocks(left_sum), own_blocks(right_sum))


def any_panels(tokens, cotangent, left_factor, right_factor, panel_rank):
    slot_count = left_factor.shape[0]
    groups = lax.axis_size("tensor")
    all_slots = slot_count * groups
    left_cols, right_cols = (
        lax.all_to_all(left_factor, "tensor", split_axis=1, concat_axis=0, tiled=True),
        lax.all_to_all(right_factor, "tensor", split_axis=1, concat_axis=0, tiled=True),
    )
    slots = jnp.arange(all_slots, dtype=jnp.int32)
    limits = jnp.repeat(panel_rank, slot_count, total_repeat_length=all_slots)
    live_rows = (slots % slot_count < limits).astype(jnp.bfloat16)[:, None]
    left_live = left_cols * live_rows
    right_live = right_cols * live_rows
    feature_dims = (((1,), (1,)), ((), ()))
    hidden_part = lax.dot_general(
        tokens, left_live, feature_dims, preferred_element_type=jnp.float32
    )
    back_part = lax.dot_general(
        cotangent, right_live, feature_dims, preferred_element_type=jnp.float32
    )
    hidden, back_hidden = lax.psum((hidden_part, back_part), "tensor")
    hidden = hidden.astype(jnp.bfloat16)
    back_hidden = back_hidden.astype(jnp.bfloat16)
    grad_scale = 1.0 / math.sqrt(tokens.shape[0] * lax.axis_size("dp"))
    token_dims = (((0,), (0,)), ((), ()))
    right_local = (
        lax.dot_general(hidden, cotangent, token_dims, preferred_element_type=jnp.float32)
        * grad_scale
    )
    left_local = (
        lax.dot_general(back_hidden, tokens, token_dims, preferred_element_type=jnp.float32)
        * grad_scale
    )
    token_grad = jnp.dot(back_hidden, left_live, preferred_element_type=jnp.float32).astype(
        jnp.bfloat16
    )
    left_grad, right_grad = settle_both(left_local, right_local)
    return (token_grad, left_grad, right_grad)


PAD = 8
SWAP = [(0, 1), (1, 0)]
WHOLE = pl.BlockSpec(memory_space=pltpu.VMEM)
FAR = pl.BlockSpec(memory_space=pltpu.HBM)
SMALL = pl.CostEstimate(flops=1, bytes_accessed=1, transcendentals=0)
LONG = pl.CostEstimate(flops=10**10, bytes_accessed=10**8, transcendentals=0)
PARAMS = pltpu.CompilerParams(vmem_limit_bytes=16 * 1024 * 1024)


def near(value):
    return pltpu.with_memory_space_constraint(value, pltpu.VMEM)


def far(value):
    return pltpu.with_memory_space_constraint(value, pltpu.HBM)


def flip(value, *bits):
    mask = sum(1 << bit for bit in bits)
    return lax.ppermute(value, "dp", [(i, i ^ mask) for i in range(lax.axis_size("dp"))])


def after_all(value, *others):
    return lax.optimization_barrier((value, *others))[0]


def stage_kernel(parts, rank, *refs):
    sources, outs, full_out, rank_here, sems = refs[:4], refs[-7:-3], *refs[-3:]
    copies = [pltpu.make_async_copy(rank, rank_here, sems.at[0])]
    for source, out in zip(sources, outs):
        if source.shape == out.shape:
            rows = source.shape[0] // parts
            pairs = [
                (source.at[pl.ds(n * rows, rows)], out.at[pl.ds(n * rows, rows)])
                for n in range(parts)
            ]
        else:
            width = out.shape[1]
            column = pl.multiple_of(lax.axis_index("tensor") * width, width)
            pairs = [(source.at[:, pl.ds(column, width)], out)]
        for pair in pairs:
            copies.append(pltpu.make_async_copy(*pair, sems.at[len(copies)]))
    for copy in copies:
        copy.start()
    copies.pop(0).wait()
    own_rank = jnp.where(lax.axis_index("tensor") == 0, rank_here[0], rank_here[1])
    full = (own_rank == outs[0].shape[0]).astype(jnp.float32)
    full_out[...] = jnp.full(full_out.shape, full)
    for copy in copies:
        copy.wait()


def stage(rank, right, cotangent, left, tokens, after):
    acts = pltpu.VMEM(tokens.shape, tokens.dtype)
    own = pltpu.VMEM((left.shape[0], tokens.shape[1]), left.dtype)
    parts = 8 if tokens.shape[0] % 128 == 0 else 1
    return pl.pallas_call(
        functools.partial(stage_kernel, parts),
        in_specs=[FAR] * 5 + [WHOLE] * len(after),
        out_specs=[WHOLE] * 5,
        out_shape=[own, acts, own, acts, pltpu.VMEM((8, 128), jnp.float32)],
        scratch_shapes=[
            pltpu.SMEM(rank.shape, rank.dtype),
            pltpu.SemaphoreType.DMA((3 + 2 * parts,)),
        ],
        compiler_params=PARAMS,
        cost_estimate=SMALL,
        name="stage",
    )(*map(far, (rank, right, cotangent, left, tokens)), *map(near, after))


def across(value, mask):
    pairs = [(i, i ^ mask) for i in range(2 * lax.axis_size("dp"))]
    return lax.ppermute(value, ("dp", "tensor"), pairs)


def own_is_full(full):
    return full[0:1, 0:1] > 0.5


def both_panels(own, piece):
    gap = jnp.zeros((PAD, piece.shape[1]), piece.dtype)
    return jnp.concatenate([own, gap, piece, gap], axis=0)


def project_kernel(flipped, low_column, chunk, given, *refs):
    own, piece, acts = refs[:3]
    others, out = refs[3 : 3 + given], refs[-1 if given < 3 else -2]
    slots, width = piece.shape
    core = lax.axis_index("dp") % 2
    start = (1 - core if flipped else core) * (own.shape[1] // 2) + low_column
    total = others[0][...] if others else None
    turned = None
    for n, low in enumerate(range(0, width, chunk)):
        column = pl.ds(pl.multiple_of(start + low, chunk), chunk)
        rows = both_panels(own[:, column], piece[:, low : low + chunk])
        if n % 2:
            part = lax.dot_general(
                acts[:, column], rows, (((1,), (1,)), ((), ())), preferred_element_type=jnp.float32
            )
            turned = part if turned is None else turned + part
        else:
            part = lax.dot_general(
                rows, acts[:, column], (((1,), (1,)), ((), ())), preferred_element_type=jnp.float32
            )
            total = part if total is None else total + part
    total += turned.T
    if given < 3:
        out[...] = total
        return
    full_here = own_is_full(others[1][...])
    shorts = []
    for n, value in enumerate((others[2][...], total)):
        own_part, other_part = value[:slots], value[slots + PAD : 2 * slots + PAD]
        out[n * slots : (n + 1) * slots] = jnp.where(full_here, own_part, other_part)
        shorts.append(jnp.where(full_here, other_part[:1], own_part[:1]))
    row = lax.broadcasted_iota(jnp.int32, (PAD, out.shape[1]), 0)
    out[2 * slots :] = jnp.where(row == 0, shorts[0], jnp.where(row == 1, shorts[1], 0.0))
    refs[-1][...] = out[...].astype(refs[-1].dtype)


def project(own, piece, acts, flipped, others, held, low=0):
    slots, width = piece.shape
    tokens = acts.shape[0]
    last = len(others) == 3
    shape = (2 * slots + (PAD if last else 2 * PAD), tokens)
    kinds = (jnp.float32, jnp.bfloat16) if last else (jnp.float32,)
    return pl.pallas_call(
        functools.partial(project_kernel, flipped, low, min(width // 2, 512), len(others)),
        in_specs=[WHOLE] * (3 + len(others) + len(held)),
        out_specs=[WHOLE] * len(kinds),
        out_shape=[pltpu.VMEM(shape, kind) for kind in kinds],
        compiler_params=PARAMS,
        cost_estimate=SMALL,
        name="project",
    )(*map(near, (own, piece, acts, *others, *held)))


def summed_rows(parts, got, n):
    slots = (parts.shape[0] - PAD) // 2
    full = slice(n * slots, (n + 1) * slots)
    short = slice(2 * slots + n, 2 * slots + n + 1)
    total = parts[...] + got[...].astype(parts.dtype)
    return total[full], total[short]


def gradient_kernel(scale, places, jobs, parts, got, tokens, cotangent, *refs):
    outs = refs[-len(jobs) :]
    rows, block = outs[0].shape[1:]
    slots = (rows - PAD) // 2
    live = slots + PAD
    position = lax.axis_index("dp")
    first = lax.broadcasted_iota(jnp.int32, (PAD, tokens.shape[0]), 0) == 0
    weights = []
    for n in range(2):
        full, short = summed_rows(parts, got, n)
        both = jnp.concatenate([full, jnp.where(first, short, 0.0)], axis=0)
        weights.append(both.astype(jnp.bfloat16))
    main = tokens.shape[0] // 256 * 256
    gap = jnp.zeros((live, tokens.shape[0] - main), jnp.bfloat16)
    rest = jnp.concatenate(
        [
            jnp.concatenate([weights[0][:, main:], gap], axis=1),
            jnp.concatenate([gap, weights[1][:, main:]], axis=1),
        ],
        axis=0,
    )
    row = lax.broadcasted_iota(jnp.int32, (PAD, block), 0)
    for (own, keep), out in zip(jobs, outs):
        core = (position + (0 if keep else 1)) % 2
        bit_3 = (position // 8 + (0 if own else 1)) % 2
        for j, q in enumerate(places):
            start = ((bit_3 * len(places) + j) * 2 + core) * block
            columns = pl.ds(pl.multiple_of(start, block), block)
            last = jnp.concatenate([tokens[main:, columns], cotangent[main:, columns]], axis=0)
            last = jnp.dot(rest, last, preferred_element_type=jnp.float32)
            left, right = (
                jnp.dot(w[:, :main], acts[:main, columns], preferred_element_type=jnp.float32)
                for w, acts in zip(weights, (tokens, cotangent))
            )
            left += last[:live]
            right += last[live:]
            short = jnp.where(row == 1, right[slots : slots + 1], left[slots:])
            grad = jnp.concatenate([left[:slots], right[:slots], short], axis=0) * scale
            out[q] = grad.astype(out.dtype)


def gradient(parts, got, tokens, cotangent, scale, jobs, after):
    places = (0, 2, 1, 3)
    shape = (len(places), parts.shape[0], tokens.shape[1] // lax.axis_size("dp"))
    return pl.pallas_call(
        functools.partial(gradient_kernel, scale, places, jobs),
        in_specs=[WHOLE] * (4 + len(after)),
        out_specs=[WHOLE] * len(jobs),
        out_shape=[pltpu.VMEM(shape, jnp.float32 if job[1] else jnp.bfloat16) for job in jobs],
        compiler_params=PARAMS,
        cost_estimate=SMALL,
        name="gradient",
    )(*map(near, (parts, got, tokens, cotangent, *after)))


def spread_kernel(chunk, full, parts, got, own, mine, theirs, after, out, buffer, sems):
    slots, width = mine.shape
    full_here = own_is_full(full[...])
    back, short = summed_rows(parts, got, 0)
    first = lax.broadcasted_iota(jnp.int32, back.shape, 0) == 0
    short = jnp.where(first, short, 0.0)
    of_own = jnp.where(full_here, back, short)
    of_other = jnp.where(full_here, short, back)
    gap = jnp.zeros((PAD, back.shape[1]), jnp.float32)
    weights = jnp.concatenate([of_own, gap, of_other, gap], axis=0).T.astype(jnp.bfloat16)
    core = lax.axis_index("dp") % 2
    copies = []
    for side, piece in enumerate((mine, theirs)):
        for low in range(0, width, chunk):
            start = (core if side == 0 else 1 - core) * width + low
            column = pl.ds(pl.multiple_of(start, chunk), chunk)
            rows = both_panels(own[:, column], piece[:, low : low + chunk])
            held = buffer.at[:, side * width + low : side * width + low + chunk]
            held[...] = jnp.dot(weights, rows, preferred_element_type=jnp.float32).astype(out.dtype)
            copy = pltpu.make_async_copy(held, out.at[:, column], sems.at[len(copies)])
            copy.start()
            copies.append(copy)
    for copy in copies:
        copy.wait()


def spread(full, parts, got, own, mine, theirs, after):
    tokens = parts.shape[1]
    width = own.shape[1]
    chunk = min(width // 2, 1024)
    return pl.pallas_call(
        functools.partial(spread_kernel, chunk),
        in_specs=[WHOLE] * 7,
        out_specs=FAR,
        out_shape=jax.ShapeDtypeStruct((tokens, width), jnp.bfloat16),
        scratch_shapes=[
            pltpu.VMEM((tokens, width), jnp.bfloat16),
            pltpu.SemaphoreType.DMA((width // chunk,)),
        ],
        compiler_params=PARAMS,
        cost_estimate=LONG,
        name="spread",
    )(*map(near, (full, parts, got, own, mine, theirs, after)))


def settle_kernel(full, keep, *refs):
    gots, (near_out, far_out) = refs[:-2], refs[-2:]
    slots, block = near_out.shape[1:]
    full_here = own_is_full(full[...])
    first = lax.broadcasted_iota(jnp.int32, (slots, block), 0) == 0
    total = keep[...]
    for got in gots:
        total += got[...].astype(jnp.float32)
    for n in range(2):
        rows = total[n * slots : (n + 1) * slots]
        short = jnp.where(first, total[2 * slots + n : 2 * slots + n + 1], 0.0)
        near_out[n] = jnp.where(full_here, rows, short).astype(near_out.dtype)
        far_out[n] = jnp.where(full_here, short, rows).astype(far_out.dtype)


def settle(full, keep, gots, kind):
    rows, block = keep.shape
    shape = (2, (rows - PAD) // 2, block)
    return pl.pallas_call(
        settle_kernel,
        in_specs=[WHOLE] * (2 + len(gots)),
        out_specs=[WHOLE, WHOLE],
        out_shape=[pltpu.VMEM(shape, kind), pltpu.VMEM(shape, jnp.bfloat16)],
        compiler_params=PARAMS,
        cost_estimate=SMALL,
        name="settle",
    )(*map(near, (full, keep, *gots)))


def gather_kernel(*refs):
    total = refs[0][...].astype(jnp.float32)
    for value in refs[1:-1]:
        total += value[...].astype(jnp.float32)
    refs[-1][...] = total


def gather(*values):
    return pl.pallas_call(
        gather_kernel,
        in_specs=[WHOLE] * len(values),
        out_specs=WHOLE,
        out_shape=pltpu.VMEM(values[0].shape, jnp.float32),
        compiler_params=PARAMS,
        cost_estimate=SMALL,
        name="gather",
    )(*map(near, values))


def place_kernel(held, far, got, left_out, right_out):
    here = lax.axis_index("tensor") == 0
    for n, out in enumerate((left_out, right_out)):
        other = far[n] + got[n].astype(out.dtype)
        out[:, 0, 0, :] = jnp.where(here, held[n], other)
        out[:, 1, 0, :] = jnp.where(here, other, held[n])


def place(held, far, got):
    shape = jax.ShapeDtypeStruct((held.shape[1], 2, 1, held.shape[2]), jnp.float32)
    return pl.pallas_call(
        place_kernel,
        in_specs=[WHOLE] * 3,
        out_specs=[WHOLE, WHOLE],
        out_shape=[shape, shape],
        compiler_params=PARAMS,
        cost_estimate=SMALL,
        name="place",
    )(*map(near, (held, far, got)))


def pick_kernel(right, left, *refs):
    outs, sems = refs[:-1], refs[-1]
    part = right.shape[1] // 4
    core = lax.axis_index("dp") % 2
    low = 0
    copies = []
    for n, out in enumerate(outs):
        size = out.shape[1]
        source = left if n else right
        column = ((1 - lax.axis_index("tensor")) * 2 + (1 - core if n == 2 else core)) * part
        here = pl.ds(pl.multiple_of(column + low, 128), size)
        copies.append(pltpu.make_async_copy(source.at[:, here], out, sems.at[n]))
        low = low + size if n else 0
    for copy in copies:
        copy.start()
    for copy in copies:
        copy.wait()


def pick(right, left):
    slots, width = left.shape
    part = width // 4
    sizes = (part, part // 2, part // 2)
    return pl.pallas_call(
        pick_kernel,
        in_specs=[FAR] * 2,
        out_specs=[WHOLE] * 3,
        out_shape=[pltpu.VMEM((slots, size), left.dtype) for size in sizes],
        scratch_shapes=[pltpu.SemaphoreType.DMA((3,))],
        compiler_params=PARAMS,
        cost_estimate=SMALL,
        name="pick",
    )(far(right), far(left))


def quarter_kernel(keep, got, *outs):
    place = lax.axis_index("dp") // 2
    for n, out in enumerate(outs):
        block = (place + n % 2) % 2 * 2 + (place // 2 + n // 2) % 2
        out[...] = (keep[block] + got[block].astype(jnp.float32)).astype(out.dtype)


def quarter(keep, got):
    kinds = [jnp.float32] + [jnp.bfloat16] * 3
    return pl.pallas_call(
        quarter_kernel,
        in_specs=[WHOLE] * 2,
        out_specs=[WHOLE] * 4,
        out_shape=[pltpu.VMEM(keep.shape[1:], kind) for kind in kinds],
        compiler_params=PARAMS,
        cost_estimate=SMALL,
        name="quarter",
    )(near(keep), near(got))


def trade(sends):
    return [flip(sends[2], 1, 2), flip(sends[0], 1), flip(sends[1], 2)]


def two_panels(tokens, cotangent, left_factor, right_factor, panel_rank):
    scale = 1.0 / math.sqrt(tokens.shape[0] * lax.axis_size("dp"))

    wanted = pick(right_factor, left_factor)
    right_mine, left_first = (lax.ppermute(w, "tensor", SWAP) for w in wanted[:2])
    left_second = across(wanted[2], 3)
    right_own, cotangent, left_own, tokens, full = stage(
        panel_rank, right_factor, cotangent, left_factor, tokens, wanted
    )
    right_mine = after_all(right_mine, right_own)
    right_theirs = flip(right_mine, 0)
    (back,) = project(right_own, right_mine, cotangent, False, (), ())
    left_first = after_all(left_first, back)
    (hidden,) = project(left_own, left_first, tokens, False, (), (cotangent,))
    left_second = after_all(left_second, hidden)
    left_mine = jnp.concatenate([left_first, left_second], axis=1)
    left_theirs = flip(left_mine, 0)
    (hidden,) = project(
        left_own, left_second, tokens, False, (hidden,), (cotangent,), left_first.shape[1]
    )
    (back,) = project(right_own, right_theirs, cotangent, True, (back,), (hidden,))
    parts, parts_send = project(
        left_own, left_theirs, tokens, True, (hidden, full, back), (cotangent,)
    )
    parts_got = lax.ppermute(parts_send, "tensor", SWAP)

    operands = (parts, parts_got, tokens, cotangent, scale)
    (other_send,) = gradient(*operands, [(False, False)], ())
    other_keep, own_send = gradient(
        *operands, [(False, True), (True, False)], (other_send,)
    )
    other = quarter(other_keep, flip(other_send, 0))
    (own_keep,) = gradient(*operands, [(True, True)], (own_send, other[1]))
    own = quarter(own_keep, flip(own_send, 0))
    other_gots, own_gots = trade(other[1:]), trade(own[1:])
    near_send, far_send = settle(full, other[0], other_gots, jnp.bfloat16)
    far_got = across(far_send, 17)
    near_got = flip(near_send, 3)
    held, send = settle(full, own[0], own_gots, jnp.float32)
    got = lax.ppermute(send, "tensor", SWAP)
    token_grad = spread(full, parts, parts_got, left_own, left_mine, left_theirs, send)
    far = gather(far_got)
    far, near_got = lax.optimization_barrier((far, near_got))
    held = gather(held, near_got)
    return token_grad, *place(held, far, after_all(got, token_grad, held))


def solution(mesh):
    placed = (P("dp", "tensor"), P("dp", "tensor"), P("tensor", None), P("tensor", None), P())
    return jax.shard_map(
        two_panels if (mesh.shape["tensor"], mesh.shape["dp"]) == (2, 16) else any_panels,
        mesh=mesh,
        in_specs=placed,
        out_specs=(P("dp", "tensor"), P("tensor", None, "dp", None), P("tensor", None, "dp", None)),
        check_vma=False,
    )
```

```python
import functools
import math

import jax
import jax.numpy as jnp
from jax import lax
from jax.experimental import pallas as pl
from jax.experimental.pallas import tpu as pltpu
from jax.sharding import PartitionSpec as P


def block_view(home):
    groups = lax.axis_size("tensor")
    width = lax.axis_size("dp")
    block = home.shape[1] // (groups * width)
    return home.reshape(home.shape[0], groups, width, block)


def own_blocks(summed):
    return lax.dynamic_slice_in_dim(summed, lax.axis_index("dp"), 1, 2)


def settle_both(left_cols, right_cols):
    left_home, right_home = (
        lax.all_to_all(left_cols, "tensor", split_axis=0, concat_axis=1, tiled=True),
        lax.all_to_all(right_cols, "tensor", split_axis=0, concat_axis=1, tiled=True),
    )
    left_home = block_view(left_home)
    right_home = block_view(right_home)
    left_sum, right_sum = lax.psum((left_home, right_home), "dp")
    return (own_blocks(left_sum), own_blocks(right_sum))


def any_panels(tokens, cotangent, left_factor, right_factor, panel_rank):
    slot_count = left_factor.shape[0]
    groups = lax.axis_size("tensor")
    all_slots = slot_count * groups
    left_cols, right_cols = (
        lax.all_to_all(left_factor, "tensor", split_axis=1, concat_axis=0, tiled=True),
        lax.all_to_all(right_factor, "tensor", split_axis=1, concat_axis=0, tiled=True),
    )
    slots = jnp.arange(all_slots, dtype=jnp.int32)
    limits = jnp.repeat(panel_rank, slot_count, total_repeat_length=all_slots)
    live_rows = (slots % slot_count < limits).astype(jnp.bfloat16)[:, None]
    left_live = left_cols * live_rows
    right_live = right_cols * live_rows
    feature_dims = (((1,), (1,)), ((), ()))
    hidden_part = lax.dot_general(
        tokens, left_live, feature_dims, preferred_element_type=jnp.float32
    )
    back_part = lax.dot_general(
        cotangent, right_live, feature_dims, preferred_element_type=jnp.float32
    )
    hidden, back_hidden = lax.psum((hidden_part, back_part), "tensor")
    hidden = hidden.astype(jnp.bfloat16)
    back_hidden = back_hidden.astype(jnp.bfloat16)
    grad_scale = 1.0 / math.sqrt(tokens.shape[0] * lax.axis_size("dp"))
    token_dims = (((0,), (0,)), ((), ()))
    right_local = (
        lax.dot_general(hidden, cotangent, token_dims, preferred_element_type=jnp.float32)
        * grad_scale
    )
    left_local = (
        lax.dot_general(back_hidden, tokens, token_dims, preferred_element_type=jnp.float32)
        * grad_scale
    )
    token_grad = jnp.dot(back_hidden, left_live, preferred_element_type=jnp.float32).astype(
        jnp.bfloat16
    )
    left_grad, right_grad = settle_both(left_local, right_local)
    return (token_grad, left_grad, right_grad)


PAD = 8
SWAP = [(0, 1), (1, 0)]
WHOLE = pl.BlockSpec(memory_space=pltpu.VMEM)
FAR = pl.BlockSpec(memory_space=pltpu.HBM)
SMALL = pl.CostEstimate(flops=1, bytes_accessed=1, transcendentals=0)
LONG = pl.CostEstimate(flops=10**10, bytes_accessed=10**8, transcendentals=0)
PARAMS = pltpu.CompilerParams(vmem_limit_bytes=16 * 1024 * 1024)


def near(value):
    return pltpu.with_memory_space_constraint(value, pltpu.VMEM)


def far(value):
    return pltpu.with_memory_space_constraint(value, pltpu.HBM)


def flip(value, *bits):
    mask = sum(1 << bit for bit in bits)
    return lax.ppermute(value, "dp", [(i, i ^ mask) for i in range(lax.axis_size("dp"))])


def after_all(value, *others):
    return lax.optimization_barrier((value, *others))[0]


def stage_kernel(parts, rank, *refs):
    sources, outs, full_out, rank_here, sems = refs[:4], refs[-7:-3], *refs[-3:]
    copies = [pltpu.make_async_copy(rank, rank_here, sems.at[0])]
    for source, out in zip(sources, outs):
        if source.shape == out.shape:
            rows = source.shape[0] // parts
            pairs = [
                (source.at[pl.ds(n * rows, rows)], out.at[pl.ds(n * rows, rows)])
                for n in range(parts)
            ]
        else:
            width = out.shape[1]
            column = pl.multiple_of(lax.axis_index("tensor") * width, width)
            pairs = [(source.at[:, pl.ds(column, width)], out)]
        for pair in pairs:
            copies.append(pltpu.make_async_copy(*pair, sems.at[len(copies)]))
    for copy in copies:
        copy.start()
    copies.pop(0).wait()
    own_rank = jnp.where(lax.axis_index("tensor") == 0, rank_here[0], rank_here[1])
    full = (own_rank == outs[0].shape[0]).astype(jnp.float32)
    full_out[...] = jnp.full(full_out.shape, full)
    for copy in copies:
        copy.wait()


def stage(rank, right, cotangent, left, tokens, after):
    acts = pltpu.VMEM(tokens.shape, tokens.dtype)
    own = pltpu.VMEM((left.shape[0], tokens.shape[1]), left.dtype)
    parts = 8 if tokens.shape[0] % 128 == 0 else 1
    return pl.pallas_call(
        functools.partial(stage_kernel, parts),
        in_specs=[FAR] * 5 + [WHOLE] * len(after),
        out_specs=[WHOLE] * 5,
        out_shape=[own, acts, own, acts, pltpu.VMEM((8, 128), jnp.float32)],
        scratch_shapes=[
            pltpu.SMEM(rank.shape, rank.dtype),
            pltpu.SemaphoreType.DMA((3 + 2 * parts,)),
        ],
        compiler_params=PARAMS,
        cost_estimate=SMALL,
        name="stage",
    )(*map(far, (rank, right, cotangent, left, tokens)), *map(near, after))


def across(value, mask):
    pairs = [(i, i ^ mask) for i in range(2 * lax.axis_size("dp"))]
    return lax.ppermute(value, ("dp", "tensor"), pairs)


def own_is_full(full):
    return full[0:1, 0:1] > 0.5


def both_panels(own, piece):
    gap = jnp.zeros((PAD, piece.shape[1]), piece.dtype)
    return jnp.concatenate([own, gap, piece, gap], axis=0)


def add_up(total, own, piece, acts, flipped, low_column):
    width = piece.shape[1]
    chunk = min(width // 2, 512)
    core = lax.axis_index("dp") % 2
    start = (1 - core if flipped else core) * (own.shape[1] // 2) + low_column
    turned = None
    for n, low in enumerate(range(0, width, chunk)):
        column = pl.ds(pl.multiple_of(start + low, chunk), chunk)
        rows = both_panels(own[:, column], piece[:, low : low + chunk])
        if n % 2:
            part = lax.dot_general(
                acts[:, column], rows, (((1,), (1,)), ((), ())), preferred_element_type=jnp.float32
            )
            turned = part if turned is None else turned + part
        else:
            part = lax.dot_general(
                rows, acts[:, column], (((1,), (1,)), ((), ())), preferred_element_type=jnp.float32
            )
            total = part if total is None else total + part
    return total + turned.T


def project_two_kernel(low, *refs):
    first, second, (first_out, second_out) = refs[:4], refs[4:8], refs[-2:]
    first_out[...] = add_up(first[3][...], *first[:3], False, low)
    second_out[...] = add_up(second[3][...], *second[:3], True, 0)


def project_two(first, low, second, held):
    shape = pltpu.VMEM(first[3].shape, jnp.float32)
    operands = (*first, *second, *held)
    return pl.pallas_call(
        functools.partial(project_two_kernel, low),
        in_specs=[WHOLE] * len(operands),
        out_specs=[WHOLE] * 2,
        out_shape=[shape, shape],
        compiler_params=PARAMS,
        cost_estimate=SMALL,
        name="project_two",
    )(*map(near, operands))


def project_kernel(flipped, low, given, *refs):
    own, piece, acts = refs[:3]
    others, out = refs[3 : 3 + given], refs[-1 if given < 3 else -2]
    slots = piece.shape[0]
    total = add_up(others[0][...] if others else None, own, piece, acts, flipped, low)
    if given < 3:
        out[...] = total
        return
    full_here = own_is_full(others[1][...])
    shorts = []
    for n, value in enumerate((others[2][...], total)):
        own_part, other_part = value[:slots], value[slots + PAD : 2 * slots + PAD]
        out[n * slots : (n + 1) * slots] = jnp.where(full_here, own_part, other_part)
        shorts.append(jnp.where(full_here, other_part[:1], own_part[:1]))
    row = lax.broadcasted_iota(jnp.int32, (PAD, out.shape[1]), 0)
    out[2 * slots :] = jnp.where(row == 0, shorts[0], jnp.where(row == 1, shorts[1], 0.0))
    refs[-1][...] = out[...].astype(refs[-1].dtype)


def project(own, piece, acts, flipped, others, held, low=0):
    slots = piece.shape[0]
    tokens = acts.shape[0]
    last = len(others) == 3
    shape = (2 * slots + (PAD if last else 2 * PAD), tokens)
    kinds = (jnp.float32, jnp.bfloat16) if last else (jnp.float32,)
    return pl.pallas_call(
        functools.partial(project_kernel, flipped, low, len(others)),
        in_specs=[WHOLE] * (3 + len(others) + len(held)),
        out_specs=[WHOLE] * len(kinds),
        out_shape=[pltpu.VMEM(shape, kind) for kind in kinds],
        compiler_params=PARAMS,
        cost_estimate=SMALL,
        name="project",
    )(*map(near, (own, piece, acts, *others, *held)))


def summed_rows(parts, got, n):
    slots = (parts.shape[0] - PAD) // 2
    full = slice(n * slots, (n + 1) * slots)
    short = slice(2 * slots + n, 2 * slots + n + 1)
    total = parts[...] + got[...].astype(parts.dtype)
    return total[full], total[short]


def gradient_kernel(scale, places, jobs, parts, got, tokens, cotangent, *refs):
    outs = refs[-len(jobs) :]
    rows, block = outs[0].shape[1:]
    slots = (rows - PAD) // 2
    live = slots + PAD
    position = lax.axis_index("dp")
    first = lax.broadcasted_iota(jnp.int32, (PAD, tokens.shape[0]), 0) == 0
    weights = []
    for n in range(2):
        full, short = summed_rows(parts, got, n)
        both = jnp.concatenate([full, jnp.where(first, short, 0.0)], axis=0)
        weights.append(both.astype(jnp.bfloat16))
    main = tokens.shape[0] // 256 * 256
    gap = jnp.zeros((live, tokens.shape[0] - main), jnp.bfloat16)
    rest = jnp.concatenate(
        [
            jnp.concatenate([weights[0][:, main:], gap], axis=1),
            jnp.concatenate([gap, weights[1][:, main:]], axis=1),
        ],
        axis=0,
    )
    row = lax.broadcasted_iota(jnp.int32, (PAD, block), 0)
    for (own, keep), out in zip(jobs, outs):
        core = (position + (0 if keep else 1)) % 2
        bit_3 = (position // 8 + (0 if own else 1)) % 2
        for j, q in enumerate(places):
            start = ((bit_3 * len(places) + j) * 2 + core) * block
            columns = pl.ds(pl.multiple_of(start, block), block)
            last = jnp.concatenate([tokens[main:, columns], cotangent[main:, columns]], axis=0)
            last = jnp.dot(rest, last, preferred_element_type=jnp.float32)
            left, right = (
                jnp.dot(w[:, :main], acts[:main, columns], preferred_element_type=jnp.float32)
                for w, acts in zip(weights, (tokens, cotangent))
            )
            left += last[:live]
            right += last[live:]
            short = jnp.where(row == 1, right[slots : slots + 1], left[slots:])
            grad = jnp.concatenate([left[:slots], right[:slots], short], axis=0) * scale
            out[q] = grad.astype(out.dtype)


def gradient(parts, got, tokens, cotangent, scale, jobs, after):
    places = (0, 2, 1, 3)
    shape = (len(places), parts.shape[0], tokens.shape[1] // lax.axis_size("dp"))
    return pl.pallas_call(
        functools.partial(gradient_kernel, scale, places, jobs),
        in_specs=[WHOLE] * (4 + len(after)),
        out_specs=[WHOLE] * len(jobs),
        out_shape=[pltpu.VMEM(shape, jnp.float32 if job[1] else jnp.bfloat16) for job in jobs],
        compiler_params=PARAMS,
        cost_estimate=SMALL,
        name="gradient",
    )(*map(near, (parts, got, tokens, cotangent, *after)))


def spread_kernel(chunk, full, parts, got, own, mine, theirs, after, out, buffer, sems):
    slots, width = mine.shape
    full_here = own_is_full(full[...])
    back, short = summed_rows(parts, got, 0)
    first = lax.broadcasted_iota(jnp.int32, back.shape, 0) == 0
    short = jnp.where(first, short, 0.0)
    of_own = jnp.where(full_here, back, short)
    of_other = jnp.where(full_here, short, back)
    gap = jnp.zeros((PAD, back.shape[1]), jnp.float32)
    weights = jnp.concatenate([of_own, gap, of_other, gap], axis=0).T.astype(jnp.bfloat16)
    core = lax.axis_index("dp") % 2
    copies = []
    for side, piece in enumerate((mine, theirs)):
        for low in range(0, width, chunk):
            start = (core if side == 0 else 1 - core) * width + low
            column = pl.ds(pl.multiple_of(start, chunk), chunk)
            rows = both_panels(own[:, column], piece[:, low : low + chunk])
            held = buffer.at[:, side * width + low : side * width + low + chunk]
            held[...] = jnp.dot(weights, rows, preferred_element_type=jnp.float32).astype(out.dtype)
            copy = pltpu.make_async_copy(held, out.at[:, column], sems.at[len(copies)])
            copy.start()
            copies.append(copy)
    for copy in copies:
        copy.wait()


def spread(full, parts, got, own, mine, theirs, after):
    tokens = parts.shape[1]
    width = own.shape[1]
    chunk = min(width // 2, 1024)
    return pl.pallas_call(
        functools.partial(spread_kernel, chunk),
        in_specs=[WHOLE] * 7,
        out_specs=FAR,
        out_shape=jax.ShapeDtypeStruct((tokens, width), jnp.bfloat16),
        scratch_shapes=[
            pltpu.VMEM((tokens, width), jnp.bfloat16),
            pltpu.SemaphoreType.DMA((width // chunk,)),
        ],
        compiler_params=PARAMS,
        cost_estimate=LONG,
        name="spread",
    )(*map(near, (full, parts, got, own, mine, theirs, after)))


def settle_kernel(full, keep, *refs):
    gots, (near_out, far_out) = refs[:-2], refs[-2:]
    slots, block = near_out.shape[1:]
    full_here = own_is_full(full[...])
    first = lax.broadcasted_iota(jnp.int32, (slots, block), 0) == 0
    total = keep[...]
    for got in gots:
        total += got[...].astype(jnp.float32)
    for n in range(2):
        rows = total[n * slots : (n + 1) * slots]
        short = jnp.where(first, total[2 * slots + n : 2 * slots + n + 1], 0.0)
        near_out[n] = jnp.where(full_here, rows, short).astype(near_out.dtype)
        far_out[n] = jnp.where(full_here, short, rows).astype(far_out.dtype)


def settle(full, keep, gots, kind):
    rows, block = keep.shape
    shape = (2, (rows - PAD) // 2, block)
    return pl.pallas_call(
        settle_kernel,
        in_specs=[WHOLE] * (2 + len(gots)),
        out_specs=[WHOLE, WHOLE],
        out_shape=[pltpu.VMEM(shape, kind), pltpu.VMEM(shape, jnp.bfloat16)],
        compiler_params=PARAMS,
        cost_estimate=SMALL,
        name="settle",
    )(*map(near, (full, keep, *gots)))


def gather_kernel(*refs):
    total = refs[0][...].astype(jnp.float32)
    for value in refs[1:-1]:
        total += value[...].astype(jnp.float32)
    refs[-1][...] = total


def gather(*values):
    return pl.pallas_call(
        gather_kernel,
        in_specs=[WHOLE] * len(values),
        out_specs=WHOLE,
        out_shape=pltpu.VMEM(values[0].shape, jnp.float32),
        compiler_params=PARAMS,
        cost_estimate=SMALL,
        name="gather",
    )(*map(near, values))


def place_kernel(held, far, got, left_out, right_out):
    here = lax.axis_index("tensor") == 0
    for n, out in enumerate((left_out, right_out)):
        other = far[n] + got[n].astype(out.dtype)
        out[:, 0, 0, :] = jnp.where(here, held[n], other)
        out[:, 1, 0, :] = jnp.where(here, other, held[n])


def place(held, far, got):
    shape = jax.ShapeDtypeStruct((held.shape[1], 2, 1, held.shape[2]), jnp.float32)
    return pl.pallas_call(
        place_kernel,
        in_specs=[WHOLE] * 3,
        out_specs=[WHOLE, WHOLE],
        out_shape=[shape, shape],
        compiler_params=PARAMS,
        cost_estimate=SMALL,
        name="place",
    )(*map(near, (held, far, got)))


def pick_kernel(right, left, *refs):
    outs, sems = refs[:-1], refs[-1]
    part = right.shape[1] // 4
    core = lax.axis_index("dp") % 2
    low = 0
    copies = []
    for n, out in enumerate(outs):
        size = out.shape[1]
        source = left if n else right
        column = ((1 - lax.axis_index("tensor")) * 2 + (1 - core if n == 2 else core)) * part
        here = pl.ds(pl.multiple_of(column + low, 128), size)
        copies.append(pltpu.make_async_copy(source.at[:, here], out, sems.at[n]))
        low = low + size if n else 0
    for copy in copies:
        copy.start()
    for copy in copies:
        copy.wait()


def pick(right, left):
    slots, width = left.shape
    part = width // 4
    sizes = (part, part // 2, part // 2)
    return pl.pallas_call(
        pick_kernel,
        in_specs=[FAR] * 2,
        out_specs=[WHOLE] * 3,
        out_shape=[pltpu.VMEM((slots, size), left.dtype) for size in sizes],
        scratch_shapes=[pltpu.SemaphoreType.DMA((3,))],
        compiler_params=PARAMS,
        cost_estimate=SMALL,
        name="pick",
    )(far(right), far(left))


def quarter_kernel(keep, got, *outs):
    place = lax.axis_index("dp") // 2
    for n, out in enumerate(outs):
        block = (place + n % 2) % 2 * 2 + (place // 2 + n // 2) % 2
        out[...] = (keep[block] + got[block].astype(jnp.float32)).astype(out.dtype)


def quarter(keep, got):
    kinds = [jnp.float32] + [jnp.bfloat16] * 3
    return pl.pallas_call(
        quarter_kernel,
        in_specs=[WHOLE] * 2,
        out_specs=[WHOLE] * 4,
        out_shape=[pltpu.VMEM(keep.shape[1:], kind) for kind in kinds],
        compiler_params=PARAMS,
        cost_estimate=SMALL,
        name="quarter",
    )(near(keep), near(got))


def trade(sends):
    return [flip(sends[2], 1, 2), flip(sends[0], 1), flip(sends[1], 2)]


def two_panels(tokens, cotangent, left_factor, right_factor, panel_rank):
    scale = 1.0 / math.sqrt(tokens.shape[0] * lax.axis_size("dp"))

    wanted = pick(right_factor, left_factor)
    right_mine, left_first = (lax.ppermute(w, "tensor", SWAP) for w in wanted[:2])
    left_second = across(wanted[2], 3)
    right_own, cotangent, left_own, tokens, full = stage(
        panel_rank, right_factor, cotangent, left_factor, tokens, wanted
    )
    right_mine = after_all(right_mine, right_own)
    right_theirs = flip(right_mine, 0)
    (back,) = project(right_own, right_mine, cotangent, False, (), ())
    left_first = after_all(left_first, back)
    (hidden,) = project(left_own, left_first, tokens, False, (), (cotangent,))
    left_second = after_all(left_second, hidden)
    left_mine = jnp.concatenate([left_first, left_second], axis=1)
    left_theirs = flip(left_mine, 0)
    hidden, back = project_two(
        (left_own, left_second, tokens, hidden), left_first.shape[1],
        (right_own, right_theirs, cotangent, back), (),
    )
    parts, parts_send = project(
        left_own, left_theirs, tokens, True, (hidden, full, back), (cotangent,)
    )
    parts_got = lax.ppermute(parts_send, "tensor", SWAP)

    operands = (parts, parts_got, tokens, cotangent, scale)
    (other_send,) = gradient(*operands, [(False, False)], ())
    other_keep, own_send = gradient(
        *operands, [(False, True), (True, False)], (other_send,)
    )
    other = quarter(other_keep, flip(other_send, 0))
    (own_keep,) = gradient(*operands, [(True, True)], (own_send, other[1]))
    own = quarter(own_keep, flip(own_send, 0))
    other_gots, own_gots = trade(other[1:]), trade(own[1:])
    near_send, far_send = settle(full, other[0], other_gots, jnp.bfloat16)
    far_got = across(far_send, 17)
    near_got = flip(near_send, 3)
    held, send = settle(full, own[0], own_gots, jnp.float32)
    got = lax.ppermute(send, "tensor", SWAP)
    token_grad = spread(full, parts, parts_got, left_own, left_mine, left_theirs, send)
    far = gather(far_got)
    far, near_got = lax.optimization_barrier((far, near_got))
    held = gather(held, near_got)
    return token_grad, *place(held, far, after_all(got, token_grad, held))


def solution(mesh):
    placed = (P("dp", "tensor"), P("dp", "tensor"), P("tensor", None), P("tensor", None), P())
    return jax.shard_map(
        two_panels if (mesh.shape["tensor"], mesh.shape["dp"]) == (2, 16) else any_panels,
        mesh=mesh,
        in_specs=placed,
        out_specs=(P("dp", "tensor"), P("tensor", None, "dp", None), P("tensor", None, "dp", None)),
        check_vma=False,
    )
```

```python
import functools
import math

import jax
import jax.numpy as jnp
from jax import lax
from jax.experimental import pallas as pl
from jax.experimental.pallas import tpu as pltpu
from jax.sharding import PartitionSpec as P


def block_view(home):
    groups = lax.axis_size("tensor")
    width = lax.axis_size("dp")
    block = home.shape[1] // (groups * width)
    return home.reshape(home.shape[0], groups, width, block)


def own_blocks(summed):
    return lax.dynamic_slice_in_dim(summed, lax.axis_index("dp"), 1, 2)


def settle_both(left_cols, right_cols):
    left_home, right_home = (
        lax.all_to_all(left_cols, "tensor", split_axis=0, concat_axis=1, tiled=True),
        lax.all_to_all(right_cols, "tensor", split_axis=0, concat_axis=1, tiled=True),
    )
    left_home = block_view(left_home)
    right_home = block_view(right_home)
    left_sum, right_sum = lax.psum((left_home, right_home), "dp")
    return (own_blocks(left_sum), own_blocks(right_sum))


def any_panels(tokens, cotangent, left_factor, right_factor, panel_rank):
    slot_count = left_factor.shape[0]
    groups = lax.axis_size("tensor")
    all_slots = slot_count * groups
    left_cols, right_cols = (
        lax.all_to_all(left_factor, "tensor", split_axis=1, concat_axis=0, tiled=True),
        lax.all_to_all(right_factor, "tensor", split_axis=1, concat_axis=0, tiled=True),
    )
    slots = jnp.arange(all_slots, dtype=jnp.int32)
    limits = jnp.repeat(panel_rank, slot_count, total_repeat_length=all_slots)
    live_rows = (slots % slot_count < limits).astype(jnp.bfloat16)[:, None]
    left_live = left_cols * live_rows
    right_live = right_cols * live_rows
    feature_dims = (((1,), (1,)), ((), ()))
    hidden_part = lax.dot_general(
        tokens, left_live, feature_dims, preferred_element_type=jnp.float32
    )
    back_part = lax.dot_general(
        cotangent, right_live, feature_dims, preferred_element_type=jnp.float32
    )
    hidden, back_hidden = lax.psum((hidden_part, back_part), "tensor")
    hidden = hidden.astype(jnp.bfloat16)
    back_hidden = back_hidden.astype(jnp.bfloat16)
    grad_scale = 1.0 / math.sqrt(tokens.shape[0] * lax.axis_size("dp"))
    token_dims = (((0,), (0,)), ((), ()))
    right_local = (
        lax.dot_general(hidden, cotangent, token_dims, preferred_element_type=jnp.float32)
        * grad_scale
    )
    left_local = (
        lax.dot_general(back_hidden, tokens, token_dims, preferred_element_type=jnp.float32)
        * grad_scale
    )
    token_grad = jnp.dot(back_hidden, left_live, preferred_element_type=jnp.float32).astype(
        jnp.bfloat16
    )
    left_grad, right_grad = settle_both(left_local, right_local)
    return (token_grad, left_grad, right_grad)


PAD = 8
SWAP = [(0, 1), (1, 0)]
WHOLE = pl.BlockSpec(memory_space=pltpu.VMEM)
FAR = pl.BlockSpec(memory_space=pltpu.HBM)
SMALL = pl.CostEstimate(flops=1, bytes_accessed=1, transcendentals=0)
LONG = pl.CostEstimate(flops=10**10, bytes_accessed=10**8, transcendentals=0)
PARAMS = pltpu.CompilerParams(vmem_limit_bytes=16 * 1024 * 1024)


def near(value):
    return pltpu.with_memory_space_constraint(value, pltpu.VMEM)


def far(value):
    return pltpu.with_memory_space_constraint(value, pltpu.HBM)


def flip(value, *bits):
    mask = sum(1 << bit for bit in bits)
    return lax.ppermute(value, "dp", [(i, i ^ mask) for i in range(lax.axis_size("dp"))])


def after_all(value, *others):
    return lax.optimization_barrier((value, *others))[0]


def stage_kernel(parts, rank, *refs):
    sources, outs, full_out, rank_here, sems = refs[:4], refs[-7:-3], *refs[-3:]
    copies = [pltpu.make_async_copy(rank, rank_here, sems.at[0])]
    for source, out in zip(sources, outs):
        if source.shape == out.shape:
            rows = source.shape[0] // parts
            pairs = [
                (source.at[pl.ds(n * rows, rows)], out.at[pl.ds(n * rows, rows)])
                for n in range(parts)
            ]
        else:
            width = out.shape[1]
            column = pl.multiple_of(lax.axis_index("tensor") * width, width)
            pairs = [(source.at[:, pl.ds(column, width)], out)]
        for pair in pairs:
            copies.append(pltpu.make_async_copy(*pair, sems.at[len(copies)]))
    for copy in copies:
        copy.start()
    copies.pop(0).wait()
    own_rank = jnp.where(lax.axis_index("tensor") == 0, rank_here[0], rank_here[1])
    full = (own_rank == outs[0].shape[0]).astype(jnp.float32)
    full_out[...] = jnp.full(full_out.shape, full)
    for copy in copies:
        copy.wait()


def stage(rank, right, cotangent, left, tokens, after):
    acts = pltpu.VMEM(tokens.shape, tokens.dtype)
    own = pltpu.VMEM((left.shape[0], tokens.shape[1]), left.dtype)
    parts = 8 if tokens.shape[0] % 128 == 0 else 1
    return pl.pallas_call(
        functools.partial(stage_kernel, parts),
        in_specs=[FAR] * 5 + [WHOLE] * len(after),
        out_specs=[WHOLE] * 5,
        out_shape=[own, acts, own, acts, pltpu.VMEM((8, 128), jnp.float32)],
        scratch_shapes=[
            pltpu.SMEM(rank.shape, rank.dtype),
            pltpu.SemaphoreType.DMA((3 + 2 * parts,)),
        ],
        compiler_params=PARAMS,
        cost_estimate=SMALL,
        name="stage",
    )(*map(far, (rank, right, cotangent, left, tokens)), *map(near, after))


def across(value, mask):
    pairs = [(i, i ^ mask) for i in range(2 * lax.axis_size("dp"))]
    return lax.ppermute(value, ("dp", "tensor"), pairs)


def own_is_full(full):
    return full[0:1, 0:1] > 0.5


def both_panels(own, piece):
    gap = jnp.zeros((PAD, piece.shape[1]), piece.dtype)
    return jnp.concatenate([own, gap, piece, gap], axis=0)


def add_up(total, own, piece, acts, flipped, low_column):
    width = piece.shape[1]
    chunk = min(width // 2, 256)
    core = lax.axis_index("dp") % 2
    start = (1 - core if flipped else core) * (own.shape[1] // 2) + low_column
    turned = None
    for n, low in enumerate(range(0, width, chunk)):
        column = pl.ds(pl.multiple_of(start + low, chunk), chunk)
        rows = both_panels(own[:, column], piece[:, low : low + chunk])
        if n % 2:
            part = lax.dot_general(
                acts[:, column], rows, (((1,), (1,)), ((), ())), preferred_element_type=jnp.float32
            )
            turned = part if turned is None else turned + part
        else:
            part = lax.dot_general(
                rows, acts[:, column], (((1,), (1,)), ((), ())), preferred_element_type=jnp.float32
            )
            total = part if total is None else total + part
    return total + turned.T


def project_two_kernel(low, *refs):
    first, second, (first_out, second_out) = refs[:4], refs[4:8], refs[-2:]
    first_out[...] = add_up(first[3][...], *first[:3], False, low)
    second_out[...] = add_up(second[3][...], *second[:3], True, 0)


def project_two(first, low, second, held):
    shape = pltpu.VMEM(first[3].shape, jnp.float32)
    operands = (*first, *second, *held)
    return pl.pallas_call(
        functools.partial(project_two_kernel, low),
        in_specs=[WHOLE] * len(operands),
        out_specs=[WHOLE] * 2,
        out_shape=[shape, shape],
        compiler_params=PARAMS,
        cost_estimate=SMALL,
        name="project_two",
    )(*map(near, operands))


def project_kernel(flipped, low, given, *refs):
    own, piece, acts = refs[:3]
    others, out = refs[3 : 3 + given], refs[-1 if given < 3 else -2]
    slots = piece.shape[0]
    total = add_up(others[0][...] if others else None, own, piece, acts, flipped, low)
    if given < 3:
        out[...] = total
        return
    full_here = own_is_full(others[1][...])
    shorts = []
    for n, value in enumerate((others[2][...], total)):
        own_part, other_part = value[:slots], value[slots + PAD : 2 * slots + PAD]
        out[n * slots : (n + 1) * slots] = jnp.where(full_here, own_part, other_part)
        shorts.append(jnp.where(full_here, other_part[:1], own_part[:1]))
    row = lax.broadcasted_iota(jnp.int32, (PAD, out.shape[1]), 0)
    out[2 * slots :] = jnp.where(row == 0, shorts[0], jnp.where(row == 1, shorts[1], 0.0))
    refs[-1][...] = out[...].astype(refs[-1].dtype)


def project(own, piece, acts, flipped, others, held, low=0):
    slots = piece.shape[0]
    tokens = acts.shape[0]
    last = len(others) == 3
    shape = (2 * slots + (PAD if last else 2 * PAD), tokens)
    kinds = (jnp.float32, jnp.bfloat16) if last else (jnp.float32,)
    return pl.pallas_call(
        functools.partial(project_kernel, flipped, low, len(others)),
        in_specs=[WHOLE] * (3 + len(others) + len(held)),
        out_specs=[WHOLE] * len(kinds),
        out_shape=[pltpu.VMEM(shape, kind) for kind in kinds],
        compiler_params=PARAMS,
        cost_estimate=SMALL,
        name="project",
    )(*map(near, (own, piece, acts, *others, *held)))


def summed_rows(parts, got, n):
    slots = (parts.shape[0] - PAD) // 2
    full = slice(n * slots, (n + 1) * slots)
    short = slice(2 * slots + n, 2 * slots + n + 1)
    total = parts[...] + got[...].astype(parts.dtype)
    return total[full], total[short]


def gradient_kernel(scale, places, jobs, parts, got, tokens, cotangent, *refs):
    outs = refs[-len(jobs) :]
    rows, block = outs[0].shape[1:]
    slots = (rows - PAD) // 2
    live = slots + PAD
    position = lax.axis_index("dp")
    first = lax.broadcasted_iota(jnp.int32, (PAD, tokens.shape[0]), 0) == 0
    weights = []
    for n in range(2):
        full, short = summed_rows(parts, got, n)
        both = jnp.concatenate([full, jnp.where(first, short, 0.0)], axis=0)
        weights.append(both.astype(jnp.bfloat16))
    main = tokens.shape[0] // 256 * 256
    gap = jnp.zeros((live, tokens.shape[0] - main), jnp.bfloat16)
    rest = jnp.concatenate(
        [
            jnp.concatenate([weights[0][:, main:], gap], axis=1),
            jnp.concatenate([gap, weights[1][:, main:]], axis=1),
        ],
        axis=0,
    )
    row = lax.broadcasted_iota(jnp.int32, (PAD, block), 0)
    for (own, keep), out in zip(jobs, outs):
        core = (position + (0 if keep else 1)) % 2
        bit_3 = (position // 8 + (0 if own else 1)) % 2
        for j, q in enumerate(places):
            start = ((bit_3 * len(places) + j) * 2 + core) * block
            columns = pl.ds(pl.multiple_of(start, block), block)
            last = jnp.concatenate([tokens[main:, columns], cotangent[main:, columns]], axis=0)
            last = jnp.dot(rest, last, preferred_element_type=jnp.float32)
            left, right = (
                jnp.dot(w[:, :main], acts[:main, columns], preferred_element_type=jnp.float32)
                for w, acts in zip(weights, (tokens, cotangent))
            )
            left += last[:live]
            right += last[live:]
            short = jnp.where(row == 1, right[slots : slots + 1], left[slots:])
            grad = jnp.concatenate([left[:slots], right[:slots], short], axis=0) * scale
            out[q] = grad.astype(out.dtype)


def gradient(parts, got, tokens, cotangent, scale, jobs, after):
    places = (0, 2, 1, 3)
    shape = (len(places), parts.shape[0], tokens.shape[1] // lax.axis_size("dp"))
    return pl.pallas_call(
        functools.partial(gradient_kernel, scale, places, jobs),
        in_specs=[WHOLE] * (4 + len(after)),
        out_specs=[WHOLE] * len(jobs),
        out_shape=[pltpu.VMEM(shape, jnp.float32 if job[1] else jnp.bfloat16) for job in jobs],
        compiler_params=PARAMS,
        cost_estimate=SMALL,
        name="gradient",
    )(*map(near, (parts, got, tokens, cotangent, *after)))


def spread_kernel(chunk, full, parts, got, own, mine, theirs, after, out, buffer, sems):
    slots, width = mine.shape
    full_here = own_is_full(full[...])
    back, short = summed_rows(parts, got, 0)
    first = lax.broadcasted_iota(jnp.int32, back.shape, 0) == 0
    short = jnp.where(first, short, 0.0)
    of_own = jnp.where(full_here, back, short)
    of_other = jnp.where(full_here, short, back)
    gap = jnp.zeros((PAD, back.shape[1]), jnp.float32)
    weights = jnp.concatenate([of_own, gap, of_other, gap], axis=0).T.astype(jnp.bfloat16)
    core = lax.axis_index("dp") % 2
    copies = []
    for side, piece in enumerate((mine, theirs)):
        for low in range(0, width, chunk):
            start = (core if side == 0 else 1 - core) * width + low
            column = pl.ds(pl.multiple_of(start, chunk), chunk)
            rows = both_panels(own[:, column], piece[:, low : low + chunk])
            held = buffer.at[:, side * width + low : side * width + low + chunk]
            held[...] = jnp.dot(weights, rows, preferred_element_type=jnp.float32).astype(out.dtype)
            copy = pltpu.make_async_copy(held, out.at[:, column], sems.at[len(copies)])
            copy.start()
            copies.append(copy)
    for copy in copies:
        copy.wait()


def spread(full, parts, got, own, mine, theirs, after):
    tokens = parts.shape[1]
    width = own.shape[1]
    chunk = min(width // 2, 1024)
    return pl.pallas_call(
        functools.partial(spread_kernel, chunk),
        in_specs=[WHOLE] * 7,
        out_specs=FAR,
        out_shape=jax.ShapeDtypeStruct((tokens, width), jnp.bfloat16),
        scratch_shapes=[
            pltpu.VMEM((tokens, width), jnp.bfloat16),
            pltpu.SemaphoreType.DMA((width // chunk,)),
        ],
        compiler_params=PARAMS,
        cost_estimate=LONG,
        name="spread",
    )(*map(near, (full, parts, got, own, mine, theirs, after)))


def settle_kernel(full, keep, *refs):
    gots, (near_out, far_out) = refs[:-2], refs[-2:]
    slots, block = near_out.shape[1:]
    full_here = own_is_full(full[...])
    first = lax.broadcasted_iota(jnp.int32, (slots, block), 0) == 0
    total = keep[...]
    for got in gots:
        total += got[...].astype(jnp.float32)
    for n in range(2):
        rows = total[n * slots : (n + 1) * slots]
        short = jnp.where(first, total[2 * slots + n : 2 * slots + n + 1], 0.0)
        near_out[n] = jnp.where(full_here, rows, short).astype(near_out.dtype)
        far_out[n] = jnp.where(full_here, short, rows).astype(far_out.dtype)


def settle(full, keep, gots, kind):
    rows, block = keep.shape
    shape = (2, (rows - PAD) // 2, block)
    return pl.pallas_call(
        settle_kernel,
        in_specs=[WHOLE] * (2 + len(gots)),
        out_specs=[WHOLE, WHOLE],
        out_shape=[pltpu.VMEM(shape, kind), pltpu.VMEM(shape, jnp.bfloat16)],
        compiler_params=PARAMS,
        cost_estimate=SMALL,
        name="settle",
    )(*map(near, (full, keep, *gots)))


def gather_kernel(*refs):
    total = refs[0][...].astype(jnp.float32)
    for value in refs[1:-1]:
        total += value[...].astype(jnp.float32)
    refs[-1][...] = total


def gather(*values):
    return pl.pallas_call(
        gather_kernel,
        in_specs=[WHOLE] * len(values),
        out_specs=WHOLE,
        out_shape=pltpu.VMEM(values[0].shape, jnp.float32),
        compiler_params=PARAMS,
        cost_estimate=SMALL,
        name="gather",
    )(*map(near, values))


def place_kernel(held, far, got, left_out, right_out):
    here = lax.axis_index("tensor") == 0
    for n, out in enumerate((left_out, right_out)):
        other = far[n] + got[n].astype(out.dtype)
        out[:, 0, 0, :] = jnp.where(here, held[n], other)
        out[:, 1, 0, :] = jnp.where(here, other, held[n])


def place(held, far, got):
    shape = jax.ShapeDtypeStruct((held.shape[1], 2, 1, held.shape[2]), jnp.float32)
    return pl.pallas_call(
        place_kernel,
        in_specs=[WHOLE] * 3,
        out_specs=[WHOLE, WHOLE],
        out_shape=[shape, shape],
        compiler_params=PARAMS,
        cost_estimate=SMALL,
        name="place",
    )(*map(near, (held, far, got)))


def pick_kernel(right, left, *refs):
    outs, sems = refs[:-1], refs[-1]
    part = right.shape[1] // 4
    core = lax.axis_index("dp") % 2
    low = 0
    copies = []
    for n, out in enumerate(outs):
        size = out.shape[1]
        source = left if n else right
        column = ((1 - lax.axis_index("tensor")) * 2 + (1 - core if n == 2 else core)) * part
        here = pl.ds(pl.multiple_of(column + low, 128), size)
        copies.append(pltpu.make_async_copy(source.at[:, here], out, sems.at[n]))
        low = low + size if n else 0
    for copy in copies:
        copy.start()
    for copy in copies:
        copy.wait()


def pick(right, left):
    slots, width = left.shape
    part = width // 4
    sizes = (part, part // 2, part // 2)
    return pl.pallas_call(
        pick_kernel,
        in_specs=[FAR] * 2,
        out_specs=[WHOLE] * 3,
        out_shape=[pltpu.VMEM((slots, size), left.dtype) for size in sizes],
        scratch_shapes=[pltpu.SemaphoreType.DMA((3,))],
        compiler_params=PARAMS,
        cost_estimate=SMALL,
        name="pick",
    )(far(right), far(left))


def quarter_kernel(keep, got, *outs):
    place = lax.axis_index("dp") // 2
    for n, out in enumerate(outs):
        block = (place + n % 2) % 2 * 2 + (place // 2 + n // 2) % 2
        out[...] = (keep[block] + got[block].astype(jnp.float32)).astype(out.dtype)


def quarter(keep, got):
    kinds = [jnp.float32] + [jnp.bfloat16] * 3
    return pl.pallas_call(
        quarter_kernel,
        in_specs=[WHOLE] * 2,
        out_specs=[WHOLE] * 4,
        out_shape=[pltpu.VMEM(keep.shape[1:], kind) for kind in kinds],
        compiler_params=PARAMS,
        cost_estimate=SMALL,
        name="quarter",
    )(near(keep), near(got))


def last_kernel(scale, places, parts, parts_got, tokens, cotangent, got, after, *refs):
    outs, keep = refs[:-1], refs[-1]
    gradient_kernel(scale, places, [(True, True)], parts, parts_got, tokens, cotangent, keep)
    quarter_kernel(keep, got, *outs)


def last_quarter(parts, parts_got, tokens, cotangent, scale, got, after):
    shape = (4, parts.shape[0], tokens.shape[1] // lax.axis_size("dp"))
    return pl.pallas_call(
        functools.partial(last_kernel, scale, (0, 2, 1, 3)),
        in_specs=[WHOLE] * 6,
        out_specs=[WHOLE] * 4,
        out_shape=[pltpu.VMEM(shape[1:], kind) for kind in [jnp.float32] + [jnp.bfloat16] * 3],
        scratch_shapes=[pltpu.VMEM(shape, jnp.float32)],
        compiler_params=PARAMS,
        cost_estimate=SMALL,
        name="last_quarter",
    )(*map(near, (parts, parts_got, tokens, cotangent, got, after)))


def trade(sends):
    return [flip(sends[2], 1, 2), flip(sends[0], 1), flip(sends[1], 2)]


def two_panels(tokens, cotangent, left_factor, right_factor, panel_rank):
    scale = 1.0 / math.sqrt(tokens.shape[0] * lax.axis_size("dp"))

    wanted = pick(right_factor, left_factor)
    right_mine, left_first = (lax.ppermute(w, "tensor", SWAP) for w in wanted[:2])
    left_second = across(wanted[2], 3)
    right_own, cotangent, left_own, tokens, full = stage(
        panel_rank, right_factor, cotangent, left_factor, tokens, wanted
    )
    right_mine = after_all(right_mine, right_own)
    right_theirs = flip(right_mine, 0)
    (back,) = project(right_own, right_mine, cotangent, False, (), ())
    left_first = after_all(left_first, back)
    (hidden,) = project(left_own, left_first, tokens, False, (), (cotangent,))
    left_second = after_all(left_second, hidden)
    left_mine = jnp.concatenate([left_first, left_second], axis=1)
    left_theirs = flip(left_mine, 0)
    hidden, back = project_two(
        (left_own, left_second, tokens, hidden), left_first.shape[1],
        (right_own, right_theirs, cotangent, back), (),
    )
    parts, parts_send = project(
        left_own, left_theirs, tokens, True, (hidden, full, back), (cotangent,)
    )
    parts_got = lax.ppermute(parts_send, "tensor", SWAP)

    operands = (parts, parts_got, tokens, cotangent, scale)
    (other_send,) = gradient(*operands, [(False, False)], ())
    other_keep, own_send = gradient(
        *operands, [(False, True), (True, False)], (other_send,)
    )
    other = quarter(other_keep, flip(other_send, 0))
    own = last_quarter(*operands, flip(own_send, 0), other[1])
    other_gots, own_gots = trade(other[1:]), trade(own[1:])
    near_send, far_send = settle(full, other[0], other_gots, jnp.bfloat16)
    far_got = across(far_send, 17)
    near_got = flip(near_send, 3)
    held, send = settle(full, own[0], own_gots, jnp.float32)
    got = lax.ppermute(send, "tensor", SWAP)
    token_grad = spread(full, parts, parts_got, left_own, left_mine, left_theirs, send)
    far = gather(far_got)
    far, near_got = lax.optimization_barrier((far, near_got))
    held = gather(held, near_got)
    return token_grad, *place(held, far, after_all(got, token_grad, held))


def solution(mesh):
    placed = (P("dp", "tensor"), P("dp", "tensor"), P("tensor", None), P("tensor", None), P())
    return jax.shard_map(
        two_panels if (mesh.shape["tensor"], mesh.shape["dp"]) == (2, 16) else any_panels,
        mesh=mesh,
        in_specs=placed,
        out_specs=(P("dp", "tensor"), P("tensor", None, "dp", None), P("tensor", None, "dp", None)),
        check_vma=False,
    )
```

```python
import functools
import math

import jax
import jax.numpy as jnp
from jax import lax
from jax.experimental import pallas as pl
from jax.experimental.pallas import tpu as pltpu
from jax.sharding import PartitionSpec as P


def block_view(home):
    groups = lax.axis_size("tensor")
    width = lax.axis_size("dp")
    block = home.shape[1] // (groups * width)
    return home.reshape(home.shape[0], groups, width, block)


def own_blocks(summed):
    return lax.dynamic_slice_in_dim(summed, lax.axis_index("dp"), 1, 2)


def settle_both(left_cols, right_cols):
    left_home, right_home = (
        lax.all_to_all(left_cols, "tensor", split_axis=0, concat_axis=1, tiled=True),
        lax.all_to_all(right_cols, "tensor", split_axis=0, concat_axis=1, tiled=True),
    )
    left_home = block_view(left_home)
    right_home = block_view(right_home)
    left_sum, right_sum = lax.psum((left_home, right_home), "dp")
    return (own_blocks(left_sum), own_blocks(right_sum))


def any_panels(tokens, cotangent, left_factor, right_factor, panel_rank):
    slot_count = left_factor.shape[0]
    groups = lax.axis_size("tensor")
    all_slots = slot_count * groups
    left_cols, right_cols = (
        lax.all_to_all(left_factor, "tensor", split_axis=1, concat_axis=0, tiled=True),
        lax.all_to_all(right_factor, "tensor", split_axis=1, concat_axis=0, tiled=True),
    )
    slots = jnp.arange(all_slots, dtype=jnp.int32)
    limits = jnp.repeat(panel_rank, slot_count, total_repeat_length=all_slots)
    live_rows = (slots % slot_count < limits).astype(jnp.bfloat16)[:, None]
    left_live = left_cols * live_rows
    right_live = right_cols * live_rows
    feature_dims = (((1,), (1,)), ((), ()))
    hidden_part = lax.dot_general(
        tokens, left_live, feature_dims, preferred_element_type=jnp.float32
    )
    back_part = lax.dot_general(
        cotangent, right_live, feature_dims, preferred_element_type=jnp.float32
    )
    hidden, back_hidden = lax.psum((hidden_part, back_part), "tensor")
    hidden = hidden.astype(jnp.bfloat16)
    back_hidden = back_hidden.astype(jnp.bfloat16)
    grad_scale = 1.0 / math.sqrt(tokens.shape[0] * lax.axis_size("dp"))
    token_dims = (((0,), (0,)), ((), ()))
    right_local = (
        lax.dot_general(hidden, cotangent, token_dims, preferred_element_type=jnp.float32)
        * grad_scale
    )
    left_local = (
        lax.dot_general(back_hidden, tokens, token_dims, preferred_element_type=jnp.float32)
        * grad_scale
    )
    token_grad = jnp.dot(back_hidden, left_live, preferred_element_type=jnp.float32).astype(
        jnp.bfloat16
    )
    left_grad, right_grad = settle_both(left_local, right_local)
    return (token_grad, left_grad, right_grad)


PAD = 8
SWAP = [(0, 1), (1, 0)]
WHOLE = pl.BlockSpec(memory_space=pltpu.VMEM)
FAR = pl.BlockSpec(memory_space=pltpu.HBM)
SMALL = pl.CostEstimate(flops=1, bytes_accessed=1, transcendentals=0)
LONG = pl.CostEstimate(flops=10**10, bytes_accessed=10**8, transcendentals=0)
PARAMS = pltpu.CompilerParams(vmem_limit_bytes=16 * 1024 * 1024)


def near(value):
    return pltpu.with_memory_space_constraint(value, pltpu.VMEM)


def far(value):
    return pltpu.with_memory_space_constraint(value, pltpu.HBM)


def flip(value, *bits):
    mask = sum(1 << bit for bit in bits)
    return lax.ppermute(value, "dp", [(i, i ^ mask) for i in range(lax.axis_size("dp"))])


def after_all(value, *others):
    return lax.optimization_barrier((value, *others))[0]


def stage_kernel(parts, rank, *refs):
    sources, outs, full_out, rank_here, sems = refs[:4], refs[-7:-3], *refs[-3:]
    copies = [pltpu.make_async_copy(rank, rank_here, sems.at[0])]
    for source, out in zip(sources, outs):
        if source.shape == out.shape:
            rows = source.shape[0] // parts
            pairs = [
                (source.at[pl.ds(n * rows, rows)], out.at[pl.ds(n * rows, rows)])
                for n in range(parts)
            ]
        else:
            width = out.shape[1]
            column = pl.multiple_of(lax.axis_index("tensor") * width, width)
            pairs = [(source.at[:, pl.ds(column, width)], out)]
        for pair in pairs:
            copies.append(pltpu.make_async_copy(*pair, sems.at[len(copies)]))
    for copy in copies:
        copy.start()
    copies.pop(0).wait()
    own_rank = jnp.where(lax.axis_index("tensor") == 0, rank_here[0], rank_here[1])
    full = (own_rank == outs[0].shape[0]).astype(jnp.float32)
    full_out[...] = jnp.full(full_out.shape, full)
    for copy in copies:
        copy.wait()


def stage(rank, right, cotangent, left, tokens, after):
    acts = pltpu.VMEM(tokens.shape, tokens.dtype)
    own = pltpu.VMEM((left.shape[0], tokens.shape[1]), left.dtype)
    parts = 4 if tokens.shape[0] % 64 == 0 else 1
    return pl.pallas_call(
        functools.partial(stage_kernel, parts),
        in_specs=[FAR] * 5 + [WHOLE] * len(after),
        out_specs=[WHOLE] * 5,
        out_shape=[own, acts, own, acts, pltpu.VMEM((8, 128), jnp.float32)],
        scratch_shapes=[
            pltpu.SMEM(rank.shape, rank.dtype),
            pltpu.SemaphoreType.DMA((3 + 2 * parts,)),
        ],
        compiler_params=PARAMS,
        cost_estimate=SMALL,
        name="stage",
    )(*map(far, (rank, right, cotangent, left, tokens)), *map(near, after))


def across(value, mask):
    pairs = [(i, i ^ mask) for i in range(2 * lax.axis_size("dp"))]
    return lax.ppermute(value, ("dp", "tensor"), pairs)


def own_is_full(full):
    return full[0:1, 0:1] > 0.5


def both_panels(own, piece):
    gap = jnp.zeros((PAD, piece.shape[1]), piece.dtype)
    return jnp.concatenate([own, gap, piece, gap], axis=0)


def add_up(total, own, piece, acts, flipped, low_column):
    width = piece.shape[1]
    chunk = min(width // 2, 256)
    core = lax.axis_index("dp") % 2
    start = (1 - core if flipped else core) * (own.shape[1] // 2) + low_column
    turned = None
    for n, low in enumerate(range(0, width, chunk)):
        column = pl.ds(pl.multiple_of(start + low, chunk), chunk)
        rows = both_panels(own[:, column], piece[:, low : low + chunk])
        if n % 2:
            part = lax.dot_general(
                acts[:, column], rows, (((1,), (1,)), ((), ())), preferred_element_type=jnp.float32
            )
            turned = part if turned is None else turned + part
        else:
            part = lax.dot_general(
                rows, acts[:, column], (((1,), (1,)), ((), ())), preferred_element_type=jnp.float32
            )
            total = part if total is None else total + part
    return total + turned.T


def project_two_kernel(low, *refs):
    first, second, (first_out, second_out) = refs[:4], refs[4:8], refs[-2:]
    first_out[...] = add_up(first[3][...], *first[:3], False, low)
    second_out[...] = add_up(second[3][...], *second[:3], True, 0)


def project_two(first, low, second, held):
    shape = pltpu.VMEM(first[3].shape, jnp.float32)
    operands = (*first, *second, *held)
    return pl.pallas_call(
        functools.partial(project_two_kernel, low),
        in_specs=[WHOLE] * len(operands),
        out_specs=[WHOLE] * 2,
        out_shape=[shape, shape],
        compiler_params=PARAMS,
        cost_estimate=SMALL,
        name="project_two",
    )(*map(near, operands))


def project_kernel(flipped, low, given, *refs):
    own, piece, acts = refs[:3]
    others, out = refs[3 : 3 + given], refs[-1 if given < 3 else -2]
    slots = piece.shape[0]
    total = add_up(others[0][...] if others else None, own, piece, acts, flipped, low)
    if given < 3:
        out[...] = total
        return
    full_here = own_is_full(others[1][...])
    shorts = []
    for n, value in enumerate((others[2][...], total)):
        own_part, other_part = value[:slots], value[slots + PAD : 2 * slots + PAD]
        out[n * slots : (n + 1) * slots] = jnp.where(full_here, own_part, other_part)
        shorts.append(jnp.where(full_here, other_part[:1], own_part[:1]))
    row = lax.broadcasted_iota(jnp.int32, (PAD, out.shape[1]), 0)
    out[2 * slots :] = jnp.where(row == 0, shorts[0], jnp.where(row == 1, shorts[1], 0.0))
    refs[-1][...] = out[...].astype(refs[-1].dtype)


def project(own, piece, acts, flipped, others, held, low=0):
    slots = piece.shape[0]
    tokens = acts.shape[0]
    last = len(others) == 3
    shape = (2 * slots + (PAD if last else 2 * PAD), tokens)
    kinds = (jnp.float32, jnp.bfloat16) if last else (jnp.float32,)
    return pl.pallas_call(
        functools.partial(project_kernel, flipped, low, len(others)),
        in_specs=[WHOLE] * (3 + len(others) + len(held)),
        out_specs=[WHOLE] * len(kinds),
        out_shape=[pltpu.VMEM(shape, kind) for kind in kinds],
        compiler_params=PARAMS,
        cost_estimate=SMALL,
        name="project",
    )(*map(near, (own, piece, acts, *others, *held)))


def summed_rows(parts, got, n):
    slots = (parts.shape[0] - PAD) // 2
    full = slice(n * slots, (n + 1) * slots)
    short = slice(2 * slots + n, 2 * slots + n + 1)
    total = parts[...] + got[...].astype(parts.dtype)
    return total[full], total[short]


def gradient_kernel(scale, places, jobs, parts, got, tokens, cotangent, *refs):
    outs = refs[-len(jobs) :]
    rows, block = outs[0].shape[1:]
    slots = (rows - PAD) // 2
    live = slots + PAD
    position = lax.axis_index("dp")
    first = lax.broadcasted_iota(jnp.int32, (PAD, tokens.shape[0]), 0) == 0
    weights = []
    for n in range(2):
        full, short = summed_rows(parts, got, n)
        both = jnp.concatenate([full, jnp.where(first, short, 0.0)], axis=0)
        weights.append(both.astype(jnp.bfloat16))
    main = tokens.shape[0] // 256 * 256
    gap = jnp.zeros((live, tokens.shape[0] - main), jnp.bfloat16)
    rest = jnp.concatenate(
        [
            jnp.concatenate([weights[0][:, main:], gap], axis=1),
            jnp.concatenate([gap, weights[1][:, main:]], axis=1),
        ],
        axis=0,
    )
    row = lax.broadcasted_iota(jnp.int32, (PAD, block), 0)
    for (own, keep), out in zip(jobs, outs):
        core = (position + (0 if keep else 1)) % 2
        bit_3 = (position // 8 + (0 if own else 1)) % 2
        for j, q in enumerate(places):
            start = ((bit_3 * len(places) + j) * 2 + core) * block
            columns = pl.ds(pl.multiple_of(start, block), block)
            last = jnp.concatenate([tokens[main:, columns], cotangent[main:, columns]], axis=0)
            last = jnp.dot(rest, last, preferred_element_type=jnp.float32)
            left, right = (
                jnp.dot(w[:, :main], acts[:main, columns], preferred_element_type=jnp.float32)
                for w, acts in zip(weights, (tokens, cotangent))
            )
            left += last[:live]
            right += last[live:]
            short = jnp.where(row == 1, right[slots : slots + 1], left[slots:])
            grad = jnp.concatenate([left[:slots], right[:slots], short], axis=0) * scale
            out[q] = grad.astype(out.dtype)


def gradient(parts, got, tokens, cotangent, scale, jobs, after):
    places = (0, 2, 1, 3)
    shape = (len(places), parts.shape[0], tokens.shape[1] // lax.axis_size("dp"))
    return pl.pallas_call(
        functools.partial(gradient_kernel, scale, places, jobs),
        in_specs=[WHOLE] * (4 + len(after)),
        out_specs=[WHOLE] * len(jobs),
        out_shape=[pltpu.VMEM(shape, jnp.float32 if job[1] else jnp.bfloat16) for job in jobs],
        compiler_params=PARAMS,
        cost_estimate=SMALL,
        name="gradient",
    )(*map(near, (parts, got, tokens, cotangent, *after)))


def spread_kernel(chunk, full, parts, got, own, mine, theirs, after, out, buffer, sems):
    slots, width = mine.shape
    full_here = own_is_full(full[...])
    back, short = summed_rows(parts, got, 0)
    first = lax.broadcasted_iota(jnp.int32, back.shape, 0) == 0
    short = jnp.where(first, short, 0.0)
    of_own = jnp.where(full_here, back, short)
    of_other = jnp.where(full_here, short, back)
    gap = jnp.zeros((PAD, back.shape[1]), jnp.float32)
    weights = jnp.concatenate([of_own, gap, of_other, gap], axis=0).T.astype(jnp.bfloat16)
    core = lax.axis_index("dp") % 2
    copies = []
    for side, piece in enumerate((mine, theirs)):
        for low in range(0, width, chunk):
            start = (core if side == 0 else 1 - core) * width + low
            column = pl.ds(pl.multiple_of(start, chunk), chunk)
            rows = both_panels(own[:, column], piece[:, low : low + chunk])
            held = buffer.at[:, side * width + low : side * width + low + chunk]
            held[...] = jnp.dot(weights, rows, preferred_element_type=jnp.float32).astype(out.dtype)
            copy = pltpu.make_async_copy(held, out.at[:, column], sems.at[len(copies)])
            copy.start()
            copies.append(copy)
    for copy in copies:
        copy.wait()


def spread(full, parts, got, own, mine, theirs, after):
    tokens = parts.shape[1]
    width = own.shape[1]
    chunk = min(width // 2, 1024)
    return pl.pallas_call(
        functools.partial(spread_kernel, chunk),
        in_specs=[WHOLE] * 7,
        out_specs=FAR,
        out_shape=jax.ShapeDtypeStruct((tokens, width), jnp.bfloat16),
        scratch_shapes=[
            pltpu.VMEM((tokens, width), jnp.bfloat16),
            pltpu.SemaphoreType.DMA((width // chunk,)),
        ],
        compiler_params=PARAMS,
        cost_estimate=LONG,
        name="spread",
    )(*map(near, (full, parts, got, own, mine, theirs, after)))


def settle_kernel(full, keep, *refs):
    gots, (near_out, far_out) = refs[:-2], refs[-2:]
    slots, block = near_out.shape[1:]
    full_here = own_is_full(full[...])
    first = lax.broadcasted_iota(jnp.int32, (slots, block), 0) == 0
    total = keep[...]
    for got in gots:
        total += got[...].astype(jnp.float32)
    for n in range(2):
        rows = total[n * slots : (n + 1) * slots]
        short = jnp.where(first, total[2 * slots + n : 2 * slots + n + 1], 0.0)
        near_out[n] = jnp.where(full_here, rows, short).astype(near_out.dtype)
        far_out[n] = jnp.where(full_here, short, rows).astype(far_out.dtype)


def settle(full, keep, gots, kind):
    rows, block = keep.shape
    shape = (2, (rows - PAD) // 2, block)
    return pl.pallas_call(
        settle_kernel,
        in_specs=[WHOLE] * (2 + len(gots)),
        out_specs=[WHOLE, WHOLE],
        out_shape=[pltpu.VMEM(shape, kind), pltpu.VMEM(shape, jnp.bfloat16)],
        compiler_params=PARAMS,
        cost_estimate=SMALL,
        name="settle",
    )(*map(near, (full, keep, *gots)))


def gather_kernel(*refs):
    total = refs[0][...].astype(jnp.float32)
    for value in refs[1:-1]:
        total += value[...].astype(jnp.float32)
    refs[-1][...] = total


def gather(*values):
    return pl.pallas_call(
        gather_kernel,
        in_specs=[WHOLE] * len(values),
        out_specs=WHOLE,
        out_shape=pltpu.VMEM(values[0].shape, jnp.float32),
        compiler_params=PARAMS,
        cost_estimate=SMALL,
        name="gather",
    )(*map(near, values))


def place_kernel(held, far, got, left_out, right_out):
    here = lax.axis_index("tensor") == 0
    for n, out in enumerate((left_out, right_out)):
        other = far[n] + got[n].astype(out.dtype)
        out[:, 0, 0, :] = jnp.where(here, held[n], other)
        out[:, 1, 0, :] = jnp.where(here, other, held[n])


def place(held, far, got):
    shape = jax.ShapeDtypeStruct((held.shape[1], 2, 1, held.shape[2]), jnp.float32)
    return pl.pallas_call(
        place_kernel,
        in_specs=[WHOLE] * 3,
        out_specs=[WHOLE, WHOLE],
        out_shape=[shape, shape],
        compiler_params=PARAMS,
        cost_estimate=SMALL,
        name="place",
    )(*map(near, (held, far, got)))


def pick_kernel(right, left, *refs):
    outs, sems = refs[:-1], refs[-1]
    part = right.shape[1] // 4
    core = lax.axis_index("dp") % 2
    low = 0
    copies = []
    for n, out in enumerate(outs):
        size = out.shape[1]
        source = left if n else right
        column = ((1 - lax.axis_index("tensor")) * 2 + (1 - core if n == 2 else core)) * part
        here = pl.ds(pl.multiple_of(column + low, 128), size)
        copies.append(pltpu.make_async_copy(source.at[:, here], out, sems.at[n]))
        low = low + size if n else 0
    for copy in copies:
        copy.start()
    for copy in copies:
        copy.wait()


def pick(right, left):
    slots, width = left.shape
    part = width // 4
    sizes = (part, part // 2, part // 2)
    return pl.pallas_call(
        pick_kernel,
        in_specs=[FAR] * 2,
        out_specs=[WHOLE] * 3,
        out_shape=[pltpu.VMEM((slots, size), left.dtype) for size in sizes],
        scratch_shapes=[pltpu.SemaphoreType.DMA((3,))],
        compiler_params=PARAMS,
        cost_estimate=SMALL,
        name="pick",
    )(far(right), far(left))


def quarter_kernel(keep, got, *outs):
    place = lax.axis_index("dp") // 2
    for n, out in enumerate(outs):
        block = (place + n % 2) % 2 * 2 + (place // 2 + n // 2) % 2
        out[...] = (keep[block] + got[block].astype(jnp.float32)).astype(out.dtype)


def quarter(keep, got):
    kinds = [jnp.float32] + [jnp.bfloat16] * 3
    return pl.pallas_call(
        quarter_kernel,
        in_specs=[WHOLE] * 2,
        out_specs=[WHOLE] * 4,
        out_shape=[pltpu.VMEM(keep.shape[1:], kind) for kind in kinds],
        compiler_params=PARAMS,
        cost_estimate=SMALL,
        name="quarter",
    )(near(keep), near(got))


def last_kernel(scale, places, parts, parts_got, tokens, cotangent, got, after, *refs):
    outs, keep = refs[:-1], refs[-1]
    gradient_kernel(scale, places, [(True, True)], parts, parts_got, tokens, cotangent, keep)
    quarter_kernel(keep, got, *outs)


def last_quarter(parts, parts_got, tokens, cotangent, scale, got, after):
    shape = (4, parts.shape[0], tokens.shape[1] // lax.axis_size("dp"))
    return pl.pallas_call(
        functools.partial(last_kernel, scale, (0, 2, 1, 3)),
        in_specs=[WHOLE] * 6,
        out_specs=[WHOLE] * 4,
        out_shape=[pltpu.VMEM(shape[1:], kind) for kind in [jnp.float32] + [jnp.bfloat16] * 3],
        scratch_shapes=[pltpu.VMEM(shape, jnp.float32)],
        compiler_params=PARAMS,
        cost_estimate=SMALL,
        name="last_quarter",
    )(*map(near, (parts, parts_got, tokens, cotangent, got, after)))


def trade(sends):
    return [flip(sends[2], 1, 2), flip(sends[0], 1), flip(sends[1], 2)]


def two_panels(tokens, cotangent, left_factor, right_factor, panel_rank):
    scale = 1.0 / math.sqrt(tokens.shape[0] * lax.axis_size("dp"))

    wanted = pick(right_factor, left_factor)
    right_mine, left_first = (lax.ppermute(w, "tensor", SWAP) for w in wanted[:2])
    left_second = across(wanted[2], 3)
    right_own, cotangent, left_own, tokens, full = stage(
        panel_rank, right_factor, cotangent, left_factor, tokens, wanted
    )
    right_mine = after_all(right_mine, right_own)
    right_theirs = flip(right_mine, 0)
    (back,) = project(right_own, right_mine, cotangent, False, (), ())
    left_first = after_all(left_first, back)
    (hidden,) = project(left_own, left_first, tokens, False, (), ())
    left_second = after_all(left_second, hidden)
    left_mine = jnp.concatenate([left_first, left_second], axis=1)
    left_theirs = flip(left_mine, 0)
    hidden, back = project_two(
        (left_own, left_second, tokens, hidden), left_first.shape[1],
        (right_own, right_theirs, cotangent, back), (),
    )
    parts, parts_send = project(
        left_own, left_theirs, tokens, True, (hidden, full, back), ()
    )
    parts_got = lax.ppermute(parts_send, "tensor", SWAP)

    operands = (parts, parts_got, tokens, cotangent, scale)
    (other_send,) = gradient(*operands, [(False, False)], ())
    other_keep, own_send = gradient(
        *operands, [(False, True), (True, False)], (other_send,)
    )
    other = quarter(other_keep, flip(other_send, 0))
    own = last_quarter(*operands, flip(own_send, 0), other[1])
    other_gots, own_gots = trade(other[1:]), trade(own[1:])
    near_send, far_send = settle(full, other[0], other_gots, jnp.bfloat16)
    far_got = across(far_send, 17)
    near_got = flip(near_send, 3)
    held, send = settle(full, own[0], own_gots, jnp.float32)
    got = lax.ppermute(send, "tensor", SWAP)
    token_grad = spread(full, parts, parts_got, left_own, left_mine, left_theirs, send)
    far = gather(far_got)
    far, near_got = lax.optimization_barrier((far, near_got))
    held = gather(held, near_got)
    return token_grad, *place(held, far, after_all(got, token_grad, held))


def solution(mesh):
    placed = (P("dp", "tensor"), P("dp", "tensor"), P("tensor", None), P("tensor", None), P())
    return jax.shard_map(
        two_panels if (mesh.shape["tensor"], mesh.shape["dp"]) == (2, 16) else any_panels,
        mesh=mesh,
        in_specs=placed,
        out_specs=(P("dp", "tensor"), P("tensor", None, "dp", None), P("tensor", None, "dp", None)),
        check_vma=False,
    )
```
